32 devices in a mesh: dp: 16 (over z, y, core), vocab: 2 (over x).
Axes of the slice: x: 2, y: 2, z: 4, core: 2. Of those that a mesh axis runs over, the one named last changes fastest.
Arguments:
- audio_codes: int32 [64, 4, 128], P('dp'), may hold values from 0 to 2047
- delay_offsets: int32 [64, 4], P('dp'), may hold values from 0 to 3
- clip_lengths: int32 [64], P('dp'), may hold values from 64 to 128
- loss_positions: int32 [64, 32], P('dp'), may hold values from 0 to 127
- teacher_ids: int32 [64, 4, 32, 64], P('dp'), may hold values from 0 to 2047
- text_states: bfloat16 [64, 64, 1024], P(('dp', 'vocab')), may hold values from -6 to 6
- step_count: int32 [], replicated, may hold values from 1 to 20
- in_proj: float32 [6, 1024, 1024], P(None, ('dp', 'vocab')), may hold values from -0.1875 to 0.1875
- in_proj_mean: float32 [6, 1024, 1024], P(None, ('dp', 'vocab')), may hold values from -0.0008544922 to 0.0008544922
- in_proj_sq: float32 [6, 1024, 1024], P(None, ('dp', 'vocab')), may hold values from 5e-09 to 3e-08
- out_proj: float32 [2, 1024, 1024], P(None, ('dp', 'vocab')), may hold values from -1 to 1
- out_proj_mean: float32 [2, 1024, 1024], P(None, ('dp', 'vocab')), may hold values from -0.0008544922 to 0.0008544922
- out_proj_sq: float32 [2, 1024, 1024], P(None, ('dp', 'vocab')), may hold values from 5e-09 to 3e-08
- ffn_proj: float32 [2, 1024, 4096], P(None, ('dp', 'vocab')), may hold values from -0.1875 to 0.1875
- ffn_proj_mean: float32 [2, 1024, 4096], P(None, ('dp', 'vocab')), may hold values from -0.0008544922 to 0.0008544922
- ffn_proj_sq: float32 [2, 1024, 4096], P(None, ('dp', 'vocab')), may hold values from 5e-09 to 3e-08
- embed_table: float32 [4, 2049, 1024], P(None, None, ('dp', 'vocab')), may hold values from -3 to 3
- embed_table_mean: float32 [4, 2049, 1024], P(None, None, ('dp', 'vocab')), may hold values from -0.00015258789 to 0.00015258789
- embed_table_sq: float32 [4, 2049, 1024], P(None, None, ('dp', 'vocab')), may hold values from 1.5e-10 to 9e-10
- head_table: float32 [4, 1024, 2048], P(None, 'dp', 'vocab'), may hold values from -0.1875 to 0.1875
- head_table_mean: float32 [4, 1024, 2048], P(None, 'dp', 'vocab'), may hold values from -0.0008544922 to 0.0008544922
- head_table_sq: float32 [4, 1024, 2048], P(None, 'dp', 'vocab'), may hold values from 5e-09 to 3e-08
- norm_gain: float32 [4, 1024], P(None, ('dp', 'vocab')), may hold values from -0.4 to 0.4
- norm_gain_mean: float32 [4, 1024], P(None, ('dp', 'vocab')), may hold values from -0.0008544922 to 0.0008544922
- norm_gain_sq: float32 [4, 1024], P(None, ('dp', 'vocab')), may hold values from 5e-09 to 3e-08
- norm_bias: float32 [4, 1024], P(None, ('dp', 'vocab')), may hold values from -3 to 3
- norm_bias_mean: float32 [4, 1024], P(None, ('dp', 'vocab')), may hold values from -0.0008544922 to 0.0008544922
- norm_bias_sq: float32 [4, 1024], P(None, ('dp', 'vocab')), may hold values from 5e-09 to 3e-08
Outputs:
- loss_value: float32 [], replicated
- grad_norm: float32 [], replicated
- in_proj_next: float32 [6, 1024, 1024], P(None, ('dp', 'vocab'))
- in_proj_mean_next: float32 [6, 1024, 1024], P(None, ('dp', 'vocab'))
- in_proj_sq_next: float32 [6, 1024, 1024], P(None, ('dp', 'vocab'))
- out_proj_next: float32 [2, 1024, 1024], P(None, ('dp', 'vocab'))
- out_proj_mean_next: float32 [2, 1024, 1024], P(None, ('dp', 'vocab'))
- out_proj_sq_next: float32 [2, 1024, 1024], P(None, ('dp', 'vocab'))
- ffn_proj_next: float32 [2, 1024, 4096], P(None, ('dp', 'vocab'))
- ffn_proj_mean_next: float32 [2, 1024, 4096], P(None, ('dp', 'vocab'))
- ffn_proj_sq_next: float32 [2, 1024, 4096], P(None, ('dp', 'vocab'))
- embed_table_next: float32 [4, 2049, 1024], P(None, None, ('dp', 'vocab'))
- embed_table_mean_next: float32 [4, 2049, 1024], P(None, None, ('dp', 'vocab'))
- embed_table_sq_next: float32 [4, 2049, 1024], P(None, None, ('dp', 'vocab'))
- head_table_next: float32 [4, 1024, 2048], P(None, 'dp', 'vocab')
- head_table_mean_next: float32 [4, 1024, 2048], P(None, 'dp', 'vocab')
- head_table_sq_next: float32 [4, 1024, 2048], P(None, 'dp', 'vocab')
- norm_gain_next: float32 [4, 1024], P(None, ('dp', 'vocab'))
- norm_gain_mean_next: float32 [4, 1024], P(None, ('dp', 'vocab'))
- norm_gain_sq_next: float32 [4, 1024], P(None, ('dp', 'vocab'))
- norm_bias_next: float32 [4, 1024], P(None, ('dp', 'vocab'))
- norm_bias_mean_next: float32 [4, 1024], P(None, ('dp', 'vocab'))
- norm_bias_sq_next: float32 [4, 1024], P(None, ('dp', 'vocab'))
The draws below stay inside these ranges and needn't reach their ends.
All inputs are finite; a program needn't handle non-finite values.
Results may differ from the reference program's by a relative error of at most 0.0064.
Values may be sent and summed in bfloat16 or wider, within the bound.
A program may use at most 448 MiB of HBM per device.

```python
import math
from functools import partial
import jax
import jax.numpy as jnp
import numpy as np
from jax import lax

D = 1024
HEADS = 16
FF = 4096
BOOKS = 4
CARD = 2048
EMB_ROWS = 2049
TEXT = 64
TEACH = 64
FRAMES = 128
POS = 32
CLIPS = 64


def place_ends(array, own_key, low, top_value):
    index_at = [jax.random.randint(jax.random.fold_in(own_key, axis), (), 0, length) for axis, length in enumerate(array.shape)]
    widest = array.shape.index(max(array.shape))
    neighbour = index_at[:widest] + [(index_at[widest] + 1) % array.shape[widest]] + index_at[widest + 1:]
    return array.at[tuple(index_at)].set(low).at[tuple(neighbour)].set(top_value)


def block_scale(rng, dims, split, least, high):
    def one(dim, shards_of):
        draws = jax.random.uniform(jax.random.fold_in(jax.random.fold_in(rng, 6), dim), (shards_of,), jnp.float32, least / len(split), high / len(split))
        return jnp.repeat(jnp.exp(draws), dims[dim] // shards_of).reshape((-1,) + (1,) * (len(dims) - dim - 1))

    factor_of = one(*split[0])
    for cut in split[1:]:
        factor_of = factor_of * one(*cut)
    return factor_of


def rank_table(number_of, slope):
    portions = [(1 << 20) // math.isqrt(grade ** slope) + 1 for grade in range(1, number_of + 1)]
    deviation = 1 + sum(portions) // (1 << 30)
    return np.cumsum(np.array([max(1, weight // deviation) for weight in portions]))


def ranked_ids(own_key, extent, amount, skew):
    table = rank_table(amount, skew)
    ticket = jax.random.randint(jax.random.fold_in(own_key, 1), extent, 0, int(table[amount - 1]))
    grade = jnp.searchsorted(jnp.asarray(table, jnp.int32), ticket, side="right")
    return jax.random.permutation(jax.random.fold_in(own_key, 2), amount)[grade].astype(jnp.int32)


def scatter_about(key, dims, scale, reach, cuts=(), kind=jnp.bfloat16):
    values = scale * jax.random.normal(key, dims, jnp.float32)
    if cuts:
        values = values * block_scale(key, dims, cuts, -0.22, 0.18)
    return jnp.clip(values, -reach, reach).astype(kind)


def setup_inputs(seed: int = 0) -> dict:
    key_of = jax.random.split(jax.random.key(seed), 29)
    return {
        "audio_codes": place_ends(ranked_ids(key_of[0], (CLIPS, BOOKS, FRAMES), CARD, 2), jax.random.fold_in(key_of[0], 3), 0, CARD - 1).astype(jnp.int32),
        "delay_offsets": place_ends(jax.random.randint(key_of[1], (CLIPS, BOOKS), 0, 4), jax.random.fold_in(key_of[1], 1), 0, 3).astype(jnp.int32),
        "clip_lengths": place_ends(jax.random.randint(key_of[2], (CLIPS,), FRAMES // 2, FRAMES + 1), jax.random.fold_in(key_of[2], 1), FRAMES // 2, FRAMES).astype(jnp.int32),
        "loss_positions": place_ends(jax.random.randint(key_of[3], (CLIPS, POS), 0, FRAMES), jax.random.fold_in(key_of[3], 1), 0, FRAMES - 1).astype(jnp.int32),
        "teacher_ids": place_ends(ranked_ids(key_of[4], (CLIPS, BOOKS, POS, TEACH), CARD, 2), jax.random.fold_in(key_of[4], 3), 0, CARD - 1).astype(jnp.int32),
        "text_states": scatter_about(key_of[5], (CLIPS, TEXT, D), 1.0, 6.0, ((0, 32),)),
        "step_count": jax.random.randint(key_of[6], (), 1, 21).astype(jnp.int32),
        "in_proj": scatter_about(key_of[7], (6, D, D), D ** -0.5, 0.1875, ((1, 32),), jnp.float32),
        "in_proj_mean": scatter_about(key_of[8], (6, D, D), (6e-5), 0.0008544922, ((1, 32),), jnp.float32),
        "in_proj_sq": jnp.clip(jnp.exp(math.log(2.999999892949745e-08) - 1.79175944 * jax.random.uniform(key_of[9], (6, D, D), jnp.float32) ** block_scale(key_of[9], (6, D, D), ((1, 32),), -0.2, 0.2)), 4.999999969612645e-09, 2.999999892949745e-08),
        "out_proj": scatter_about(key_of[10], (2, D, D), (D // 32) ** -0.5, 1.0, ((1, 32),), jnp.float32),
        "out_proj_mean": scatter_about(key_of[11], (2, D, D), (6e-5), 0.0008544922, ((1, 32),), jnp.float32),
        "out_proj_sq": jnp.clip(jnp.exp(math.log(2.999999892949745e-08) - 1.79175944 * jax.random.uniform(key_of[12], (2, D, D), jnp.float32) ** block_scale(key_of[12], (2, D, D), ((1, 32),), -0.2, 0.2)), 4.999999969612645e-09, 2.999999892949745e-08),
        "ffn_proj": scatter_about(key_of[13], (2, D, FF), D ** -0.5, 0.1875, ((1, 32),), jnp.float32),
        "ffn_proj_mean": scatter_about(key_of[14], (2, D, FF), (6e-5), 0.0008544922, ((1, 32),), jnp.float32),
        "ffn_proj_sq": jnp.clip(jnp.exp(math.log(2.999999892949745e-08) - 1.79175944 * jax.random.uniform(key_of[15], (2, D, FF), jnp.float32) ** block_scale(key_of[15], (2, D, FF), ((1, 32),), -0.2, 0.2)), 4.999999969612645e-09, 2.999999892949745e-08),
        "embed_table": scatter_about(key_of[16], (BOOKS, EMB_ROWS, D), 0.2, 3.0, ((2, 32),), jnp.float32),
        "embed_table_mean": scatter_about(key_of[17], (BOOKS, EMB_ROWS, D), (1e-5), 0.00015258789, ((2, 32),), jnp.float32),
        "embed_table_sq": jnp.clip(jnp.exp(math.log(9.000000189551827e-10) - 1.7917595 * jax.random.uniform(key_of[18], (BOOKS, EMB_ROWS, D), jnp.float32) ** block_scale(key_of[18], (BOOKS, EMB_ROWS, D), ((2, 32),), -0.2, 0.2)), 1.4999999853326784e-10, 9.000000189551827e-10),
        "head_table": scatter_about(key_of[19], (BOOKS, D, CARD), D ** -0.5, 0.1875, ((1, 16), (2, 2)), jnp.float32),
        "head_table_mean": scatter_about(key_of[20], (BOOKS, D, CARD), (6e-5), 0.0008544922, ((1, 16), (2, 2)), jnp.float32),
        "head_table_sq": jnp.clip(jnp.exp(math.log(2.999999892949745e-08) - 1.79175944 * jax.random.uniform(key_of[21], (BOOKS, D, CARD), jnp.float32) ** block_scale(key_of[21], (BOOKS, D, CARD), ((1, 16), (2, 2)), -0.2, 0.2)), 4.999999969612645e-09, 2.999999892949745e-08),
        "norm_gain": jnp.clip(jax.random.uniform(key_of[22], (4, D), jnp.float32, -0.4, 0.4) * block_scale(key_of[22], (4, D), ((1, 32),), -0.4, 0.0), -0.4, 0.4),
        "norm_gain_mean": scatter_about(key_of[23], (4, D), (6e-5), 0.0008544922, ((1, 32),), jnp.float32),
        "norm_gain_sq": jnp.clip(jnp.exp(math.log(2.999999892949745e-08) - 1.79175944 * jax.random.uniform(key_of[24], (4, D), jnp.float32) ** block_scale(key_of[24], (4, D), ((1, 32),), -0.2, 0.2)), 4.999999969612645e-09, 2.999999892949745e-08),
        "norm_bias": scatter_about(key_of[25], (4, D), 0.2, 3.0, ((1, 32),), jnp.float32),
        "norm_bias_mean": scatter_about(key_of[26], (4, D), (6e-5), 0.0008544922, ((1, 32),), jnp.float32),
        "norm_bias_sq": jnp.clip(jnp.exp(math.log(2.999999892949745e-08) - 1.79175944 * jax.random.uniform(key_of[27], (4, D), jnp.float32) ** block_scale(key_of[27], (4, D), ((1, 32),), -0.2, 0.2)), 4.999999969612645e-09, 2.999999892949745e-08),
    }


@jax.custom_vjp
def low(v):
    return lax.optimization_barrier(v.astype(jnp.bfloat16)).astype(jnp.float32)

@jax.custom_vjp
def low_back(v):
    return v

def low_keep(v):
    return (low(v), None)

def low_pass(kept, grad):
    return (grad,)

def back_keep(v):
    return (v, None)

def back_low(kept, grad):
    return (low(grad),)
low.defvjp(low_keep, low_pass)
low_back.defvjp(back_keep, back_low)
HIGHEST = lax.Precision.HIGHEST
NORM_EPS = 1e-05
SCORE_SCALE = 0.125
NEG_FILL = -1e+30
CLIP_LIMIT = 3.0
BETA_ONE = 0.9
BETA_TWO = 0.95
LEARN_RATE = 0.05
DECAY_RATE = 0.1
ADAM_EPS = 1e-08

def layer_norm(values, gain, bias):
    average = lax.optimization_barrier(jnp.mean(values, axis=-1, keepdims=True))
    centred = values - average
    spread = lax.optimization_barrier(jnp.mean(centred * centred, axis=-1, keepdims=True))
    return centred * lax.rsqrt(spread + NORM_EPS) * (1.0 + gain) + bias

def sinusoid(frames, model_width):
    half_width = model_width // 2
    freq_rates = jnp.exp(jnp.arange(half_width, dtype=jnp.float32) * (-math.log(10000.0) / (half_width - 1)))
    angles = jnp.arange(frames, dtype=jnp.float32)[:, None] * freq_rates[None, :]
    return jnp.concatenate([jnp.sin(angles), jnp.cos(angles)], axis=1)

def delay_ids(codes_clip, offsets_clip, special):
    frames = codes_clip.shape[1]
    frame_shift = jnp.arange(frames, dtype=jnp.int32)[None, :] - offsets_clip[:, None].astype(jnp.int32)
    picked = jnp.take_along_axis(codes_clip, jnp.clip(frame_shift, 0, frames - 1), axis=1)
    targets = jnp.where(frame_shift >= 0, picked, special)
    before = frame_shift - 1
    picked_before = jnp.take_along_axis(codes_clip, jnp.clip(before, 0, frames - 1), axis=1)
    inputs = jnp.where(before >= 0, picked_before, special)
    return (inputs.astype(jnp.int32), targets.astype(jnp.int32))

def split_heads(matrix):
    row_count = matrix.shape[0]
    return matrix.reshape(row_count, HEADS, -1).transpose(1, 0, 2)

def join_heads(tensor):
    return tensor.transpose(1, 0, 2).reshape(tensor.shape[1], -1)

def matmul_high(left, right):
    return jnp.dot(left, right, precision=HIGHEST)

def rounded_proj(values, weight):
    return low(low_back(matmul_high(values, weight)))

def attention(queries, keyset, valset, causal):
    scores = jnp.einsum('hqe,hke->hqk', queries, keyset, precision=HIGHEST) * SCORE_SCALE
    if causal:
        length_q = scores.shape[1]
        allowed = jnp.arange(length_q)[:, None] >= jnp.arange(length_q)[None, :]
        scores = jnp.where(allowed[None], scores, NEG_FILL)
    scores = low_back(scores)
    weights = jax.nn.softmax(scores, axis=-1)
    return jnp.einsum('hqk,hke->hqe', low(weights), valset, precision=HIGHEST)

def clip_loss(lowered, codes_clip, offsets_clip, length_clip, positions_clip, teacher_clip, text_clip):
    in_weight, out_weight, ffn_weight, embed_weight, head_weight, gain_rows, biases = lowered
    special = embed_weight.shape[1] - 1
    frames = codes_clip.shape[1]
    model_width = embed_weight.shape[2]
    inputs, targets = delay_ids(codes_clip, offsets_clip, special)
    embedded = jnp.zeros((frames, model_width), jnp.float32)
    for codebook in range(embed_weight.shape[0]):
        embedded = embedded + jnp.take(embed_weight[codebook], inputs[codebook], axis=0)
    start_rows = embedded + sinusoid(frames, model_width)
    normed = low(layer_norm(start_rows, gain_rows[0], biases[0]))
    mixed_heads = attention(split_heads(rounded_proj(normed, in_weight[0])), split_heads(rounded_proj(normed, in_weight[1])), split_heads(rounded_proj(normed, in_weight[2])), True)
    joined = low(low_back(join_heads(mixed_heads)))
    after_self = start_rows + low_back(matmul_high(joined, out_weight[0]))
    normed = low(layer_norm(after_self, gain_rows[1], biases[1]))
    text_values = text_clip.astype(jnp.float32)
    mixed_heads = attention(split_heads(rounded_proj(normed, in_weight[3])), split_heads(rounded_proj(text_values, in_weight[4])), split_heads(rounded_proj(text_values, in_weight[5])), False)
    joined = low(low_back(join_heads(mixed_heads)))
    after_cross = after_self + low_back(matmul_high(joined, out_weight[1]))
    normed = low(layer_norm(after_cross, gain_rows[2], biases[2]))
    up_values = low_back(matmul_high(normed, ffn_weight[0]))
    active = low(jax.nn.gelu(up_values, approximate=False))
    after_ffn = after_cross + low_back(matmul_high(active, ffn_weight[1].T))
    final_norm = layer_norm(after_ffn, gain_rows[3], biases[3])
    chosen = low(jnp.take(final_norm, positions_clip, axis=0))
    logits = low_back(jnp.einsum('pd,kdv->kpv', chosen, head_weight, precision=HIGHEST))
    log_total = jax.nn.logsumexp(logits, axis=-1)
    target_at = jnp.take(targets, positions_clip, axis=1)
    target_valid = (target_at != special).astype(jnp.float32)
    vocab_size = logits.shape[2]
    target_logit = jnp.take_along_axis(logits, jnp.clip(target_at, 0, vocab_size - 1)[:, :, None], axis=2)[:, :, 0]
    teacher_logit = lax.optimization_barrier(jnp.mean(jnp.take_along_axis(logits, teacher_clip, axis=2), axis=2))
    row_weight = (positions_clip < length_clip).astype(jnp.float32)
    terms = row_weight[None, :] * ((target_valid + 1.0) * log_total - (target_valid * target_logit + teacher_logit))
    return jnp.sum(terms)

def group_loss(lowered, batch_arrays):
    per_clip = partial(clip_loss, lowered)
    losses = jax.vmap(per_clip)(batch_arrays[0], batch_arrays[1], batch_arrays[2], batch_arrays[3], batch_arrays[4], batch_arrays[5])
    return jnp.sum(losses)

def adam_step(weight, first_moment, second_moment, gradient, factor, corr_one, corr_two):
    clipped = gradient * factor
    first_next = BETA_ONE * first_moment + (1.0 - BETA_ONE) * clipped
    second_next = BETA_TWO * second_moment + (1.0 - BETA_TWO) * clipped * clipped
    update = first_next / corr_one / (jnp.sqrt(second_next / corr_two) + ADAM_EPS) + DECAY_RATE * weight
    return (weight - LEARN_RATE * update, first_next, second_next)

def reference(audio_codes, delay_offsets, clip_lengths, loss_positions, teacher_ids, text_states, step_count, in_proj, in_proj_mean, in_proj_sq, out_proj, out_proj_mean, out_proj_sq, ffn_proj, ffn_proj_mean, ffn_proj_sq, embed_table, embed_table_mean, embed_table_sq, head_table, head_table_mean, head_table_sq, norm_gain, norm_gain_mean, norm_gain_sq, norm_bias, norm_bias_mean, norm_bias_sq):
    masters = (in_proj, out_proj, ffn_proj, embed_table, head_table, norm_gain, norm_bias)
    mean_list = (in_proj_mean, out_proj_mean, ffn_proj_mean, embed_table_mean, head_table_mean, norm_gain_mean, norm_bias_mean)
    square_list = (in_proj_sq, out_proj_sq, ffn_proj_sq, embed_table_sq, head_table_sq, norm_gain_sq, norm_bias_sq)
    clip_total = audio_codes.shape[0]
    frames = audio_codes.shape[2]
    per_group = 1
    for group_try in range(1, clip_total + 1):
        if clip_total % group_try == 0 and group_try * frames <= 4096:
            per_group = group_try
    groups = clip_total // per_group

    def regroup(source):
        return source.reshape((groups, per_group) + source.shape[1:])
    batches = (regroup(audio_codes), regroup(delay_offsets), regroup(clip_lengths), regroup(loss_positions), regroup(teacher_ids), regroup(text_states))
    denominator = float(clip_total * loss_positions.shape[1] * audio_codes.shape[1])
    checked = jax.checkpoint(group_loss)

    def total_loss(weights):
        lowered = tuple((low(weight) for weight in weights))

        def scan_step(running, batch_arrays):
            return (running + checked(lowered, batch_arrays), None)
        summed, unused = lax.scan(scan_step, jnp.zeros((), jnp.float32), batches)
        return summed / denominator
    loss_value, pull_back = jax.vjp(total_loss, masters)
    gradients = pull_back(jnp.ones((), jnp.float32))[0]
    square_total = jnp.zeros((), jnp.float32)
    for gradient in gradients:
        square_total = square_total + jnp.sum(gradient * gradient)
    grad_norm = jnp.sqrt(square_total)
    factor = CLIP_LIMIT / jnp.maximum(grad_norm, CLIP_LIMIT)
    steps_float = step_count.astype(jnp.float32)
    corr_one = 1.0 - jnp.power(BETA_ONE, steps_float)
    corr_two = 1.0 - jnp.power(BETA_TWO, steps_float)
    results = [adam_step(masters[index], mean_list[index], square_list[index], gradients[index], factor, corr_one, corr_two) for index in range(7)]
    return (loss_value, grad_norm, results[0][0], results[0][1], results[0][2], results[1][0], results[1][1], results[1][2], results[2][0], results[2][1], results[2][2], results[3][0], results[3][1], results[3][2], results[4][0], results[4][1], results[4][2], results[5][0], results[5][1], results[5][2], results[6][0], results[6][1], results[6][2])
```

```python
import functools
import math

import jax
import jax.numpy as jnp
from jax import lax
from jax.experimental import pallas as pl
from jax.experimental.pallas import tpu as pltpu
from jax.sharding import PartitionSpec as P

HEADS = 16
NORM_EPS = 1e-05
SCORE_SCALE = 0.125
NEG_FILL = -1e30
CLIP_LIMIT = 3.0
BETA_ONE = 0.9
BETA_TWO = 0.95
LEARN_RATE = 0.05
DECAY_RATE = 0.1
ADAM_EPS = 1e-08
BOTH = ("dp", "vocab")
MESH = pl.DeviceIdType.MESH
BF = jnp.bfloat16
F32 = jnp.float32
GROUPS = (3, 1, 1, 2, 1, 4, 4)
UNITS = tuple((group, index) for group, size in enumerate(GROUPS) for index in range(size))


def place():
    dp, x = lax.axis_index("dp"), lax.axis_index("vocab")
    return lax.div(dp, 4), lax.rem(lax.div(dp, 2), 2), lax.rem(dp, 2), x


def device(z, y, c, x):
    return ((z * 2 + y) * 2 + c, x)


def partners():
    z, y, c, x = place()
    line = [lax.rem(z + step, 4) for step in (1, 2, 3)]
    return (
        line,
        [device(other, y, c, x) for other in line],
        device(z, 1 - y, c, x),
        device(z, y, c, 1 - x),
        device(z, y, 1 - c, x),
    )


def greet(targets):
    barrier = pltpu.get_barrier_semaphore()
    for target in targets:
        pl.semaphore_signal(barrier, inc=1, device_id=target, device_id_type=MESH)
    pl.semaphore_wait(barrier, len(targets))


def transfer_order(heads):
    order, head = [], 0
    for unit in range(len(UNITS)):
        order.append(("b" if unit % 4 == 3 else "a", unit))
        if unit % 4 == 1 and head < heads:
            order.append(("h", head))
            head += 1
    return tuple(order)


def gather_kernel(order, delays, *refs):
    layer_ref, head_ref = refs[:2]
    outs, head_out = refs[2:9], refs[9]
    send_sem, recv_sem, local_sem = refs[10:]
    z, y, c, x = place()
    line, z_dev, y_dev, x_dev, c_dev = partners()
    greet(z_dev + [y_dev, x_dev, c_dev])

    def copy(src, dst, item, slot, target):
        return pltpu.make_async_remote_copy(
            src_ref=src,
            dst_ref=dst,
            send_sem=send_sem.at[item, slot],
            recv_sem=recv_sem.at[item, slot],
            device_id=target,
            device_id_type=MESH,
        )

    def whole(unit):
        group, index = UNITS[unit]
        return outs[group].at[index]

    own = []
    for unit in range(len(UNITS)):
        own.append(
            pltpu.make_async_copy(
                layer_ref.at[unit], whole(unit).at[z, y, c, x], local_sem.at[unit]
            )
        )
    own.append(
        pltpu.make_async_copy(head_ref, head_out.at[:, z, y, c], local_sem.at[len(UNITS)])
    )
    for piece in own:
        piece.start()
    count = len(order)

    def first(item):
        kind, unit = order[item]
        if kind == "h":
            src, dst = head_ref.at[unit], head_out.at[unit, z, y, c]
        else:
            src, dst = layer_ref.at[unit], whole(unit).at[z, y, c, x]
        return [copy(src, dst, item, slot, target) for slot, target in enumerate(z_dev)]

    def second(item):
        kind, unit = order[item]
        block = head_out.at[unit, :, y, c] if kind == "h" else whole(unit).at[:, y, c, x]
        return copy(block, block, item, 3, x_dev if kind == "b" else y_dev)

    def third(item):
        kind, unit = order[item]
        if kind == "h":
            return None
        block = whole(unit).at[:, :, c, x] if kind == "a" else whole(unit).at[:, y, c]
        return copy(block, block, item, 4, x_dev if kind == "a" else y_dev)

    def fourth(item):
        kind, unit = order[item]
        block = head_out.at[unit, :, :, c] if kind == "h" else whole(unit).at[:, :, c]
        return copy(block, block, item, 5, c_dev)

    for piece in own:
        piece.wait()
    late_two, late_three, late_four = delays
    for tick in range(count + late_four):
        if tick < count:
            for part in first(tick):
                part.start()
        item = tick - late_two
        if 0 <= item < count:
            for part in first(item):
                part.wait_recv()
            second(item).start()
        item = tick - late_three
        if 0 <= item < count:
            second(item).wait_recv()
            part = third(item)
            if part is not None:
                part.start()
        item = tick - late_four
        if 0 <= item < count:
            part = third(item)
            if part is not None:
                part.wait_recv()
            fourth(item).start()
    for item in range(count):
        fourth(item).wait_recv()
        for part in first(item) + [second(item), third(item), fourth(item)]:
            if part is not None:
                part.wait_send()


def gather_fast(layer, head):
    order = transfer_order(head.shape[0])
    count = len(order)
    shapes = [jax.ShapeDtypeStruct((size, 4, 2, 2, 2) + layer.shape[1:], BF) for size in GROUPS]
    shapes.append(jax.ShapeDtypeStruct((head.shape[0], 4, 2, 2) + head.shape[1:], BF))
    results = pl.pallas_call(
        functools.partial(gather_kernel, order, (1, 2, 3)),
        out_shape=tuple(shapes),
        in_specs=[pl.BlockSpec(memory_space=pltpu.VMEM)] * 2,
        out_specs=(pl.BlockSpec(memory_space=pl.ANY),) * len(shapes),
        scratch_shapes=[
            pltpu.SemaphoreType.DMA((count, 6)),
            pltpu.SemaphoreType.DMA((count, 6)),
            pltpu.SemaphoreType.DMA((len(UNITS) + 1,)),
        ],
        compiler_params=pltpu.CompilerParams(
            collective_id=1, has_side_effects=True, vmem_limit_bytes=32 * 2**20
        ),
    )(layer, head)
    weights = [
        part.reshape(size, -1, part.shape[-1]) for size, part in zip(GROUPS, results[:7])
    ]
    return weights, results[7].reshape(head.shape[0], -1, head.shape[2])


def reduce_kernel(order, delays, *refs):
    grads, head_grad = refs[:7], refs[7]
    out, head_out = refs[8:10]
    core_in, first_in, second_in, line_in, head_core, head_y, head_line, own, send_sem, recv_sem, local_sem = refs[10:]
    z, y, c, x = place()
    line, z_dev, y_dev, x_dev, c_dev = partners()
    greet(z_dev + [y_dev, x_dev, c_dev])
    count, slots = len(order), own.shape[0]

    def copy(src, dst, item, slot, target):
        return pltpu.make_async_remote_copy(
            src_ref=src,
            dst_ref=dst,
            send_sem=send_sem.at[item, slot],
            recv_sem=recv_sem.at[item, slot],
            device_id=target,
            device_id_type=MESH,
        )

    def whole(kind, unit):
        if kind == "h":
            return head_grad.at[unit]
        group, index = UNITS[unit]
        return grads[group].at[index]

    def to_core(item):
        kind, unit = order[item]
        target = head_core.at[unit] if kind == "h" else core_in.at[unit]
        return copy(whole(kind, unit).at[:, :, 1 - c], target, item, 0, c_dev)

    def own_half(item):
        kind, unit = order[item]
        slot = own.at[item % slots]
        if kind == "h":
            slot = slot.reshape(head_core.shape[1:])
        return pltpu.make_async_copy(whole(kind, unit).at[:, :, c], slot, local_sem.at[item % slots])

    def first(item):
        kind, unit = order[item]
        if kind == "h":
            return None
        if kind == "a":
            return copy(core_in.at[unit, :, :, 1 - x], first_in.at[unit], item, 1, x_dev)
        return copy(core_in.at[unit, :, 1 - y], first_in.at[unit], item, 1, y_dev)

    def second(item):
        kind, unit = order[item]
        if kind == "h":
            return copy(head_core.at[unit, :, 1 - y], head_y.at[unit], item, 2, y_dev)
        if kind == "a":
            return copy(first_in.at[unit, :, 1 - y], second_in.at[unit], item, 2, y_dev)
        return copy(first_in.at[unit, :, 1 - x], second_in.at[unit], item, 2, x_dev)

    def third(item):
        kind, unit = order[item]
        parts = []
        for slot, other in enumerate(line):
            if kind == "h":
                src, dst = head_y.at[unit, other], head_line.at[unit, slot]
            else:
                src, dst = second_in.at[unit, other], line_in.at[unit, slot]
            parts.append(copy(src, dst, item, 3 + slot, z_dev[slot]))
        return parts

    def wide(value):
        return value.astype(F32)

    late_one, late_two, late_three, late_four = delays
    for tick in range(count + late_four):
        if tick < count:
            to_core(tick).start()
            own_half(tick).start()
        item = tick - late_one
        if 0 <= item < count:
            kind, unit = order[item]
            own_half(item).wait()
            to_core(item).wait_recv()

            def join_core(k, carry):
                kept = own[item % slots, k]
                if kind == "h":
                    kept = kept.reshape(head_core.shape[2:])
                    head_core[unit, k] = (wide(head_core[unit, k]) + wide(kept)).astype(BF)
                else:
                    core_in[unit, k] = (wide(core_in[unit, k]) + wide(kept)).astype(BF)
                return carry

            lax.fori_loop(0, 4, join_core, 0)
            if kind != "h":
                first(item).start()
        item = tick - late_two
        if 0 <= item < count:
            kind, unit = order[item]
            if kind != "h":
                first(item).wait_recv()

                def join_first(k, carry):
                    kept = core_in[unit, k, :, x] if kind == "a" else core_in[unit, k, y]
                    first_in[unit, k] = (wide(first_in[unit, k]) + wide(kept)).astype(BF)
                    return carry

                lax.fori_loop(0, 4, join_first, 0)
            second(item).start()
        item = tick - late_three
        if 0 <= item < count:
            kind, unit = order[item]
            second(item).wait_recv()

            def join_second(k, carry):
                if kind == "h":
                    head_y[unit, k] = (wide(head_y[unit, k]) + wide(head_core[unit, k, y])).astype(BF)
                else:
                    kept = first_in[unit, k, y if kind == "a" else x]
                    second_in[unit, k] = (wide(second_in[unit, k]) + wide(kept)).astype(BF)
                return carry

            lax.fori_loop(0, 4, join_second, 0)
            for part in third(item):
                part.start()
        item = tick - late_four
        if 0 <= item < count:
            kind, unit = order[item]
            for part in third(item):
                part.wait_recv()
            held, landed = (head_y, head_line) if kind == "h" else (second_in, line_in)
            total = wide(held[unit, z])
            for slot in range(3):
                total = total + wide(landed[unit, slot])
            if kind == "h":
                head_out[unit] = total
            else:
                out[unit] = total
    for item in range(count):
        for part in [to_core(item), first(item), second(item)] + third(item):
            if part is not None:
                part.wait_send()


def reduce_fast(grads, head_grad):
    books, rows, width = head_grad.shape
    order = transfer_order(books)
    count = len(order)
    deep, head_deep = grads[0].shape[1] // 32, rows // 16
    split = [g.reshape(g.shape[0], 4, 2, 2, 2, deep, g.shape[2]) for g in grads]
    head_split = head_grad.reshape(books, 4, 2, 2, head_deep, width)
    tile, head_tile = (deep, grads[0].shape[2]), (head_deep, width)
    units = len(UNITS)
    vmem = pltpu.VMEM
    return pl.pallas_call(
        functools.partial(reduce_kernel, order, (2, 5, 8, 10)),
        out_shape=(
            jax.ShapeDtypeStruct((units,) + tile, F32),
            jax.ShapeDtypeStruct((books,) + head_tile, F32),
        ),
        in_specs=[pl.BlockSpec(memory_space=pl.ANY)] * 8,
        out_specs=(pl.BlockSpec(memory_space=vmem),) * 2,
        scratch_shapes=[
            vmem((units, 4, 2, 2) + tile, BF),
            vmem((units, 4, 2) + tile, BF),
            vmem((units, 4) + tile, BF),
            vmem((units, 3) + tile, BF),
            vmem((books, 4, 2) + head_tile, BF),
            vmem((books, 4) + head_tile, BF),
            vmem((books, 3) + head_tile, BF),
            vmem((4, 4, 2, 2) + tile, BF),
            pltpu.SemaphoreType.DMA((count, 6)),
            pltpu.SemaphoreType.DMA((count, 6)),
            pltpu.SemaphoreType.DMA((4,)),
        ],
        compiler_params=pltpu.CompilerParams(
            collective_id=2, has_side_effects=True, vmem_limit_bytes=58 * 2**20
        ),
    )(*split, head_split)


def lookup_kernel(ids_ref, table_ref, out_ref, stacked):
    books, columns, lanes = stacked.shape[0], out_ref.shape[1], stacked.shape[2]
    width = out_ref.shape[2]
    high_count = stacked.shape[1] // columns

    @pl.when(pl.program_id(0) == 0)
    def _():
        for book in range(books):
            for high in range(high_count):
                stacked[book, high * columns : (high + 1) * columns, :] = table_ref[
                    book, :, high * lanes : (high + 1) * lanes
                ].astype(BF)

    total = jnp.zeros((columns, width), F32)
    spread = lax.broadcasted_iota(jnp.int32, (lanes, width), 0)
    for book in range(books):
        ids = ids_ref[0, book : book + 1, :]
        low = ids % lanes
        high_ids = ids // lanes
        hot = jnp.where(spread == low, 1.0, 0.0).astype(BF)
        found = jnp.dot(stacked[book], hot, preferred_element_type=F32)
        for high in range(high_count):
            total = total + jnp.where(
                high_ids == high, found[high * columns : (high + 1) * columns], 0.0
            )
    out_ref[0] = total


def lookup(ids, table_t):
    blocks, books, width = ids.shape
    columns, rows = table_t.shape[1:]
    lanes = 256
    high_count = -(-rows // lanes)
    padded = jnp.pad(table_t, ((0, 0), (0, 0), (0, high_count * lanes - rows)))
    return pl.pallas_call(
        lookup_kernel,
        grid=(blocks,),
        out_shape=jax.ShapeDtypeStruct((blocks, columns, width), F32),
        in_specs=[
            pl.BlockSpec((1, books, width), lambda i: (i, 0, 0)),
            pl.BlockSpec(padded.shape, lambda i: (0, 0, 0)),
        ],
        out_specs=pl.BlockSpec((1, columns, width), lambda i: (i, 0, 0)),
        scratch_shapes=[pltpu.VMEM((books, high_count * columns, lanes), BF)],
        compiler_params=pltpu.CompilerParams(vmem_limit_bytes=40 * 2**20),
    )(ids, padded)


def spread_kernel(ids_ref, rows_ref, out_ref, total):
    books, columns, rows = out_ref.shape
    width = rows_ref.shape[2]
    lanes = total.shape[2]
    high_count = total.shape[1] // columns
    step = pl.program_id(0)

    @pl.when(step == 0)
    def _():
        total[...] = jnp.zeros_like(total)

    values = rows_ref[0].astype(F32)
    spread = lax.broadcasted_iota(jnp.int32, (lanes, width), 0)
    for book in range(books):
        ids = ids_ref[0, book : book + 1, :]
        low = ids % lanes
        high_ids = ids // lanes
        hot = jnp.where(spread == low, 1.0, 0.0).astype(BF)
        parted = jnp.concatenate(
            [jnp.where(high_ids == high, values, 0.0) for high in range(high_count)], axis=0
        ).astype(BF)
        total[book] += lax.dot_general(
            parted, hot, (((1,), (1,)), ((), ())), preferred_element_type=F32
        )

    @pl.when(step == pl.num_programs(0) - 1)
    def _():
        for book in range(books):
            for high in range(high_count):
                first = high * lanes
                last = min(rows, first + lanes)
                out_ref[book, :, first:last] = total[
                    book, high * columns : (high + 1) * columns, : last - first
                ]


def spread_rows(ids, values, rows):
    blocks, books, width = ids.shape
    columns = values.shape[1]
    lanes = 256
    high_count = -(-rows // lanes)
    return pl.pallas_call(
        spread_kernel,
        grid=(blocks,),
        out_shape=jax.ShapeDtypeStruct((books, columns, rows), F32),
        in_specs=[
            pl.BlockSpec((1, books, width), lambda i: (i, 0, 0)),
            pl.BlockSpec((1, columns, width), lambda i: (i, 0, 0)),
        ],
        out_specs=pl.BlockSpec((books, columns, rows), lambda i: (0, 0, 0)),
        scratch_shapes=[pltpu.VMEM((books, high_count * columns, lanes), F32)],
        compiler_params=pltpu.CompilerParams(vmem_limit_bytes=40 * 2**20),
    )(ids, values)


def low(values):
    return values.astype(BF)


def ein(formula, left, right):
    return jnp.einsum(formula, left, right, preferred_element_type=F32)


def norm_stats(values):
    average = jnp.mean(values, axis=-1, keepdims=True)
    centred = values - average
    spread = jnp.mean(centred * centred, axis=-1, keepdims=True)
    scale = lax.rsqrt(spread + NORM_EPS)
    return centred * scale, scale


def norm_forward(values, gain, bias):
    hat, scale = norm_stats(values)
    return hat * (1.0 + gain) + bias


def norm_backward(values, gain, cotangent):
    hat, scale = norm_stats(values)
    scaled = cotangent * (1.0 + gain)
    mean_one = jnp.mean(scaled, axis=-1, keepdims=True)
    mean_two = jnp.mean(scaled * hat, axis=-1, keepdims=True)
    return (
        (scaled - mean_one - hat * mean_two) * scale,
        jnp.sum(cotangent * hat, axis=0),
        jnp.sum(cotangent, axis=0),
    )


def sinusoid(frames, model_width):
    half_width = model_width // 2
    freq_rates = jnp.exp(
        jnp.arange(half_width, dtype=F32) * (-math.log(10000.0) / (half_width - 1))
    )
    angles = jnp.arange(frames, dtype=F32)[:, None] * freq_rates[None, :]
    return jnp.concatenate([jnp.sin(angles), jnp.cos(angles)], axis=1)


def delay_ids(codes, offsets, special):
    frames = codes.shape[2]
    frame = jnp.arange(frames, dtype=jnp.int32)[None, None, :]
    inputs = jnp.full_like(codes, special)
    targets = jnp.full_like(codes, special)
    padded = jnp.pad(codes, ((0, 0), (0, 0), (4, 0)), constant_values=special)
    for shift in range(4):
        is_shift = (offsets == shift)[:, :, None]
        targets = jnp.where(is_shift, padded[:, :, 4 - shift : 4 - shift + frames], targets)
        inputs = jnp.where(is_shift, padded[:, :, 3 - shift : 3 - shift + frames], inputs)
    return inputs, targets


def split_heads(matrix, clips):
    return matrix.reshape(clips, matrix.shape[0] // clips, HEADS, -1)


def raw_scores(queries, keyset, causal):
    scores = ein("bqhe,bkhe->bhqk", queries, keyset) * SCORE_SCALE
    if causal:
        length = scores.shape[2]
        allowed = jnp.arange(length)[:, None] >= jnp.arange(length)[None, :]
        scores = jnp.where(allowed[None, None], scores, NEG_FILL)
    return scores


def attend_forward(queries, keyset, valset, clips, causal):
    queries, keyset, valset = (split_heads(m, clips) for m in (queries, keyset, valset))
    scores = raw_scores(queries, keyset, causal)
    highest = jnp.max(scores, axis=-1, keepdims=True)
    exponents = jnp.exp(scores - highest)
    denominator = jnp.sum(exponents, axis=-1, keepdims=True)
    probs = exponents / denominator
    mixed = ein("bhqk,bkhe->bqhe", low(probs), valset)
    return low(mixed).reshape(mixed.shape[0] * mixed.shape[1], -1), probs


def attend_backward(queries, keyset, valset, probs, grad_mixed, clips):
    queries, keyset, valset, grad_mixed = (
        split_heads(m, clips) for m in (queries, keyset, valset, grad_mixed)
    )
    grad_probs = ein("bqhe,bkhe->bhqk", grad_mixed, valset)
    grad_values = low(ein("bhqk,bqhe->bkhe", low(probs), grad_mixed))
    grad_scores = low(
        probs * (grad_probs - jnp.sum(probs * grad_probs, axis=-1, keepdims=True))
    )
    grad_queries = low(ein("bhqk,bkhe->bqhe", grad_scores, keyset) * SCORE_SCALE)
    grad_keys = low(ein("bhqk,bqhe->bkhe", grad_scores, queries) * SCORE_SCALE)
    return tuple(
        m.reshape(m.shape[0] * m.shape[1], -1) for m in (grad_queries, grad_keys, grad_values)
    )


def normal_cdf(values):
    return 0.5 * (1.0 + lax.erf(values * math.sqrt(0.5)))


def adam_step(weight, first_moment, second_moment, gradient, factor, corr_one, corr_two):
    clipped = gradient * factor
    first_next = BETA_ONE * first_moment + (1.0 - BETA_ONE) * clipped
    second_next = BETA_TWO * second_moment + (1.0 - BETA_TWO) * clipped * clipped
    update = (
        first_next / corr_one / (jnp.sqrt(second_next / corr_two) + ADAM_EPS) + DECAY_RATE * weight
    )
    return (weight - LEARN_RATE * update, first_next, second_next)


def columns_apart(matrix, pieces):
    count, rows, width = matrix.shape
    parts = matrix.reshape(count, rows, pieces, width // pieces).transpose(0, 2, 1, 3)
    return parts.reshape(count * pieces, rows, width // pieces)


def columns_together(parts, pieces):
    total, rows, width = parts.shape
    matrix = parts.reshape(total // pieces, pieces, rows, width).transpose(0, 2, 1, 3)
    return matrix.reshape(total // pieces, rows, pieces * width)


def local(
    fast,
    audio_codes,
    delay_offsets,
    clip_lengths,
    loss_positions,
    teacher_ids,
    text_states,
    step_count,
    in_proj,
    in_proj_mean,
    in_proj_sq,
    out_proj,
    out_proj_mean,
    out_proj_sq,
    ffn_proj,
    ffn_proj_mean,
    ffn_proj_sq,
    embed_table,
    embed_table_mean,
    embed_table_sq,
    head_table,
    head_table_mean,
    head_table_sq,
    norm_gain,
    norm_gain_mean,
    norm_gain_sq,
    norm_bias,
    norm_bias_mean,
    norm_bias_sq,
):
    clips = text_states.shape[0]
    vocab_count = lax.axis_size("vocab")
    device_count = lax.axis_size("dp") * vocab_count
    vocab_index = lax.axis_index("vocab")
    book_count = head_table.shape[0]
    pos_count = loss_positions.shape[1]
    frames = audio_codes.shape[2]
    table_rows = embed_table.shape[1]
    special = table_rows - 1
    half_vocab = head_table.shape[2]
    vocab_base = vocab_index * half_vocab
    model_width = text_states.shape[2]
    rows = clips * frames
    ffn_pieces = ffn_proj.shape[2] // model_width
    denominator = float(clips * device_count * pos_count * book_count)

    inputs, targets = delay_ids(audio_codes, delay_offsets, special)
    own_first = vocab_index * clips
    own_inputs = lax.dynamic_slice_in_dim(inputs, own_first, clips, 0)
    own_positions = lax.dynamic_slice_in_dim(loss_positions, own_first, clips, 0)

    layer_local = jnp.concatenate(
        [
            low(in_proj[0:3]),
            low(out_proj[0:1]),
            low(in_proj[3:6]),
            low(out_proj[1:2]),
            columns_apart(low(ffn_proj), ffn_pieces),
        ],
        axis=0,
    )
    head_local = low(head_table)
    norms = lax.all_gather(
        low(jnp.concatenate([norm_gain, norm_bias], axis=0)), BOTH, axis=1, tiled=True
    ).astype(F32)
    gains, biases = norms[:4], norms[4:]
    if fast:
        all_inputs = lax.all_gather(inputs, "dp", axis=0, tiled=True)
        block_ids = (
            all_inputs.reshape(device_count, clips, book_count, frames)
            .transpose(0, 2, 1, 3)
            .reshape(device_count, book_count, rows)
        )
        table_t = jnp.swapaxes(embed_table, 1, 2)
        looked = lookup(block_ids, table_t)
        looked = lax.all_to_all(looked, BOTH, 0, 0, tiled=True)
        embedded = looked.reshape(model_width, rows).T
        layer_parts, head_all = gather_fast(layer_local, head_local)
    else:
        table = lax.all_gather(low(embed_table), BOTH, axis=2, tiled=True)
        embedded = jnp.zeros((rows, model_width), F32)
        for book in range(book_count):
            embedded = embedded + jnp.take(
                table[book], own_inputs[:, book].reshape(-1), axis=0
            ).astype(F32)
        layer_all = lax.all_gather(layer_local, BOTH, axis=1, tiled=True)
        starts = [sum(GROUPS[:g]) for g in range(len(GROUPS))]
        layer_parts = [layer_all[s : s + g] for s, g in zip(starts, GROUPS)]
        head_all = lax.all_gather(head_local, "dp", axis=1, tiled=True)
    w_self, w_self_out, w_query, w_text, w_cross_out, w_up, w_down = layer_parts

    start = embedded + jnp.tile(sinusoid(frames, model_width), (clips, 1))
    normed_self = low(norm_forward(start, gains[0], biases[0]))
    proj = low(ein("rd,kde->kre", normed_self, w_self))
    self_out, self_probs = attend_forward(proj[0], proj[1], proj[2], clips, True)
    after_self = start + ein("rd,de->re", self_out, w_self_out[0])
    normed_cross = low(norm_forward(after_self, gains[1], biases[1]))
    cross_query = low(ein("rd,de->re", normed_cross, w_query[0]))
    text = text_states.reshape(-1, model_width)
    cross_text = low(ein("td,kde->kte", text, w_text))
    cross_out, cross_probs = attend_forward(cross_query, cross_text[0], cross_text[1], clips, False)
    after_cross = after_self + ein("rd,de->re", cross_out, w_cross_out[0])
    normed_ffn = low(norm_forward(after_cross, gains[2], biases[2]))
    upper = ein("rd,jdf->jrf", normed_ffn, w_up)
    cdf = normal_cdf(upper)
    active = low(upper * cdf)
    after_ffn = after_cross + ein("jrf,jdf->rd", active, w_down)
    final_norm = low(norm_forward(after_ffn, gains[3], biases[3]))
    flat_positions = (own_positions + jnp.arange(clips, dtype=jnp.int32)[:, None] * frames).reshape(-1)
    pick = flat_positions[:, None] == jnp.arange(rows, dtype=jnp.int32)[None, :]
    chosen = low(ein("pr,rd->pd", pick.astype(BF), final_norm))

    pair_rows = lax.all_gather(chosen, "vocab", axis=0, tiled=True)
    pair_count = pair_rows.shape[0]
    target_at = jnp.take_along_axis(targets, loss_positions[:, None, :], axis=2)
    target_at = target_at.transpose(1, 0, 2).reshape(book_count, pair_count)
    teach = teacher_ids.transpose(1, 0, 2, 3).reshape(book_count, pair_count, -1)
    row_weight = (loss_positions < clip_lengths[:, None]).astype(F32).reshape(pair_count)
    local_ids = vocab_base + jnp.arange(half_vocab, dtype=jnp.int32)
    counts = jnp.sum(
        (teach[:, :, :, None] == local_ids[None, None, None, :]).astype(F32), axis=2
    )
    valid = (target_at != special).astype(F32)
    wanted = counts / teach.shape[2] + valid[:, :, None] * (
        target_at[:, :, None] == local_ids[None, None, :]
    ).astype(F32)
    logits = ein("rd,kdv->krv", pair_rows, head_all)
    highest = jnp.max(logits, axis=-1)
    exp_sum = jnp.sum(jnp.exp(logits - highest[:, :, None]), axis=-1)
    stats = lax.all_gather(jnp.stack([highest, exp_sum]), "vocab")
    top_all = jnp.max(stats[:, 0], axis=0)
    sum_all = jnp.sum(stats[:, 1] * jnp.exp(stats[:, 0] - top_all[None]), axis=0)
    log_total = top_all + jnp.log(sum_all)
    row_loss = row_weight[None, :] * (valid + 1.0) * log_total
    own_rows = clips * pos_count
    loss_sum = jnp.sum(
        lax.dynamic_slice_in_dim(row_loss, vocab_index * own_rows, own_rows, 1)
    ) - jnp.sum(row_weight[None, :] * jnp.sum(wanted * logits, axis=-1))
    scaled = (row_weight / denominator)[None, :, None]
    grad_logits = low(
        scaled * ((valid + 1.0)[:, :, None] * jnp.exp(logits - log_total[:, :, None]) - wanted)
    )
    grad_head = ein("rd,krv->kdv", pair_rows, grad_logits)
    grad_rows = ein("krv,kdv->rd", grad_logits, head_all)
    grad_chosen = lax.psum_scatter(low(grad_rows), "vocab", scatter_dimension=0, tiled=True).astype(F32)

    grad_final = jnp.einsum(
        "pr,pd->rd", pick.astype(F32), grad_chosen, precision=lax.Precision.HIGHEST
    )
    grad_ffn_res, gain_three, bias_three = norm_backward(after_ffn, gains[3], grad_final)
    low_ffn = low(grad_ffn_res)
    grad_down = ein("rd,jrf->jdf", low_ffn, active)
    grad_active = ein("rd,jdf->jrf", low_ffn, w_down)
    slope = cdf + upper * jnp.exp(-0.5 * upper * upper) * (1.0 / math.sqrt(2.0 * math.pi))
    grad_upper = low(grad_active * slope)
    grad_up = ein("rd,jrf->jdf", normed_ffn, grad_upper)
    grad_normed = ein("jrf,jdf->rd", grad_upper, w_up)
    grad_inner, gain_two, bias_two = norm_backward(after_cross, gains[2], grad_normed)
    grad_cross_res = grad_ffn_res + grad_inner
    low_cross = low(grad_cross_res)
    grad_cross_out = ein("rd,re->de", cross_out, low_cross)[None]
    grad_mixed = low(ein("re,de->rd", low_cross, w_cross_out[0]))
    grad_query, grad_key, grad_value = attend_backward(
        cross_query, cross_text[0], cross_text[1], cross_probs, grad_mixed, clips
    )
    grad_w_query = ein("rd,re->de", normed_cross, grad_query)[None]
    grad_w_text = ein("td,kte->kde", text, jnp.stack([grad_key, grad_value]))
    grad_normed = ein("re,de->rd", grad_query, w_query[0])
    grad_inner, gain_one, bias_one = norm_backward(after_self, gains[1], grad_normed)
    grad_self_res = grad_cross_res + grad_inner
    low_self = low(grad_self_res)
    grad_self_out = ein("rd,re->de", self_out, low_self)[None]
    grad_mixed = low(ein("re,de->rd", low_self, w_self_out[0]))
    grad_proj = jnp.stack(
        attend_backward(proj[0], proj[1], proj[2], self_probs, grad_mixed, clips)
    )
    grad_w_self = ein("rd,kre->kde", normed_self, grad_proj)
    grad_normed = ein("kre,kde->rd", grad_proj, w_self)
    grad_inner, gain_zero, bias_zero = norm_backward(start, gains[0], grad_normed)
    grad_start = grad_self_res + grad_inner

    layer_grads = (
        grad_w_self, grad_self_out, grad_w_query, grad_w_text, grad_cross_out, grad_up, grad_down
    )
    norm_grads = jnp.stack(
        [gain_zero, gain_one, gain_two, gain_three, bias_zero, bias_one, bias_two, bias_three]
    )
    norm_shard = lax.psum_scatter(norm_grads, BOTH, scatter_dimension=1, tiled=True)
    if fast:
        parted = low(grad_start).T.reshape(device_count, -1, rows)
        parted = lax.all_to_all(parted, BOTH, 0, 0, tiled=True)
        embed_shard = jnp.swapaxes(spread_rows(block_ids, parted, table_rows), 1, 2)
        layer_shard, head_shard = reduce_fast([low(g) for g in layer_grads], low(grad_head))
    else:
        embed_sum = jnp.stack(
            [
                jax.ops.segment_sum(
                    grad_start, own_inputs[:, book].reshape(-1), num_segments=table_rows
                )
                for book in range(book_count)
            ]
        )
        embed_shard = lax.psum_scatter(embed_sum, BOTH, scatter_dimension=2, tiled=True)
        layer_shard = lax.psum_scatter(
            jnp.concatenate(layer_grads, axis=0), BOTH, scatter_dimension=1, tiled=True
        )
        head_shard = lax.psum_scatter(grad_head, "dp", scatter_dimension=1, tiled=True)
    gradients = (
        jnp.concatenate([layer_shard[0:3], layer_shard[4:7]], axis=0),
        jnp.concatenate([layer_shard[3:4], layer_shard[7:8]], axis=0),
        columns_together(layer_shard[8:], ffn_pieces),
        embed_shard,
        head_shard,
        norm_shard[:4],
        norm_shard[4:],
    )
    square_sum = jnp.zeros((), F32)
    for shard_grad in gradients:
        square_sum = square_sum + jnp.sum(shard_grad * shard_grad)
    square_total, loss_total = lax.psum((square_sum, loss_sum), BOTH)
    loss_value = loss_total / denominator
    grad_norm = jnp.sqrt(square_total)
    factor = CLIP_LIMIT / jnp.maximum(grad_norm, CLIP_LIMIT)
    steps_float = step_count.astype(F32)
    corr_one = 1.0 - jnp.power(BETA_ONE, steps_float)
    corr_two = 1.0 - jnp.power(BETA_TWO, steps_float)
    masters = (in_proj, out_proj, ffn_proj, embed_table, head_table, norm_gain, norm_bias)
    mean_list = (
        in_proj_mean,
        out_proj_mean,
        ffn_proj_mean,
        embed_table_mean,
        head_table_mean,
        norm_gain_mean,
        norm_bias_mean,
    )
    square_list = (
        in_proj_sq,
        out_proj_sq,
        ffn_proj_sq,
        embed_table_sq,
        head_table_sq,
        norm_gain_sq,
        norm_bias_sq,
    )
    outputs = [loss_value, grad_norm]
    for index in range(7):
        outputs.extend(
            adam_step(
                masters[index],
                mean_list[index],
                square_list[index],
                gradients[index],
                factor,
                corr_one,
                corr_two,
            )
        )
    return tuple(outputs)


def solution(mesh):
    by_row = P(None, BOTH, None)
    by_column = P(None, None, BOTH)
    by_head = P(None, "dp", "vocab")
    by_feature = P(None, BOTH)
    weights = (
        (by_row,) * 9 + (by_column,) * 3 + (by_head,) * 3 + (by_feature,) * 6
    )
    placed = (
        P("dp", None, None),
        P("dp", None),
        P("dp"),
        P("dp", None),
        P("dp", None, None, None),
        P(BOTH, None, None),
        P(),
    ) + weights
    fast = dict(mesh.shape) == {"dp": 16, "vocab": 2}
    return jax.shard_map(
        functools.partial(local, fast),
        mesh=mesh,
        in_specs=placed,
        out_specs=(P(), P()) + weights,
        check_vma=False,
    )
```

```python
import functools
import math
from typing import Any, NamedTuple

import jax
import jax.numpy as jnp
from jax import lax
from jax.experimental import pallas as pl
from jax.experimental.pallas import tpu as pltpu
from jax.sharding import PartitionSpec as P

HEADS = 16
NORM_EPS = 1e-05
SCORE_SCALE = 0.125
NEG_FILL = -1e30
CLIP_LIMIT = 3.0
BETA_ONE = 0.9
BETA_TWO = 0.95
LEARN_RATE = 0.05
DECAY_RATE = 0.1
ADAM_EPS = 1e-08
BOTH = ("dp", "vocab")
MESH = pl.DeviceIdType.MESH
BF = jnp.bfloat16
F32 = jnp.float32
GROUPS = (3, 1, 1, 2, 1, 4, 4)
UNITS = tuple((group, index) for group, size in enumerate(GROUPS) for index in range(size))


def place():
    dp, x = lax.axis_index("dp"), lax.axis_index("vocab")
    return lax.div(dp, 4), lax.rem(lax.div(dp, 2), 2), lax.rem(dp, 2), x


def device(z, y, c, x):
    return ((z * 2 + y) * 2 + c, x)


def partners():
    z, y, c, x = place()
    line = [lax.rem(z + step, 4) for step in (1, 2, 3)]
    return (
        line,
        [device(other, y, c, x) for other in line],
        device(z, 1 - y, c, x),
        device(z, y, c, 1 - x),
        device(z, y, 1 - c, x),
    )


def greet(targets):
    barrier = pltpu.get_barrier_semaphore()
    for target in targets:
        pl.semaphore_signal(barrier, inc=1, device_id=target, device_id_type=MESH)
    pl.semaphore_wait(barrier, len(targets))


def transfer_order(heads):
    order, head = [], 0
    for unit in range(len(UNITS)):
        order.append(("b" if unit % 4 == 3 else "a", unit))
        if unit % 4 == 1 and head < heads:
            order.append(("h", head))
            head += 1
    return tuple(order)


def total_kernel(value_ref, out_ref, landed, send_sem, recv_sem):
    z, y, c, x = place()
    line, z_dev, y_dev, x_dev, c_dev = partners()
    greet(z_dev + [y_dev, x_dev, c_dev])

    def copy(src, dst, slot, target):
        return pltpu.make_async_remote_copy(
            src_ref=src,
            dst_ref=dst,
            send_sem=send_sem.at[slot],
            recv_sem=recv_sem.at[slot],
            device_id=target,
            device_id_type=MESH,
        )

    landed[z] = value_ref[...]
    parts = [copy(value_ref, landed.at[z], k, z_dev[k]) for k in range(3)]
    for part in parts:
        part.start()
    for part in parts:
        part.wait()
    landed[4] = landed[0] + landed[1] + landed[2] + landed[3]
    for step, target in enumerate((y_dev, x_dev, c_dev)):
        part = copy(landed.at[4 + 2 * step], landed.at[5 + 2 * step], 3 + step, target)
        part.start()
        part.wait()
        summed = landed[4 + 2 * step] + landed[5 + 2 * step]
        if step == 2:
            out_ref[...] = summed
        else:
            landed[6 + 2 * step] = summed


def total_over_all(value):
    return pl.pallas_call(
        total_kernel,
        out_shape=jax.ShapeDtypeStruct(value.shape, F32),
        in_specs=[pl.BlockSpec(memory_space=pltpu.VMEM)],
        out_specs=pl.BlockSpec(memory_space=pltpu.VMEM),
        scratch_shapes=[
            pltpu.VMEM((10,) + value.shape, F32),
            pltpu.SemaphoreType.DMA((6,)),
            pltpu.SemaphoreType.DMA((6,)),
        ],
        compiler_params=pltpu.CompilerParams(collective_id=4, has_side_effects=True),
    )(value)


def spread_kernel(ids_ref, rows_ref, out_ref, total):
    books, columns, rows = out_ref.shape
    width = rows_ref.shape[2]
    lanes = total.shape[2]
    high_count = total.shape[1] // columns
    step = pl.program_id(0)

    @pl.when(step == 0)
    def _():
        total[...] = jnp.zeros_like(total)

    values = rows_ref[0].astype(F32)
    spread = lax.broadcasted_iota(jnp.int32, (lanes, width), 0)
    for book in range(books):
        ids = ids_ref[0, book : book + 1, :]
        low = ids % lanes
        high_ids = ids // lanes
        hot = jnp.where(spread == low, 1.0, 0.0).astype(BF)
        parted = jnp.concatenate(
            [jnp.where(high_ids == high, values, 0.0) for high in range(high_count)], axis=0
        ).astype(BF)
        total[book] += lax.dot_general(
            parted, hot, (((1,), (1,)), ((), ())), preferred_element_type=F32
        )

    @pl.when(step == pl.num_programs(0) - 1)
    def _():
        for book in range(books):
            for high in range(high_count):
                first = high * lanes
                last = min(rows, first + lanes)
                out_ref[book, :, first:last] = total[
                    book, high * columns : (high + 1) * columns, : last - first
                ]


def spread_rows(ids, values, rows):
    blocks, books, width = ids.shape
    columns = values.shape[1]
    lanes = 256
    high_count = -(-rows // lanes)
    return pl.pallas_call(
        spread_kernel,
        grid=(blocks,),
        out_shape=jax.ShapeDtypeStruct((books, columns, rows), F32),
        in_specs=[
            pl.BlockSpec((1, books, width), lambda i: (i, 0, 0)),
            pl.BlockSpec((1, columns, width), lambda i: (i, 0, 0)),
        ],
        out_specs=pl.BlockSpec((books, columns, rows), lambda i: (0, 0, 0)),
        scratch_shapes=[pltpu.VMEM((books, high_count * columns, lanes), F32)],
        compiler_params=pltpu.CompilerParams(vmem_limit_bytes=40 * 2**20),
    )(ids, values)


PAIR, RES3, FFN, MIX2, CROSS, TEXT, MIX1, SELF = range(8)
LOGIT, ACT, UP = 0, 4, 8
RES2, QUERY2, KEY2, VALUE2, RES1, QUERY1, KEY1, VALUE1 = range(12, 20)
PLAN = (
    ("h", 0, PAIR, LOGIT + 0),
    ("a", 12, RES3, ACT + 0),
    ("a", 13, RES3, ACT + 1),
    ("h", 1, PAIR, LOGIT + 1),
    ("a", 8, FFN, UP + 0),
    ("a", 14, RES3, ACT + 2),
    ("b", 9, FFN, UP + 1),
    ("a", 15, RES3, ACT + 3),
    ("a", 10, FFN, UP + 2),
    ("h", 2, PAIR, LOGIT + 2),
    ("b", 11, FFN, UP + 3),
    ("a", 7, MIX2, RES2),
    ("a", 4, CROSS, QUERY2),
    ("b", 5, TEXT, KEY2),
    ("a", 6, TEXT, VALUE2),
    ("h", 3, PAIR, LOGIT + 3),
    ("a", 3, MIX1, RES1),
    ("a", 0, SELF, QUERY1),
    ("b", 1, SELF, KEY1),
    ("a", 2, SELF, VALUE1),
)
LATE = (2, 4, 6, 8)


def dot_nn(left, right):
    return jnp.dot(left, right, preferred_element_type=F32)


def dot_nt(left, right):
    return lax.dot_general(left, right, (((1,), (1,)), ((), ())), preferred_element_type=F32)


def dot_tn(left, right):
    return lax.dot_general(left, right, (((0,), (0,)), ((), ())), preferred_element_type=F32)


def chunk(index, size):
    return pl.ds(pl.multiple_of(index * size, size), size)


def norm_back_rows(values_ref, gain_ref, grad_ref, add_ref, out_ref, low_ref, gain_out, bias_out):
    size = 32
    one_gain = 1.0 + gain_ref[...]

    def block(index, carry):
        gain_sum, bias_sum = carry
        rows = chunk(index, size)
        values, cotangent = values_ref[rows, :], grad_ref[rows, :]
        average = jnp.mean(values, axis=-1, keepdims=True)
        centred = values - average
        scale = lax.rsqrt(jnp.mean(centred * centred, axis=-1, keepdims=True) + NORM_EPS)
        hat = centred * scale
        scaled = cotangent * one_gain
        mean_one = jnp.mean(scaled, axis=-1, keepdims=True)
        mean_two = jnp.mean(scaled * hat, axis=-1, keepdims=True)
        result = (scaled - mean_one - hat * mean_two) * scale
        if add_ref is not None:
            result = result + add_ref[rows, :]
        out_ref[rows, :] = result
        if low_ref is not None:
            low_ref[rows, :] = result.astype(BF)
        return (
            gain_sum + jnp.sum(cotangent * hat, axis=0, keepdims=True),
            bias_sum + jnp.sum(cotangent, axis=0, keepdims=True),
        )

    zero = jnp.zeros((1, values_ref.shape[1]), F32)
    gain_sum, bias_sum = lax.fori_loop(0, values_ref.shape[0] // size, block, (zero, zero))
    gain_out[...] = gain_sum
    bias_out[...] = bias_sum


def attend_back_rows(query, key, value, grad, query_out, key_out, value_out, clips, causal):
    rows, keys = query.shape[0] // clips, key.shape[0] // clips
    pairs = query.shape[1] // 128
    lane = lax.broadcasted_iota(jnp.int32, (1, 128), 1)
    halves = [(lane < 64).astype(F32).astype(BF), (lane >= 64).astype(F32).astype(BF)]

    def pair(index, carry):
        at_q = chunk(lax.div(index, pairs), rows)
        at_k = chunk(lax.div(index, pairs), keys)
        lanes = chunk(lax.rem(index, pairs), 128)
        q, k, v, g = query[at_q, lanes], key[at_k, lanes], value[at_k, lanes], grad[at_q, lanes]
        dq = jnp.zeros((rows, 128), F32)
        dk = jnp.zeros((keys, 128), F32)
        dv = jnp.zeros((keys, 128), F32)
        for half in halves:
            qh, kh, gh = q * half, k * half, g * half
            scores = dot_nt(qh, k) * SCORE_SCALE
            if causal:
                allowed = lax.broadcasted_iota(jnp.int32, (rows, keys), 0) >= lax.broadcasted_iota(
                    jnp.int32, (rows, keys), 1
                )
                scores = jnp.where(allowed, scores, NEG_FILL)
            exponents = jnp.exp(scores - jnp.max(scores, axis=-1, keepdims=True))
            probs = exponents / jnp.sum(exponents, axis=-1, keepdims=True)
            grad_probs = dot_nt(gh, v)
            dv = dv + dot_tn(probs.astype(BF), gh)
            inner = jnp.sum(probs * grad_probs, axis=-1, keepdims=True)
            grad_scores = (probs * (grad_probs - inner)).astype(BF)
            dq = dq + dot_nn(grad_scores, kh)
            dk = dk + dot_tn(grad_scores, qh)
        query_out[at_q, lanes] = (dq * SCORE_SCALE).astype(BF)
        key_out[at_k, lanes] = (dk * SCORE_SCALE).astype(BF)
        value_out[at_k, lanes] = dv.astype(BF)
        return carry

    lax.fori_loop(0, clips * pairs, pair, 0)


class BackwardRefs(NamedTuple):
    grad_logits: Any
    pair_rows: Any
    pick: Any
    x0: Any
    x1: Any
    x2: Any
    x3: Any
    h1: Any
    h2: Any
    h3: Any
    q1: Any
    k1: Any
    v1: Any
    o1: Any
    q2: Any
    k2: Any
    v2: Any
    o2: Any
    upper: Any
    act: Any
    text: Any
    gains: Any
    head: Any
    w0: Any
    w1: Any
    w2: Any
    w3: Any
    w4: Any
    w5: Any
    w6: Any
    layer_out: Any
    head_out: Any
    norm_out: Any
    start_out: Any
    core_in: Any
    first_in: Any
    second_in: Any
    line_in: Any
    head_y: Any
    head_line: Any
    core_slot: Any
    send_slot: Any
    held: Any
    acts: Any
    ups: Any
    logit: Any
    upper_slot: Any
    qkv: Any
    query2: Any
    kv2: Any
    left: Any
    left_pair: Any
    left_text: Any
    weight: Any
    lows: Any
    query2_grad: Any
    kv2_grad: Any
    grad_x: Any
    grad_h: Any
    values: Any
    rows_in: Any
    pair_in: Any
    pick_in: Any
    gain_in: Any
    pair_grad: Any
    pair_send: Any
    pair_land: Any
    send_sem: Any
    recv_sem: Any
    weight_sem: Any
    load_sem: Any
    core_sem: Any
    upper_sem: Any
    pair_sem: Any


def backward_kernel(clips, *refs):
    r = BackwardRefs(*refs)
    z, y, c, x = place()
    line, z_dev, y_dev, x_dev, c_dev = partners()
    items = PLAN
    count = len(items)
    frames_all = r.x0.shape[0]
    pieces = 4

    load_count = [0]

    def load(src, dst):
        piece = pltpu.make_async_copy(src, dst, r.load_sem.at[load_count[0]])
        load_count[0] += 1
        piece.start()
        return piece

    load_logit = load(r.grad_logits, r.logit)
    load_pair = load(r.pair_rows, r.pair_in)
    load_pick = load(r.pick, r.pick_in)
    load_gains = load(r.gains, r.gain_in)
    load_x3 = load(r.x3, r.values)
    load_act = load(r.act, r.acts)
    load_h3 = load(r.h3, r.rows_in.at[0])
    load_q1 = load(r.q1, r.qkv.at[0])
    load_k1 = load(r.k1, r.qkv.at[1])
    load_v1 = load(r.v1, r.qkv.at[2])
    load_q2 = load(r.q2, r.query2)
    load_k2 = load(r.k2, r.kv2.at[0])
    load_v2 = load(r.v2, r.kv2.at[1])

    sequence = [(r.head, k) for k in range(pieces)]
    sequence += [(ref, j) for j in range(pieces) for ref in (r.w6, r.w5)]
    sequence += [(r.w4, 0), (r.w2, 0), (r.w1, 0)] + [(r.w0, k) for k in range(3)]
    slots = r.weight.shape[0]
    taken = [0]

    def weight_copy(index):
        ref, at = sequence[index]
        return pltpu.make_async_copy(
            ref.at[at], r.weight.at[index % slots], r.weight_sem.at[index % slots]
        )

    for index in range(slots - 1):
        weight_copy(index).start()

    def next_weight():
        index = taken[0]
        taken[0] += 1
        if index + slots - 1 < len(sequence):
            weight_copy(index + slots - 1).start()
        weight_copy(index).wait()
        return r.weight.at[index % slots]

    def upper_copy(j):
        return pltpu.make_async_copy(
            r.upper.at[j], r.upper_slot.at[j % 2], r.upper_sem.at[j % 2]
        )

    upper_copy(0).start()
    upper_copy(1).start()
    greet(z_dev + [y_dev, x_dev, c_dev])

    left = (
        r.left_pair, r.left.at[0], r.left.at[1], r.left.at[2],
        r.left.at[3], r.left_text, r.left.at[0], r.left.at[1],
    )
    right = [r.logit.at[k] for k in range(pieces)]
    right += [r.acts.at[j] for j in range(pieces)] + [r.ups.at[j] for j in range(pieces)]
    right += [r.lows.at[1], r.query2_grad, r.kv2_grad.at[0], r.kv2_grad.at[1]]
    right += [r.acts.at[3], r.acts.at[0], r.acts.at[1], r.acts.at[2]]

    def copy(src, dst, item, slot, target):
        return pltpu.make_async_remote_copy(
            src_ref=src,
            dst_ref=dst,
            send_sem=r.send_sem.at[item, slot],
            recv_sem=r.recv_sem.at[item, slot],
            device_id=target,
            device_id_type=MESH,
        )

    held_slots = r.held.shape[0]

    def to_core(item):
        return copy(r.send_slot.at[item % 2], r.core_in.at[item], item, 0, c_dev)

    def core_load(item):
        return pltpu.make_async_copy(
            r.core_in.at[item], r.core_slot.at[item % 2], r.core_sem.at[item % 2]
        )

    def first(item):
        kind, unit = items[item][:2]
        held = r.held.at[item % held_slots]
        if kind == "a":
            return copy(held.at[:, :, 1 - x], r.first_in.at[unit], item, 1, x_dev)
        target = r.head_y if kind == "h" else r.first_in
        return copy(held.at[:, 1 - y], target.at[unit], item, 1, y_dev)

    def second(item):
        kind, unit = items[item][:2]
        if kind == "h":
            return None
        if kind == "a":
            return copy(r.first_in.at[unit, :, 1 - y], r.second_in.at[unit], item, 2, y_dev)
        return copy(r.first_in.at[unit, :, 1 - x], r.second_in.at[unit], item, 2, x_dev)

    def third(item):
        kind, unit = items[item][:2]
        ready, landed = (
            (r.head_y, r.head_line) if kind == "h" else (r.second_in, r.line_in)
        )
        return [
            copy(ready.at[unit, other], landed.at[unit, slot], item, 3 + slot, z_dev[slot])
            for slot, other in enumerate(line)
        ]

    def left_rows(name, core):
        ref = left[name]
        return jnp.concatenate(
            [ref[pl.ds(pl.multiple_of(k * 128 + core * 64, 64), 64), :] for k in range(8)], axis=0
        )

    def wide(value):
        return value.astype(F32)

    def make(item):
        kind, unit, left_name, right_name = items[item]
        if item >= 2:
            to_core(item - 2).wait_send()
        slot = r.send_slot.at[item % 2]

        def columns(n, carry):
            cols = chunk(n, 256)
            value = dot_nn(left_rows(left_name, 1 - c), right[right_name][:, cols]).astype(BF)
            slot[:, :, :, :, cols] = value.reshape(4, 2, 2, 32, 256)
            return carry

        lax.fori_loop(0, 4, columns, 0)
        to_core(item).start()

    def join_core(item):
        kind, unit, left_name, right_name = items[item]
        core_load(item).wait()
        if item >= held_slots:
            first(item - held_slots).wait_send()
        held, landed = r.held.at[item % held_slots], r.core_slot.at[item % 2]

        def columns(n, carry):
            cols = chunk(n, 256)
            value = dot_nn(left_rows(left_name, c), right[right_name][:, cols])
            value = value.reshape(4, 2, 2, 32, 256) + wide(landed[:, :, :, :, cols])
            held[:, :, :, :, cols] = value.astype(BF)
            return carry

        lax.fori_loop(0, 4, columns, 0)
        first(item).start()

    def join_first(item):
        kind, unit = items[item][:2]
        first(item).wait_recv()
        held = r.held.at[item % held_slots]
        target = r.head_y.at[unit] if kind == "h" else r.first_in.at[unit]

        def planes(k, carry):
            kept = held[k, :, x] if kind == "a" else held[k, y]
            target[k] = (wide(target[k]) + wide(kept)).astype(BF)
            return carry

        lax.fori_loop(0, 4, planes, 0)
        parts = third(item) if kind == "h" else [second(item)]
        for part in parts:
            part.start()

    def join_second(item):
        kind, unit = items[item][:2]
        if kind == "h":
            return
        second(item).wait_recv()

        def planes(k, carry):
            kept = r.first_in[unit, k, y if kind == "a" else x]
            r.second_in[unit, k] = (wide(r.second_in[unit, k]) + wide(kept)).astype(BF)
            return carry

        lax.fori_loop(0, 4, planes, 0)
        for part in third(item):
            part.start()

    def finish(item):
        kind, unit = items[item][:2]
        for part in third(item):
            part.wait_recv()
        if kind == "h":
            total = wide(r.head_y[unit, z])
            for slot in range(3):
                total = total + wide(r.head_line[unit, slot])
            r.head_out[unit] = total
        else:
            total = wide(r.second_in[unit, z])
            for slot in range(3):
                total = total + wide(r.line_in[unit, slot])
            r.layer_out[unit] = total

    ticks = [0]

    def pump():
        tick = ticks[0]
        ticks[0] += 1
        item = tick - 1
        if 0 <= item < count:
            to_core(item).wait_recv()
            core_load(item).start()
        for late, stage in zip(LATE, (join_core, join_first, join_second, finish)):
            item = tick - late
            if 0 <= item < count:
                stage(item)

    def unit(right_name):
        item = ticks[0]
        assert items[item][3] == right_name
        make(item)
        pump()

    load_logit.wait()
    load_pair.wait()
    r.left_pair[...] = r.pair_in[...].T
    unit(LOGIT + 0)

    def pair_rows_of(k, w):
        def columns(n, carry):
            cols = chunk(n, 256)
            value = dot_nt(r.logit[k], w[cols, :])
            r.pair_grad[:, cols] = value if k == 0 else r.pair_grad[:, cols] + value
            return carry

        lax.fori_loop(0, 4, columns, 0)

    for k in range(pieces):
        pair_rows_of(k, next_weight())
    half = r.pair_send.shape[0]
    r.pair_send[...] = r.pair_grad[chunk(1 - x, half), :].astype(BF)
    exchange = pltpu.make_async_remote_copy(
        src_ref=r.pair_send,
        dst_ref=r.pair_land,
        send_sem=r.pair_sem.at[0],
        recv_sem=r.pair_sem.at[1],
        device_id=x_dev,
        device_id_type=MESH,
    )
    exchange.start()
    load_h3.wait()
    r.left[1] = r.rows_in[0].T
    load_pick.wait()
    load_gains.wait()
    load_x3.wait()
    load_act.wait()
    exchange.wait()
    chosen = r.pair_grad[chunk(x, half), :].astype(BF).astype(F32) + wide(r.pair_land[...])
    chosen_top = chosen.astype(BF)
    chosen_rest = (chosen - wide(chosen_top)).astype(BF)
    r.grad_h[...] = dot_nn(r.pick_in[...], chosen_top) + dot_nn(r.pick_in[...], chosen_rest)

    def norm_back(index, add, low_ref):
        norm_back_rows(
            r.values,
            r.gain_in.at[index : index + 1],
            r.grad_h,
            add,
            r.grad_x,
            low_ref,
            r.norm_out.at[index : index + 1],
            r.norm_out.at[4 + index : 5 + index],
        )

    norm_back(3, None, r.lows.at[0])
    load_x2 = load(r.x2, r.values)
    r.left[0] = r.lows[0].T
    load_o2 = load(r.o2, r.rows_in.at[1])
    load_h2 = load(r.h2, r.rows_in.at[0])

    def down_back(j):
        w = next_weight()
        upper_copy(j).wait()

        def columns(n, carry):
            cols = chunk(n, 256)
            grad = dot_nn(r.lows[0], w[:, cols])
            upper = r.upper_slot[j % 2, :, cols]
            slope = 0.5 * (1.0 + lax.erf(upper * math.sqrt(0.5))) + upper * jnp.exp(
                -0.5 * upper * upper
            ) * (1.0 / math.sqrt(2.0 * math.pi))
            r.ups[j, :, cols] = (grad * slope).astype(BF)
            return carry

        lax.fori_loop(0, 4, columns, 0)
        if j + 2 < pieces:
            upper_copy(j + 2).start()

    def into_grad_h(value_ref, w, fresh):
        def columns(n, carry):
            cols = chunk(n, 256)
            value = dot_nt(value_ref[...], w[cols, :])
            r.grad_h[:, cols] = value if fresh else r.grad_h[:, cols] + value
            return carry

        lax.fori_loop(0, 4, columns, 0)

    def up_back(j):
        into_grad_h(r.ups.at[j], next_weight(), j == 0)

    unit(ACT + 0)
    down_back(0)
    unit(ACT + 1)
    up_back(0)
    unit(LOGIT + 1)
    unit(UP + 0)
    down_back(1)
    unit(ACT + 2)
    up_back(1)
    unit(UP + 1)
    down_back(2)
    unit(ACT + 3)
    up_back(2)
    unit(UP + 2)
    down_back(3)
    unit(LOGIT + 2)
    up_back(3)
    unit(UP + 3)
    load_x2.wait()
    norm_back(2, r.grad_x, r.lows.at[1])
    load_x1 = load(r.x1, r.values)

    load_o2.wait()
    r.left[2] = r.rows_in[1].T
    load_o1 = load(r.o1, r.rows_in.at[1])
    unit(RES2)
    for piece in (load_q2, load_k2, load_v2):
        piece.wait()

    def into_mixed(low_ref):
        w = next_weight()

        def columns(n, carry):
            cols = chunk(n, 256)
            r.lows[0, :, cols] = dot_nt(low_ref[...], w[cols, :]).astype(BF)
            return carry

        lax.fori_loop(0, 4, columns, 0)

    into_mixed(r.lows.at[1])
    attend_back_rows(
        r.query2, r.kv2.at[0], r.kv2.at[1], r.lows.at[0],
        r.query2_grad, r.kv2_grad.at[0], r.kv2_grad.at[1], clips, False,
    )
    load_h2.wait()
    r.left[3] = r.rows_in[0].T
    load_text = load(r.text, r.pair_in)
    unit(QUERY2)
    load_text.wait()
    r.left_text[...] = r.pair_in[...].T
    load_h1 = load(r.h1, r.rows_in.at[0])
    unit(KEY2)
    into_grad_h(r.query2_grad, next_weight(), True)
    unit(VALUE2)
    load_x1.wait()
    norm_back(1, r.grad_x, r.acts.at[3])
    load_x0 = load(r.x0, r.values)

    load_o1.wait()
    r.left[0] = r.rows_in[1].T
    unit(LOGIT + 3)
    unit(RES1)
    for piece in (load_q1, load_k1, load_v1):
        piece.wait()
    into_mixed(r.acts.at[3])
    attend_back_rows(
        r.qkv.at[0], r.qkv.at[1], r.qkv.at[2], r.lows.at[0],
        r.acts.at[0], r.acts.at[1], r.acts.at[2], clips, True,
    )
    load_h1.wait()
    r.left[1] = r.rows_in[0].T
    unit(QUERY1)
    into_grad_h(r.acts.at[0], next_weight(), True)
    unit(KEY1)
    into_grad_h(r.acts.at[1], next_weight(), False)
    unit(VALUE1)
    into_grad_h(r.acts.at[2], next_weight(), False)
    load_x0.wait()
    norm_back(0, r.grad_x, r.lows.at[1])
    r.start_out[...] = r.lows[1].T
    while ticks[0] < count + LATE[-1]:
        pump()
    for item in range(count):
        if item >= count - 2:
            to_core(item).wait_send()
        if item >= count - held_slots:
            first(item).wait_send()
        if items[item][0] != "h":
            second(item).wait_send()
        for part in third(item):
            part.wait_send()


def backward_fast(clips, operands):
    named = BackwardRefs(*operands, *(None,) * (len(BackwardRefs._fields) - len(operands)))
    rows, width = named.x0.shape
    pair_count = named.pair_rows.shape[0]
    text_rows = named.text.shape[0]
    books = named.head.shape[0]
    units, count = len(UNITS), len(PLAN)
    block = (32, width)
    vmem, dma = pltpu.VMEM, pltpu.SemaphoreType.DMA
    any_spec, vmem_spec = pl.BlockSpec(memory_space=pl.ANY), pl.BlockSpec(memory_space=vmem)
    held_slots = LATE[1] - LATE[0] + 1
    results = pl.pallas_call(
        functools.partial(backward_kernel, clips),
        out_shape=(
            jax.ShapeDtypeStruct((units,) + block, F32),
            jax.ShapeDtypeStruct((books, 2) + block, F32),
            jax.ShapeDtypeStruct((8, width), F32),
            jax.ShapeDtypeStruct((width, rows), BF),
            jax.ShapeDtypeStruct((count, 4, 2, 2) + block, BF),
        ),
        in_specs=[any_spec] * len(operands),
        out_specs=(vmem_spec,) * 4 + (any_spec,),
        scratch_shapes=[
            vmem((units, 4, 2) + block, BF),
            vmem((units, 4) + block, BF),
            vmem((units, 3) + block, BF),
            vmem((books, 4, 2) + block, BF),
            vmem((books, 3, 2) + block, BF),
            vmem((2, 4, 2, 2) + block, BF),
            vmem((2, 4, 2, 2) + block, BF),
            vmem((held_slots, 4, 2, 2) + block, BF),
            vmem((4, rows, width), BF),
            vmem((4, rows, width), BF),
            vmem((books, pair_count, width), BF),
            vmem((2, rows, width), F32),
            vmem((3, rows, width), BF),
            vmem((rows, width), BF),
            vmem((2, text_rows, width), BF),
            vmem((4, width, rows), BF),
            vmem((width, pair_count), BF),
            vmem((width, text_rows), BF),
            vmem((2, width, width), BF),
            vmem((2, rows, width), BF),
            vmem((rows, width), BF),
            vmem((2, text_rows, width), BF),
            vmem((rows, width), F32),
            vmem((rows, width), F32),
            vmem((rows, width), F32),
            vmem((2, rows, width), BF),
            vmem((pair_count, width), BF),
            vmem(named.pick.shape, BF),
            vmem(named.gains.shape, F32),
            vmem((pair_count, width), F32),
            vmem((pair_count // 2, width), BF),
            vmem((pair_count // 2, width), BF),
            dma((count, 6)),
            dma((count, 6)),
            dma((2,)),
            dma((24,)),
            dma((2,)),
            dma((2,)),
            dma((2,)),
        ],
        compiler_params=pltpu.CompilerParams(
            collective_id=2, has_side_effects=True, vmem_limit_bytes=60 * 2**20
        ),
    )(*operands)
    layer_shard, head_shard, norm_grads, start_grad = results[:4]
    return layer_shard, head_shard.reshape(books, -1, width), norm_grads, start_grad


class ForwardRefs(NamedTuple):
    ids: Any
    norms: Any
    table: Any
    layer: Any
    head_own: Any
    angles: Any
    text: Any
    pick: Any
    teach: Any
    row_info: Any
    ids_all: Any
    gains: Any
    loss: Any
    head: Any
    w0: Any
    w1: Any
    w2: Any
    w3: Any
    w4: Any
    w5: Any
    w6: Any
    grad_logits: Any
    pair_rows: Any
    x0: Any
    x1: Any
    x2: Any
    x3: Any
    h1: Any
    h2: Any
    h3: Any
    q1: Any
    k1: Any
    v1: Any
    o1: Any
    q2: Any
    k2: Any
    v2: Any
    o2: Any
    upper: Any
    act: Any
    norms_all: Any
    norm_rows: Any
    stacked: Any
    looked: Any
    landed: Any
    xs: Any
    hs: Any
    qkv: Any
    mixed: Any
    query2: Any
    kv2: Any
    uppers: Any
    acts: Any
    final: Any
    pair: Any
    wanted: Any
    logits: Any
    logit_grads: Any
    stats: Any
    weight: Any
    send_sem: Any
    recv_sem: Any
    local_sem: Any
    small_send: Any
    small_recv: Any
    look_send: Any
    look_recv: Any
    weight_sem: Any
    store_sem: Any
    pair_send: Any
    pair_recv: Any


GATHER_LATE = (2, 4, 6, 7)


def norm_rows_low(values_ref, gain_ref, bias_ref, low_ref):
    size = 32
    one_gain, bias = 1.0 + gain_ref[...], bias_ref[...]

    def block(index, carry):
        rows = chunk(index, size)
        values = values_ref[rows, :]
        average = jnp.mean(values, axis=-1, keepdims=True)
        centred = values - average
        spread = jnp.mean(centred * centred, axis=-1, keepdims=True)
        low_ref[rows, :] = (centred * lax.rsqrt(spread + NORM_EPS) * one_gain + bias).astype(BF)
        return carry

    lax.fori_loop(0, values_ref.shape[0] // size, block, 0)


def attend_rows(query, key, value, out, clips, causal):
    rows, keys = query.shape[0] // clips, key.shape[0] // clips
    pairs = query.shape[1] // 128
    lane = lax.broadcasted_iota(jnp.int32, (1, 128), 1)
    halves = [(lane < 64).astype(F32).astype(BF), (lane >= 64).astype(F32).astype(BF)]

    def pair(index, carry):
        at_q = chunk(lax.div(index, pairs), rows)
        at_k = chunk(lax.div(index, pairs), keys)
        lanes = chunk(lax.rem(index, pairs), 128)
        q, k, v = query[at_q, lanes], key[at_k, lanes], value[at_k, lanes]
        total = jnp.zeros((rows, 128), F32)
        for half in halves:
            scores = dot_nt(q * half, k) * SCORE_SCALE
            if causal:
                allowed = lax.broadcasted_iota(jnp.int32, (rows, keys), 0) >= lax.broadcasted_iota(
                    jnp.int32, (rows, keys), 1
                )
                scores = jnp.where(allowed, scores, NEG_FILL)
            exponents = jnp.exp(scores - jnp.max(scores, axis=-1, keepdims=True))
            probs = exponents / jnp.sum(exponents, axis=-1, keepdims=True)
            total = total + dot_nn(probs.astype(BF), v * half)
        out[at_q, lanes] = total.astype(BF)
        return carry

    lax.fori_loop(0, clips * pairs, pair, 0)


def forward_kernel(clips, denominator, special, *refs):
    r = ForwardRefs(*refs)
    z, y, c, x = place()
    me = lax.axis_index("dp") * 2 + x
    line, z_dev, y_dev, x_dev, c_dev = partners()
    books, frames = r.ids.shape[1], r.ids.shape[2]
    rows = clips * frames
    order = transfer_order(books)
    count = len(order)
    outs = (r.w0, r.w1, r.w2, r.w3, r.w4, r.w5, r.w6)
    columns, lanes = r.looked.shape[1], r.stacked.shape[2]
    high_count = r.stacked.shape[1] // columns
    devices = 32

    def device_of(index):
        return (lax.div(index, 2), lax.rem(index, 2))

    barrier = pltpu.get_barrier_semaphore()

    def signal(step, carry):
        pl.semaphore_signal(
            barrier, inc=1, device_id=device_of(lax.rem(me + step, devices)), device_id_type=MESH
        )
        return carry

    lax.fori_loop(1, devices, signal, 0)
    pl.semaphore_wait(barrier, devices - 1)

    def copy(src, dst, item, slot, target):
        return pltpu.make_async_remote_copy(
            src_ref=src,
            dst_ref=dst,
            send_sem=r.send_sem.at[item, slot],
            recv_sem=r.recv_sem.at[item, slot],
            device_id=target,
            device_id_type=MESH,
        )

    def whole(unit):
        group, index = UNITS[unit]
        return outs[group].at[index]

    own = [
        pltpu.make_async_copy(r.layer.at[unit], whole(unit).at[z, y, c, x], r.local_sem.at[unit])
        for unit in range(len(UNITS))
    ]
    own.append(
        pltpu.make_async_copy(r.head_own, r.head.at[:, z, y, c], r.local_sem.at[len(UNITS)])
    )

    def first(item):
        kind, unit = order[item]
        if kind == "h":
            src, dst = r.head_own.at[unit], r.head.at[unit, z, y, c]
        else:
            src, dst = r.layer.at[unit], whole(unit).at[z, y, c, x]
        return [copy(src, dst, item, slot, target) for slot, target in enumerate(z_dev)]

    def second(item):
        kind, unit = order[item]
        block = r.head.at[unit, :, y, c] if kind == "h" else whole(unit).at[:, y, c, x]
        parts = [
            copy(block, block, item, 3, x_dev if kind == "b" else y_dev),
            copy(block, block, item, 6, c_dev),
        ]
        if kind != "h":
            parts.append(copy(block, block, item, 4, y_dev if kind == "b" else x_dev))
        return parts

    def third(item):
        kind, unit = order[item]
        if kind == "h":
            block = r.head.at[unit, :, 1 - y, c]
        elif kind == "b":
            block = whole(unit).at[:, y, c, 1 - x]
        else:
            block = whole(unit).at[:, 1 - y, c, x]
        parts = [copy(block, block, item, 7, c_dev)]
        if kind != "h":
            parts.append(copy(block, block, item, 5, y_dev if kind == "b" else x_dev))
        return parts

    def fourth(item):
        kind, unit = order[item]
        if kind == "h":
            return []
        block = whole(unit).at[:, 1 - y, c] if kind == "b" else whole(unit).at[:, :, c, 1 - x]
        return [copy(block, block, item, 8, c_dev)]

    ticks = [0]

    def pump():
        tick = ticks[0]
        ticks[0] += 1
        if tick < count:
            for part in first(tick):
                part.start()
        item = tick - GATHER_LATE[0]
        if 0 <= item < count:
            for part in first(item):
                part.wait_recv()
            for part in second(item):
                part.start()
        item = tick - GATHER_LATE[1]
        if 0 <= item < count:
            second(item)[0].wait_recv()
            for part in third(item):
                part.start()
        item = tick - GATHER_LATE[2]
        if 0 <= item < count:
            for part in second(item)[2:] + third(item)[1:]:
                part.wait_recv()
            for part in fourth(item):
                part.start()
        item = tick - GATHER_LATE[3]
        if 0 <= item < count:
            for part in [second(item)[1], third(item)[0]] + fourth(item):
                part.wait_recv()
        advance_loads()

    item_of = {entry: item for item, entry in enumerate(order)}

    def ticks_for(kind, unit):
        return item_of[kind, unit] + GATHER_LATE[3] + 1

    def unit_kind(unit):
        return "b" if unit % 4 == 3 else "a"

    taken, loading = [0], [0]
    weight_slots = r.weight.shape[0]
    sequence = [(unit_kind(unit), unit) for unit in range(len(UNITS))]
    sequence += [("h", k) for k in range(books)]

    def weight_copy(index):
        kind, unit = sequence[index]
        slot = index % weight_slots
        if kind == "h":
            src, dst = r.head.at[unit], r.weight.at[slot].reshape(r.head.shape[1:])
        else:
            src, dst = whole(unit), r.weight.at[slot].reshape(whole(unit).shape)
        return pltpu.make_async_copy(src, dst, r.weight_sem.at[slot])

    def advance_loads():
        while (
            loading[0] < min(len(sequence), taken[0] + weight_slots)
            and ticks_for(*sequence[loading[0]]) <= ticks[0]
        ):
            weight_copy(loading[0]).start()
            loading[0] += 1

    def next_weight():
        index = taken[0]
        while loading[0] <= index:
            pump()
        weight_copy(index).wait()
        taken[0] += 1
        return r.weight.at[index % weight_slots]

    stores = []

    def store(src, dst):
        piece = pltpu.make_async_copy(src, dst, r.store_sem.at[len(stores)])
        piece.start()
        stores.append(piece)

    def small(block, slot, target):
        return pltpu.make_async_remote_copy(
            src_ref=block,
            dst_ref=block,
            send_sem=r.small_send.at[slot],
            recv_sem=r.small_recv.at[slot],
            device_id=target,
            device_id_type=MESH,
        )

    for piece in own:
        piece.start()
    r.ids_all[z, y, c] = r.ids[...]
    r.norms_all[z, y, c, x] = r.norms[...]
    small_stages = (
        [small(r.ids_all.at[z, y, c], k, z_dev[k]) for k in range(3)]
        + [small(r.norms_all.at[z, y, c, x], 3 + k, z_dev[k]) for k in range(3)],
        [small(r.ids_all.at[:, y, c], 6, y_dev), small(r.norms_all.at[:, y, c, x], 7, y_dev)],
        [small(r.ids_all.at[:, :, c], 8, c_dev), small(r.norms_all.at[:, :, c, x], 9, c_dev)],
        [small(r.norms_all.at[:, :, :, x], 10, x_dev)],
    )
    for number, stage in enumerate(small_stages):
        for part in stage:
            part.start()
        if number == 0:
            for piece in own:
                piece.wait()
            pump()
            pump()
            for book in range(books):
                for high in range(high_count):
                    r.stacked[book, high * columns : (high + 1) * columns, :] = r.table[
                        book, :, high * lanes : (high + 1) * lanes
                    ].astype(BF)
        for part in stage:
            part.wait()
        if number == 2:
            pump()
    for group in range(8):
        parts = [
            r.norms_all[group // 2, group % 2, j // 2, j % 2] for j in range(4)
        ]
        r.norm_rows[:, group * 128 : (group + 1) * 128] = parts[0] + parts[1] + parts[2] + parts[3]
    r.gains[...] = r.norm_rows[0:4, :]

    spread = lax.broadcasted_iota(jnp.int32, (lanes, rows), 0)

    def look_block(step, carry):
        target = lax.rem(me + step, devices)
        dp, member = lax.div(target, 2), lax.rem(target, 2)
        at = (lax.div(dp, 4), lax.rem(lax.div(dp, 2), 2), lax.rem(dp, 2))
        total = jnp.zeros((columns, rows), F32)
        for book in range(books):
            ids = jnp.concatenate(
                [r.ids_all[(*at, clips * member + m, pl.ds(book, 1))] for m in range(clips)], axis=1
            )
            low_ids, high_ids = ids & (lanes - 1), lax.shift_right_logical(ids, 8)
            hot = jnp.where(spread == low_ids, 1.0, 0.0).astype(BF)
            found = dot_nn(r.stacked[book], hot)
            for high in range(high_count):
                total = total + jnp.where(
                    high_ids == high, found[high * columns : (high + 1) * columns], 0.0
                )
        r.looked[step] = total
        return carry

    def look_copy(step):
        return pltpu.make_async_remote_copy(
            src_ref=r.looked.at[step],
            dst_ref=r.landed.at[me],
            send_sem=r.look_send.at[step],
            recv_sem=r.look_recv.at[step],
            device_id=device_of(lax.rem(me + step, devices)),
            device_id_type=MESH,
        )

    def look_and_send(step, carry):
        look_block(step, carry)
        look_copy(step).start()
        return carry

    for part in range(4):
        lax.fori_loop(1 + 8 * part, min(9 + 8 * part, devices), look_and_send, 0)
        pump()
    look_block(0, 0)
    r.landed[me] = r.looked[0]

    code = lax.broadcasted_iota(jnp.int32, (128, r.teach.shape[2]), 0)
    teach_count = r.teach.shape[1] - 8

    def want(book):
        def block(index, carry):
            here = code + index * 128
            total = jnp.zeros(here.shape, F32)
            for i in range(teach_count):
                total = total + jnp.where(here == r.teach[book, i : i + 1, :], 1.0, 0.0)
            hit = jnp.where(here == r.teach[book, teach_count : teach_count + 1, :], 1.0, 0.0)
            r.wanted[book, :, chunk(index, 128)] = (total * (1.0 / teach_count) + hit).T
            return carry

        lax.fori_loop(0, r.wanted.shape[2] // 128, block, 0)

    for book in range(books):
        want(book)
        pump()

    def look_wait(step, carry):
        look_copy(step).wait_recv()
        return carry

    lax.fori_loop(1, devices, look_wait, 0)

    def place_rows(index, carry):
        cols = chunk(index, 128)
        block = jnp.concatenate([r.landed[index * 4 + j] for j in range(4)], axis=0).T
        angles = r.angles[:, cols]
        r.xs[0, :, cols] = block + jnp.concatenate([angles] * clips, axis=0)
        return carry

    lax.fori_loop(0, r.xs.shape[2] // 128, place_rows, 0)

    def norm(index, low_ref):
        norm_rows_low(
            r.xs.at[index],
            r.norm_rows.at[index : index + 1],
            r.norm_rows.at[4 + index : 5 + index],
            low_ref,
        )

    def product(left_ref, w, out_ref):
        def part(n, carry):
            cols = chunk(n, 256)
            out_ref[:, cols] = dot_nn(left_ref[...], w[:, cols]).astype(BF)
            return carry

        lax.fori_loop(0, 4, part, 0)

    def residual(left_ref, w, before, after):
        def part(n, carry):
            cols = chunk(n, 256)
            r.xs[after, :, cols] = r.xs[before, :, cols] + dot_nn(left_ref[...], w[:, cols])
            return carry

        lax.fori_loop(0, 4, part, 0)

    store(r.xs.at[0], r.x0)
    norm(0, r.hs.at[0])
    store(r.hs.at[0], r.h1)
    for k in range(3):
        product(r.hs.at[0], next_weight(), r.qkv.at[k])
        store(r.qkv.at[k], (r.q1, r.k1, r.v1)[k])
    pump()
    attend_rows(r.qkv.at[0], r.qkv.at[1], r.qkv.at[2], r.mixed.at[0], clips, True)
    store(r.mixed.at[0], r.o1)
    residual(r.mixed.at[0], next_weight(), 0, 1)
    store(r.xs.at[1], r.x1)
    norm(1, r.hs.at[1])
    store(r.hs.at[1], r.h2)
    product(r.hs.at[1], next_weight(), r.query2)
    store(r.query2, r.q2)
    for k in range(2):
        product(r.text, next_weight(), r.kv2.at[k])
        store(r.kv2.at[k], (r.k2, r.v2)[k])
    pump()
    attend_rows(r.query2, r.kv2.at[0], r.kv2.at[1], r.mixed.at[1], clips, False)
    store(r.mixed.at[1], r.o2)
    residual(r.mixed.at[1], next_weight(), 1, 2)
    store(r.xs.at[2], r.x2)
    norm(2, r.hs.at[2])
    store(r.hs.at[2], r.h3)
    pieces = r.uppers.shape[0]
    for j in range(pieces):
        w = next_weight()

        def part(n, carry):
            cols = chunk(n, 256)
            upper = dot_nn(r.hs[2], w[:, cols])
            r.uppers[j, :, cols] = upper
            r.acts[j, :, cols] = (upper * (0.5 * (1.0 + lax.erf(upper * math.sqrt(0.5))))).astype(BF)
            return carry

        lax.fori_loop(0, 4, part, 0)
        store(r.uppers.at[j], r.upper.at[j])
        store(r.acts.at[j], r.act.at[j])
    for j in range(pieces):
        w = next_weight()

        def part(n, carry):
            cols = chunk(n, 256)
            before = r.xs[2, :, cols] if j == 0 else r.xs[3, :, cols]
            r.xs[3, :, cols] = before + dot_nt(r.acts[j], w[cols, :])
            return carry

        lax.fori_loop(0, 4, part, 0)
    store(r.xs.at[3], r.x3)
    norm(3, r.final)
    half = r.pair.shape[1]
    r.pair[x] = dot_nn(r.pick[...], r.final[...]).astype(BF)

    def exchange(ref, slot):
        return pltpu.make_async_remote_copy(
            src_ref=ref.at[x],
            dst_ref=ref.at[x],
            send_sem=r.pair_send.at[slot],
            recv_sem=r.pair_recv.at[slot],
            device_id=x_dev,
            device_id_type=MESH,
        )

    trade = exchange(r.pair, 0)
    trade.start()
    trade.wait()
    pair_count = 2 * half
    stat_lane = lax.broadcasted_iota(jnp.int32, (pair_count, 128), 1)
    stats = jnp.zeros((pair_count, 128), F32)
    for k in range(books):
        w = next_weight()

        def part(n, carry):
            cols = chunk(n, 256)
            pair = jnp.concatenate([r.pair[0], r.pair[1]], axis=0)
            r.logits[k, :, cols] = dot_nn(pair, w[:, cols])
            return carry

        lax.fori_loop(0, 4, part, 0)
        highest = jnp.max(r.logits[k], axis=-1, keepdims=True)
        exp_sum = jnp.sum(jnp.exp(r.logits[k] - highest), axis=-1, keepdims=True)
        stats = jnp.where(stat_lane == k, highest, stats)
        stats = jnp.where(stat_lane == books + k, exp_sum, stats)
    r.stats[x] = stats
    trade = exchange(r.stats, 1)
    trade.start()
    store(r.pair.at[0], r.pair_rows.at[0])
    store(r.pair.at[1], r.pair_rows.at[1])
    trade.wait()
    weight_col = r.row_info[:, books : books + 1]
    owned = r.row_info[:, books + 1 : books + 2]
    loss_col = jnp.zeros((pair_count, 1), F32)
    for k in range(books):
        valid = r.row_info[:, k : k + 1]
        tops = [r.stats[m][:, k : k + 1] for m in range(2)]
        sums = [r.stats[m][:, books + k : books + k + 1] for m in range(2)]
        top = jnp.maximum(tops[0], tops[1])
        log_total = top + jnp.log(sums[0] * jnp.exp(tops[0] - top) + sums[1] * jnp.exp(tops[1] - top))
        loss_col = loss_col + owned * weight_col * (valid + 1.0) * log_total
        scaled = weight_col * (1.0 / denominator)

        def part(n, total):
            cols = chunk(n, 256)
            logits, wanted = r.logits[k, :, cols], r.wanted[k, :, cols]
            r.logit_grads[k, :, cols] = (
                scaled * ((valid + 1.0) * jnp.exp(logits - log_total) - wanted)
            ).astype(BF)
            return total + jnp.sum(wanted * logits, axis=-1, keepdims=True)

        picked = lax.fori_loop(0, 4, part, jnp.zeros((pair_count, 1), F32))
        loss_col = loss_col - weight_col * picked
        store(r.logit_grads.at[k], r.grad_logits.at[k])
    r.loss[...] = jnp.broadcast_to(jnp.sum(loss_col, axis=0, keepdims=True), r.loss.shape)

    def look_done(step, carry):
        look_copy(step).wait_send()
        return carry

    lax.fori_loop(1, devices, look_done, 0)
    for item in range(count):
        for part in first(item) + second(item) + third(item) + fourth(item):
            part.wait_send()
    for piece in stores:
        piece.wait()


def forward_fast(clips, denominator, special, operands):
    named = ForwardRefs(*operands, *(None,) * (len(ForwardRefs._fields) - len(operands)))
    books, frames = named.ids.shape[1:]
    rows, width = clips * frames, named.layer.shape[2]
    text_rows, pair_count = named.text.shape[0], named.teach.shape[2]
    codes, columns = named.head_own.shape[2], named.table.shape[1]
    lanes = 256
    high_count = named.table.shape[2] // lanes
    count = books + len(UNITS)
    pieces = GROUPS[-1]
    vmem, dma = pltpu.VMEM, pltpu.SemaphoreType.DMA
    any_spec, vmem_spec = pl.BlockSpec(memory_space=pl.ANY), pl.BlockSpec(memory_space=vmem)

    def shaped(shape, dtype=BF):
        return jax.ShapeDtypeStruct(shape, dtype)

    in_vmem = (
        shaped((4, 2, 2) + named.ids.shape, jnp.int32),
        shaped((4, width), F32),
        shaped((8, 128), F32),
    )
    in_hbm = (
        (shaped((books, 4, 2, 2) + named.head_own.shape[1:]),)
        + tuple(shaped((size, 4, 2, 2, 2) + named.layer.shape[1:]) for size in GROUPS)
        + (shaped((books, pair_count, codes)), shaped((2, pair_count // 2, width)))
        + (shaped((rows, width), F32),) * 4
        + (shaped((rows, width)),) * 8
        + (shaped((text_rows, width)),) * 2
        + (shaped((rows, width)), shaped((pieces, rows, width), F32), shaped((pieces, rows, width)))
    )
    results = pl.pallas_call(
        functools.partial(forward_kernel, clips, denominator, special),
        out_shape=in_vmem + in_hbm,
        in_specs=[vmem_spec] * len(operands),
        out_specs=(vmem_spec,) * len(in_vmem) + (any_spec,) * len(in_hbm),
        scratch_shapes=[
            vmem((4, 2, 2, 2, 8, 128), F32),
            vmem((8, width), F32),
            vmem((books, high_count * columns, lanes), BF),
            vmem((32, columns, rows), F32),
            vmem((32, columns, rows), F32),
            vmem((4, rows, width), F32),
            vmem((3, rows, width), BF),
            vmem((3, rows, width), BF),
            vmem((2, rows, width), BF),
            vmem((rows, width), BF),
            vmem((2, text_rows, width), BF),
            vmem((pieces, rows, width), F32),
            vmem((pieces, rows, width), BF),
            vmem((rows, width), BF),
            vmem((2, pair_count // 2, width), BF),
            vmem((books, pair_count, codes), F32),
            vmem((books, pair_count, codes), F32),
            vmem((books, pair_count, codes), BF),
            vmem((2, pair_count, 128), F32),
            vmem((3, width, width), BF),
            dma((count, 9)),
            dma((count, 9)),
            dma((len(UNITS) + 1,)),
            dma((11,)),
            dma((11,)),
            dma((32,)),
            dma((32,)),
            dma((3,)),
            dma((40,)),
            dma((2,)),
            dma((2,)),
        ],
        compiler_params=pltpu.CompilerParams(
            collective_id=1, has_side_effects=True, vmem_limit_bytes=58 * 2**20
        ),
    )(*operands)
    return ForwardRefs(
        *operands,
        *results,
        *(None,) * (len(ForwardRefs._fields) - len(operands) - len(results)),
    )


def low(values):
    return values.astype(BF)


def ein(formula, left, right):
    return jnp.einsum(formula, left, right, preferred_element_type=F32)


def norm_stats(values):
    average = jnp.mean(values, axis=-1, keepdims=True)
    centred = values - average
    spread = jnp.mean(centred * centred, axis=-1, keepdims=True)
    scale = lax.rsqrt(spread + NORM_EPS)
    return centred * scale, scale


def norm_forward(values, gain, bias):
    hat, scale = norm_stats(values)
    return hat * (1.0 + gain) + bias


def norm_backward(values, gain, cotangent):
    hat, scale = norm_stats(values)
    scaled = cotangent * (1.0 + gain)
    mean_one = jnp.mean(scaled, axis=-1, keepdims=True)
    mean_two = jnp.mean(scaled * hat, axis=-1, keepdims=True)
    return (
        (scaled - mean_one - hat * mean_two) * scale,
        jnp.sum(cotangent * hat, axis=0),
        jnp.sum(cotangent, axis=0),
    )


def sinusoid(frames, model_width):
    half_width = model_width // 2
    freq_rates = jnp.exp(
        jnp.arange(half_width, dtype=F32) * (-math.log(10000.0) / (half_width - 1))
    )
    angles = jnp.arange(frames, dtype=F32)[:, None] * freq_rates[None, :]
    return jnp.concatenate([jnp.sin(angles), jnp.cos(angles)], axis=1)


def delay_ids(codes, offsets, special):
    frames = codes.shape[2]
    frame = jnp.arange(frames, dtype=jnp.int32)[None, None, :]
    inputs = jnp.full_like(codes, special)
    targets = jnp.full_like(codes, special)
    padded = jnp.pad(codes, ((0, 0), (0, 0), (4, 0)), constant_values=special)
    for shift in range(4):
        is_shift = (offsets == shift)[:, :, None]
        targets = jnp.where(is_shift, padded[:, :, 4 - shift : 4 - shift + frames], targets)
        inputs = jnp.where(is_shift, padded[:, :, 3 - shift : 3 - shift + frames], inputs)
    return inputs, targets


def split_heads(matrix, clips):
    return matrix.reshape(clips, matrix.shape[0] // clips, HEADS, -1)


def raw_scores(queries, keyset, causal):
    scores = ein("bqhe,bkhe->bhqk", queries, keyset) * SCORE_SCALE
    if causal:
        length = scores.shape[2]
        allowed = jnp.arange(length)[:, None] >= jnp.arange(length)[None, :]
        scores = jnp.where(allowed[None, None], scores, NEG_FILL)
    return scores


def attend_forward(queries, keyset, valset, clips, causal):
    queries, keyset, valset = (split_heads(m, clips) for m in (queries, keyset, valset))
    scores = raw_scores(queries, keyset, causal)
    highest = jnp.max(scores, axis=-1, keepdims=True)
    exponents = jnp.exp(scores - highest)
    denominator = jnp.sum(exponents, axis=-1, keepdims=True)
    probs = exponents / denominator
    mixed = ein("bhqk,bkhe->bqhe", low(probs), valset)
    return low(mixed).reshape(mixed.shape[0] * mixed.shape[1], -1), probs


def attend_backward(queries, keyset, valset, probs, grad_mixed, clips):
    queries, keyset, valset, grad_mixed = (
        split_heads(m, clips) for m in (queries, keyset, valset, grad_mixed)
    )
    grad_probs = ein("bqhe,bkhe->bhqk", grad_mixed, valset)
    grad_values = low(ein("bhqk,bqhe->bkhe", low(probs), grad_mixed))
    grad_scores = low(
        probs * (grad_probs - jnp.sum(probs * grad_probs, axis=-1, keepdims=True))
    )
    grad_queries = low(ein("bhqk,bkhe->bqhe", grad_scores, keyset) * SCORE_SCALE)
    grad_keys = low(ein("bhqk,bqhe->bkhe", grad_scores, queries) * SCORE_SCALE)
    return tuple(
        m.reshape(m.shape[0] * m.shape[1], -1) for m in (grad_queries, grad_keys, grad_values)
    )


def normal_cdf(values):
    return 0.5 * (1.0 + lax.erf(values * math.sqrt(0.5)))


def adam_step(weight, first_moment, second_moment, gradient, factor, corr_one, corr_two):
    clipped = gradient * factor
    first_next = BETA_ONE * first_moment + (1.0 - BETA_ONE) * clipped
    second_next = BETA_TWO * second_moment + (1.0 - BETA_TWO) * clipped * clipped
    update = (
        first_next / corr_one / (jnp.sqrt(second_next / corr_two) + ADAM_EPS) + DECAY_RATE * weight
    )
    return (weight - LEARN_RATE * update, first_next, second_next)


def columns_apart(matrix, pieces):
    count, rows, width = matrix.shape
    parts = matrix.reshape(count, rows, pieces, width // pieces).transpose(0, 2, 1, 3)
    return parts.reshape(count * pieces, rows, width // pieces)


def columns_together(parts, pieces):
    total, rows, width = parts.shape
    matrix = parts.reshape(total // pieces, pieces, rows, width).transpose(0, 2, 1, 3)
    return matrix.reshape(total // pieces, rows, pieces * width)


def local(
    fast,
    audio_codes,
    delay_offsets,
    clip_lengths,
    loss_positions,
    teacher_ids,
    text_states,
    step_count,
    in_proj,
    in_proj_mean,
    in_proj_sq,
    out_proj,
    out_proj_mean,
    out_proj_sq,
    ffn_proj,
    ffn_proj_mean,
    ffn_proj_sq,
    embed_table,
    embed_table_mean,
    embed_table_sq,
    head_table,
    head_table_mean,
    head_table_sq,
    norm_gain,
    norm_gain_mean,
    norm_gain_sq,
    norm_bias,
    norm_bias_mean,
    norm_bias_sq,
):
    clips = text_states.shape[0]
    vocab_count = lax.axis_size("vocab")
    device_count = lax.axis_size("dp") * vocab_count
    vocab_index = lax.axis_index("vocab")
    book_count = head_table.shape[0]
    pos_count = loss_positions.shape[1]
    frames = audio_codes.shape[2]
    table_rows = embed_table.shape[1]
    special = table_rows - 1
    half_vocab = head_table.shape[2]
    vocab_base = vocab_index * half_vocab
    model_width = text_states.shape[2]
    rows = clips * frames
    ffn_pieces = ffn_proj.shape[2] // model_width
    denominator = float(clips * device_count * pos_count * book_count)

    inputs, targets = delay_ids(audio_codes, delay_offsets, special)
    own_first = vocab_index * clips
    own_inputs = lax.dynamic_slice_in_dim(inputs, own_first, clips, 0)
    own_positions = lax.dynamic_slice_in_dim(loss_positions, own_first, clips, 0)

    layer_local = jnp.concatenate(
        [
            low(in_proj[0:3]),
            low(out_proj[0:1]),
            low(in_proj[3:6]),
            low(out_proj[1:2]),
            columns_apart(low(ffn_proj), ffn_pieces),
        ],
        axis=0,
    )
    head_local = low(head_table)
    norms_local = low(jnp.concatenate([norm_gain, norm_bias], axis=0))
    target_at = jnp.take_along_axis(targets, loss_positions[:, None, :], axis=2)
    pair_count = target_at.shape[0] * pos_count
    target_at = target_at.transpose(1, 0, 2).reshape(book_count, pair_count)
    valid = (target_at != special).astype(F32)
    row_weight = (loss_positions < clip_lengths[:, None]).astype(F32).reshape(pair_count)
    flat_positions = (own_positions + jnp.arange(clips, dtype=jnp.int32)[:, None] * frames).reshape(-1)
    pick = flat_positions[:, None] == jnp.arange(rows, dtype=jnp.int32)[None, :]
    text = text_states.reshape(-1, model_width)
    angles = sinusoid(frames, model_width)
    if fast:
        device_index = lax.axis_index("dp") * vocab_count + vocab_index
        norm_width = norm_gain.shape[1]
        norms_placed = lax.dynamic_update_slice(
            jnp.zeros((8, 128), F32),
            norms_local.astype(F32),
            (0, lax.rem(device_index, 128 // norm_width) * norm_width),
        )
        table_t = jnp.swapaxes(embed_table, 1, 2)
        table_t = jnp.pad(table_t, ((0, 0), (0, 0), (0, -table_rows % 256)))
        teach = jnp.concatenate(
            [
                teacher_ids.transpose(1, 3, 0, 2).reshape(book_count, -1, pair_count) - vocab_base,
                jnp.where(target_at == special, -1, target_at - vocab_base)[:, None, :],
                jnp.full((book_count, 7, pair_count), -1, jnp.int32),
            ],
            axis=1,
        )
        owned = (jnp.arange(pair_count) // (clips * pos_count) == vocab_index).astype(F32)
        row_info = jnp.concatenate([valid, row_weight[None], owned[None]], axis=0).T
        row_info = jnp.pad(row_info, ((0, 0), (0, 128 - row_info.shape[1])))
        kept = forward_fast(
            clips,
            denominator,
            special,
            (
                inputs,
                norms_placed,
                table_t,
                layer_local,
                head_local,
                angles,
                text,
                pick.astype(BF),
                teach,
                row_info,
            ),
        )
        block_ids = (
            kept.ids_all.reshape(device_count, clips, book_count, frames)
            .transpose(0, 2, 1, 3)
            .reshape(device_count, book_count, rows)
        )
        loss_sum = kept.loss[0, 0]

        def joined(part):
            return part.reshape(part.shape[0], -1, part.shape[-1])

        layer_shard, head_shard, norm_grads, start_grad = backward_fast(
            clips,
            (
                kept.grad_logits,
                kept.pair_rows.reshape(pair_count, model_width),
                pick.T.astype(BF),
                kept.x0,
                kept.x1,
                kept.x2,
                kept.x3,
                kept.h1,
                kept.h2,
                kept.h3,
                kept.q1,
                kept.k1,
                kept.v1,
                kept.o1,
                kept.q2,
                kept.k2,
                kept.v2,
                kept.o2,
                kept.upper,
                kept.act,
                text,
                kept.gains,
                joined(kept.head),
                joined(kept.w0),
                joined(kept.w1),
                joined(kept.w2),
                joined(kept.w3),
                joined(kept.w4),
                joined(kept.w5),
                joined(kept.w6),
            ),
        )
        parted = start_grad.reshape(device_count, -1, rows)
        parted = lax.all_to_all(parted, BOTH, 0, 0, tiled=True)
        embed_shard = jnp.swapaxes(spread_rows(block_ids, parted, table_rows), 1, 2)
    else:
        norms = lax.all_gather(norms_local, BOTH, axis=1, tiled=True).astype(F32)
        table = lax.all_gather(low(embed_table), BOTH, axis=2, tiled=True)
        embedded = jnp.zeros((rows, model_width), F32)
        for book in range(book_count):
            embedded = embedded + jnp.take(
                table[book], own_inputs[:, book].reshape(-1), axis=0
            ).astype(F32)
        layer_all = lax.all_gather(layer_local, BOTH, axis=1, tiled=True)
        starts = [sum(GROUPS[:g]) for g in range(len(GROUPS))]
        layer_parts = [layer_all[s : s + g] for s, g in zip(starts, GROUPS)]
        head_all = lax.all_gather(head_local, "dp", axis=1, tiled=True)
        w_self, w_self_out, w_query, w_text, w_cross_out, w_up, w_down = layer_parts
        gains, biases = norms[:4], norms[4:]

        start = embedded + jnp.tile(angles, (clips, 1))
        normed_self = low(norm_forward(start, gains[0], biases[0]))
        proj = low(ein("rd,kde->kre", normed_self, w_self))
        self_out, self_probs = attend_forward(proj[0], proj[1], proj[2], clips, True)
        after_self = start + ein("rd,de->re", self_out, w_self_out[0])
        normed_cross = low(norm_forward(after_self, gains[1], biases[1]))
        cross_query = low(ein("rd,de->re", normed_cross, w_query[0]))
        cross_text = low(ein("td,kde->kte", text, w_text))
        cross_out, cross_probs = attend_forward(cross_query, cross_text[0], cross_text[1], clips, False)
        after_cross = after_self + ein("rd,de->re", cross_out, w_cross_out[0])
        normed_ffn = low(norm_forward(after_cross, gains[2], biases[2]))
        upper = ein("rd,jdf->jrf", normed_ffn, w_up)
        cdf = normal_cdf(upper)
        active = low(upper * cdf)
        after_ffn = after_cross + ein("jrf,jdf->rd", active, w_down)
        final_norm = low(norm_forward(after_ffn, gains[3], biases[3]))
        chosen = low(ein("pr,rd->pd", pick.astype(BF), final_norm))

        pair_rows = lax.all_gather(chosen, "vocab", axis=0, tiled=True)
        teach = teacher_ids.transpose(1, 0, 2, 3).reshape(book_count, pair_count, -1)
        local_ids = vocab_base + jnp.arange(half_vocab, dtype=jnp.int32)
        counts = jnp.sum(
            (teach[:, :, :, None] == local_ids[None, None, None, :]).astype(F32), axis=2
        )
        wanted = counts / teach.shape[2] + valid[:, :, None] * (
            target_at[:, :, None] == local_ids[None, None, :]
        ).astype(F32)
        logits = ein("rd,kdv->krv", pair_rows, head_all)
        highest = jnp.max(logits, axis=-1)
        exp_sum = jnp.sum(jnp.exp(logits - highest[:, :, None]), axis=-1)
        stats = lax.all_gather(jnp.stack([highest, exp_sum]), "vocab")
        top_all = jnp.max(stats[:, 0], axis=0)
        sum_all = jnp.sum(stats[:, 1] * jnp.exp(stats[:, 0] - top_all[None]), axis=0)
        log_total = top_all + jnp.log(sum_all)
        row_loss = row_weight[None, :] * (valid + 1.0) * log_total
        own_rows = clips * pos_count
        loss_sum = jnp.sum(
            lax.dynamic_slice_in_dim(row_loss, vocab_index * own_rows, own_rows, 1)
        ) - jnp.sum(row_weight[None, :] * jnp.sum(wanted * logits, axis=-1))
        scaled = (row_weight / denominator)[None, :, None]
        grad_logits = low(
            scaled * ((valid + 1.0)[:, :, None] * jnp.exp(logits - log_total[:, :, None]) - wanted)
        )
        grad_head = ein("rd,krv->kdv", pair_rows, grad_logits)
        grad_rows = ein("krv,kdv->rd", grad_logits, head_all)
        grad_chosen = lax.psum_scatter(low(grad_rows), "vocab", scatter_dimension=0, tiled=True).astype(F32)

        grad_final = jnp.einsum(
            "pr,pd->rd", pick.astype(F32), grad_chosen, precision=lax.Precision.HIGHEST
        )
        grad_ffn_res, gain_three, bias_three = norm_backward(after_ffn, gains[3], grad_final)
        low_ffn = low(grad_ffn_res)
        grad_down = ein("rd,jrf->jdf", low_ffn, active)
        grad_active = ein("rd,jdf->jrf", low_ffn, w_down)
        slope = cdf + upper * jnp.exp(-0.5 * upper * upper) * (1.0 / math.sqrt(2.0 * math.pi))
        grad_upper = low(grad_active * slope)
        grad_up = ein("rd,jrf->jdf", normed_ffn, grad_upper)
        grad_normed = ein("jrf,jdf->rd", grad_upper, w_up)
        grad_inner, gain_two, bias_two = norm_backward(after_cross, gains[2], grad_normed)
        grad_cross_res = grad_ffn_res + grad_inner
        low_cross = low(grad_cross_res)
        grad_cross_out = ein("rd,re->de", cross_out, low_cross)[None]
        grad_mixed = low(ein("re,de->rd", low_cross, w_cross_out[0]))
        grad_query, grad_key, grad_value = attend_backward(
            cross_query, cross_text[0], cross_text[1], cross_probs, grad_mixed, clips
        )
        grad_w_query = ein("rd,re->de", normed_cross, grad_query)[None]
        grad_w_text = ein("td,kte->kde", text, jnp.stack([grad_key, grad_value]))
        grad_normed = ein("re,de->rd", grad_query, w_query[0])
        grad_inner, gain_one, bias_one = norm_backward(after_self, gains[1], grad_normed)
        grad_self_res = grad_cross_res + grad_inner
        low_self = low(grad_self_res)
        grad_self_out = ein("rd,re->de", self_out, low_self)[None]
        grad_mixed = low(ein("re,de->rd", low_self, w_self_out[0]))
        grad_proj = jnp.stack(
            attend_backward(proj[0], proj[1], proj[2], self_probs, grad_mixed, clips)
        )
        grad_w_self = ein("rd,kre->kde", normed_self, grad_proj)
        grad_normed = ein("kre,kde->rd", grad_proj, w_self)
        grad_inner, gain_zero, bias_zero = norm_backward(start, gains[0], grad_normed)
        grad_start = grad_self_res + grad_inner

        layer_grads = (
            grad_w_self, grad_self_out, grad_w_query, grad_w_text, grad_cross_out, grad_up, grad_down
        )
        norm_grads = jnp.stack(
            [gain_zero, gain_one, gain_two, gain_three, bias_zero, bias_one, bias_two, bias_three]
        )
        embed_sum = jnp.stack(
            [
                jax.ops.segment_sum(
                    grad_start, own_inputs[:, book].reshape(-1), num_segments=table_rows
                )
                for book in range(book_count)
            ]
        )
        embed_shard = lax.psum_scatter(embed_sum, BOTH, scatter_dimension=2, tiled=True)
        layer_shard = lax.psum_scatter(
            jnp.concatenate(layer_grads, axis=0), BOTH, scatter_dimension=1, tiled=True
        )
        head_shard = lax.psum_scatter(grad_head, "dp", scatter_dimension=1, tiled=True)
    big_gradients = (
        jnp.concatenate([layer_shard[0:3], layer_shard[4:7]], axis=0),
        jnp.concatenate([layer_shard[3:4], layer_shard[7:8]], axis=0),
        columns_together(layer_shard[8:], ffn_pieces),
        embed_shard,
        head_shard,
    )
    square_sum = jnp.zeros((), F32)
    for shard_grad in big_gradients:
        square_sum = square_sum + jnp.sum(shard_grad * shard_grad)
    if fast:
        scalars = jnp.pad(jnp.stack([square_sum, loss_sum])[None], ((0, 7), (0, model_width - 2)))
        totals = total_over_all(jnp.concatenate([norm_grads, scalars], axis=0))
        norm_total, square_total, loss_total = totals[:8], totals[8, 0], totals[8, 1]
    else:
        norm_total = lax.psum(norm_grads, BOTH)
        square_total, loss_total = lax.psum((square_sum, loss_sum), BOTH)
    square_total = square_total + jnp.sum(norm_total * norm_total)
    norm_width = norm_gain.shape[1]
    norm_shard = lax.dynamic_slice_in_dim(
        norm_total, (lax.axis_index("dp") * vocab_count + vocab_index) * norm_width, norm_width, 1
    )
    gradients = big_gradients + (norm_shard[:4], norm_shard[4:])
    loss_value = loss_total / denominator
    grad_norm = jnp.sqrt(square_total)
    factor = CLIP_LIMIT / jnp.maximum(grad_norm, CLIP_LIMIT)
    steps_float = step_count.astype(F32)
    corr_one = 1.0 - jnp.power(BETA_ONE, steps_float)
    corr_two = 1.0 - jnp.power(BETA_TWO, steps_float)
    masters = (in_proj, out_proj, ffn_proj, embed_table, head_table, norm_gain, norm_bias)
    mean_list = (
        in_proj_mean,
        out_proj_mean,
        ffn_proj_mean,
        embed_table_mean,
        head_table_mean,
        norm_gain_mean,
        norm_bias_mean,
    )
    square_list = (
        in_proj_sq,
        out_proj_sq,
        ffn_proj_sq,
        embed_table_sq,
        head_table_sq,
        norm_gain_sq,
        norm_bias_sq,
    )
    outputs = [loss_value, grad_norm]
    for index in range(7):
        outputs.extend(
            adam_step(
                masters[index],
                mean_list[index],
                square_list[index],
                gradients[index],
                factor,
                corr_one,
                corr_two,
            )
        )
    return tuple(outputs)


def solution(mesh):
    by_row = P(None, BOTH, None)
    by_column = P(None, None, BOTH)
    by_head = P(None, "dp", "vocab")
    by_feature = P(None, BOTH)
    weights = (
        (by_row,) * 9 + (by_column,) * 3 + (by_head,) * 3 + (by_feature,) * 6
    )
    placed = (
        P("dp", None, None),
        P("dp", None),
        P("dp"),
        P("dp", None),
        P("dp", None, None, None),
        P(BOTH, None, None),
        P(),
    ) + weights
    fast = dict(mesh.shape) == {"dp": 16, "vocab": 2}
    return jax.shard_map(
        functools.partial(local, fast),
        mesh=mesh,
        in_specs=placed,
        out_specs=(P(), P()) + weights,
        check_vma=False,
    )
```

```python
import functools
import math
from typing import Any, NamedTuple

import jax
import jax.numpy as jnp
from jax import lax
from jax.experimental import pallas as pl
from jax.experimental.pallas import tpu as pltpu
from jax.sharding import PartitionSpec as P

HEADS = 16
NORM_EPS = 1e-05
SCORE_SCALE = 0.125
NEG_FILL = -1e30
CLIP_LIMIT = 3.0
BETA_ONE = 0.9
BETA_TWO = 0.95
LEARN_RATE = 0.05
DECAY_RATE = 0.1
ADAM_EPS = 1e-08
BOTH = ("dp", "vocab")
MESH = pl.DeviceIdType.MESH
BF = jnp.bfloat16
F32 = jnp.float32
DEVICES = 32
GROUPS = (3, 1, 1, 2, 1, 4, 4)
UNITS = tuple((group, index) for group, size in enumerate(GROUPS) for index in range(size))


def place():
    dp, x = lax.axis_index("dp"), lax.axis_index("vocab")
    return lax.div(dp, 4), lax.rem(lax.div(dp, 2), 2), lax.rem(dp, 2), x


def device(z, y, c, x):
    return ((z * 2 + y) * 2 + c, x)


def partners():
    z, y, c, x = place()
    line = [lax.rem(z + step, 4) for step in (1, 2, 3)]
    return (
        line,
        [device(other, y, c, x) for other in line],
        device(z, 1 - y, c, x),
        device(z, y, c, 1 - x),
        device(z, y, 1 - c, x),
    )


def device_of(index):
    return (lax.div(index, 2), lax.rem(index, 2))


def greet_all(me):
    barrier = pltpu.get_barrier_semaphore()

    def signal(step, carry):
        pl.semaphore_signal(
            barrier, inc=1, device_id=device_of(lax.rem(me + step, DEVICES)), device_id_type=MESH
        )
        return carry

    lax.fori_loop(1, DEVICES, signal, 0)
    pl.semaphore_wait(barrier, DEVICES - 1)


def transfer_order(heads):
    order, head = [], 0
    for unit in range(len(UNITS)):
        order.append(("a", unit))
        if unit % 4 == 1 and head < heads:
            order.append(("h", head))
            head += 1
    return tuple(order)


PAIR, RES3, FFN, MIX2, CROSS, TEXT, MIX1, SELF = range(8)
LOGIT, ACT, UP = 0, 4, 8
RES2, QUERY2, KEY2, VALUE2, RES1, QUERY1, KEY1, VALUE1 = range(12, 20)
PLAN = (
    ("h", 0, PAIR, LOGIT + 0),
    ("h", 1, PAIR, LOGIT + 1),
    ("h", 2, PAIR, LOGIT + 2),
    ("h", 3, PAIR, LOGIT + 3),
    ("a", 12, RES3, ACT + 0),
    ("a", 13, RES3, ACT + 1),
    ("a", 14, RES3, ACT + 2),
    ("a", 15, RES3, ACT + 3),
    ("a", 8, FFN, UP + 0),
    ("a", 7, MIX2, RES2),
    ("a", 4, CROSS, QUERY2),
    ("a", 5, TEXT, KEY2),
    ("a", 6, TEXT, VALUE2),
    ("a", 3, MIX1, RES1),
    ("a", 9, FFN, UP + 1),
    ("a", 0, SELF, QUERY1),
    ("a", 1, SELF, KEY1),
    ("a", 2, SELF, VALUE1),
    ("a", 10, FFN, UP + 2),
    ("a", 11, FFN, UP + 3),
)
LATE = (2, 4, 6, 8)
HEAD_LATE = (2, 10, 12, 13)


def dot_nn(left, right):
    return jnp.dot(left, right, preferred_element_type=F32)


def dot_nt(left, right):
    return lax.dot_general(left, right, (((1,), (1,)), ((), ())), preferred_element_type=F32)


def dot_tn(left, right):
    return lax.dot_general(left, right, (((0,), (0,)), ((), ())), preferred_element_type=F32)


def chunk(index, size):
    return pl.ds(pl.multiple_of(index * size, size), size)


def norm_back_rows(values_ref, gain_ref, grad_ref, add_ref, out_ref, low_ref, gain_out, bias_out):
    size = 32
    one_gain = 1.0 + gain_ref[...]

    def block(index, carry):
        gain_sum, bias_sum = carry
        rows = chunk(index, size)
        values, cotangent = values_ref[rows, :], grad_ref[rows, :]
        average = jnp.mean(values, axis=-1, keepdims=True)
        centred = values - average
        scale = lax.rsqrt(jnp.mean(centred * centred, axis=-1, keepdims=True) + NORM_EPS)
        hat = centred * scale
        scaled = cotangent * one_gain
        mean_one = jnp.mean(scaled, axis=-1, keepdims=True)
        mean_two = jnp.mean(scaled * hat, axis=-1, keepdims=True)
        result = (scaled - mean_one - hat * mean_two) * scale
        if add_ref is not None:
            result = result + add_ref[rows, :]
        out_ref[rows, :] = result
        if low_ref is not None:
            low_ref[rows, :] = result.astype(BF)
        return (
            gain_sum + jnp.sum(cotangent * hat, axis=0, keepdims=True),
            bias_sum + jnp.sum(cotangent, axis=0, keepdims=True),
        )

    zero = jnp.zeros((1, values_ref.shape[1]), F32)
    gain_sum, bias_sum = lax.fori_loop(0, values_ref.shape[0] // size, block, (zero, zero))
    gain_out[...] = gain_sum
    bias_out[...] = bias_sum


def attend_back_rows(query, key, value, grad, query_out, key_out, value_out, clips, causal, share):
    rows, keys = query.shape[0] // clips, key.shape[0] // clips
    pairs = query.shape[1] // 128
    lane = lax.broadcasted_iota(jnp.int32, (1, 128), 1)
    halves = [(lane < 64).astype(F32).astype(BF), (lane >= 64).astype(F32).astype(BF)]

    def pair(index, carry):
        at_q = chunk(lax.div(index, pairs), rows)
        at_k = chunk(lax.div(index, pairs), keys)
        lanes = chunk(lax.rem(index, pairs), 128)
        q, k, v, g = query[at_q, lanes], key[at_k, lanes], value[at_k, lanes], grad[at_q, lanes]
        dq = jnp.zeros((rows, 128), F32)
        dk = jnp.zeros((keys, 128), F32)
        dv = jnp.zeros((keys, 128), F32)
        for half in halves:
            qh, kh, gh = q * half, k * half, g * half
            scores = dot_nt(qh, k) * SCORE_SCALE
            if causal:
                allowed = lax.broadcasted_iota(jnp.int32, (rows, keys), 0) >= lax.broadcasted_iota(
                    jnp.int32, (rows, keys), 1
                )
                scores = jnp.where(allowed, scores, NEG_FILL)
            exponents = jnp.exp(scores - jnp.max(scores, axis=-1, keepdims=True))
            probs = exponents / jnp.sum(exponents, axis=-1, keepdims=True)
            grad_probs = dot_nt(gh, v)
            dv = dv + dot_tn(probs.astype(BF), gh)
            inner = jnp.sum(probs * grad_probs, axis=-1, keepdims=True)
            grad_scores = (probs * (grad_probs - inner)).astype(BF)
            dq = dq + dot_nn(grad_scores, kh)
            dk = dk + dot_tn(grad_scores, qh)
        query_out[at_q, lanes] = (dq * SCORE_SCALE).astype(BF)
        key_out[at_k, lanes] = (dk * SCORE_SCALE).astype(BF)
        value_out[at_k, lanes] = dv.astype(BF)
        return carry

    first, count = share[0] * clips * pairs // share[1], clips * pairs // share[1]
    lax.fori_loop(first, first + count, pair, 0)


class BackwardRefs(NamedTuple):
    grad_logits: Any
    pair_rows: Any
    pick: Any
    x0: Any
    x1: Any
    x2: Any
    x3: Any
    h1: Any
    h2: Any
    h3: Any
    q1: Any
    k1: Any
    v1: Any
    o1: Any
    q2: Any
    k2: Any
    v2: Any
    o2: Any
    upper: Any
    act: Any
    text: Any
    gains: Any
    head: Any
    w0: Any
    w1: Any
    w2: Any
    w3: Any
    w4: Any
    w5: Any
    w6: Any
    ids_all: Any
    loss: Any
    in_out: Any
    out_out: Any
    ffn_out: Any
    head_out: Any
    embed_out: Any
    norm_out: Any
    total_out: Any
    core_in: Any
    diagonal_in: Any
    side_in: Any
    line_in: Any
    head_line: Any
    head_send: Any
    head_y: Any
    head_held: Any
    core_slot: Any
    send_slot: Any
    held: Any
    acts: Any
    ups: Any
    logit: Any
    upper_slot: Any
    qkv: Any
    query2: Any
    kv2: Any
    left: Any
    left_pair: Any
    left_text: Any
    weight: Any
    lows: Any
    query2_grad: Any
    kv2_grad: Any
    grad_x: Any
    grad_h: Any
    values: Any
    rows_in: Any
    pair_in: Any
    pick_in: Any
    gain_in: Any
    pair_send: Any
    pair_land: Any
    head_total: Any
    norm_grads: Any
    starts: Any
    starts_in: Any
    norms_in: Any
    spread: Any
    squares: Any
    totals: Any
    totals_in: Any
    send_sem: Any
    recv_sem: Any
    weight_sem: Any
    load_sem: Any
    core_sem: Any
    upper_sem: Any
    pair_sem: Any
    far_send: Any
    far_recv: Any


def backward_kernel(clips, *refs):
    r = BackwardRefs(*refs)
    z, y, c, x = place()
    me = lax.axis_index("dp") * 2 + x
    line, z_dev, y_dev, x_dev, c_dev = partners()
    items = PLAN
    count = len(items)
    frames_all = r.x0.shape[0]
    pieces = 4

    load_count = [0]

    def load(src, dst):
        piece = pltpu.make_async_copy(src, dst, r.load_sem.at[load_count[0]])
        load_count[0] += 1
        piece.start()
        return piece

    load_logit = load(r.grad_logits, r.logit)
    load_pair = load(r.pair_rows, r.pair_in)
    load_pick = load(r.pick, r.pick_in)
    load_gains = load(r.gains, r.gain_in)
    load_x3 = load(r.x3, r.values)
    load_act = load(r.act, r.acts)
    load_h3 = load(r.h3, r.rows_in.at[0])
    load_q1 = load(r.q1, r.qkv.at[0])
    load_k1 = load(r.k1, r.qkv.at[1])
    load_v1 = load(r.v1, r.qkv.at[2])
    load_q2 = load(r.q2, r.query2)
    load_k2 = load(r.k2, r.kv2.at[0])
    load_v2 = load(r.v2, r.kv2.at[1])

    sequence = [(r.head, k) for k in range(pieces)]
    sequence += [(ref, j) for j in range(pieces) for ref in (r.w6, r.w5)]
    sequence += [(r.w4, 0), (r.w2, 0), (r.w1, 0)] + [(r.w0, k) for k in range(3)]
    slots = r.weight.shape[0]
    taken = [0]

    def weight_copy(index):
        ref, at = sequence[index]
        slot = r.weight.at[index % slots]
        if ref is r.head:
            slot = slot.at[:, 0 : ref.shape[2]]
        return pltpu.make_async_copy(ref.at[at], slot, r.weight_sem.at[index % slots])

    for index in range(slots - 1):
        weight_copy(index).start()

    def next_weight():
        index = taken[0]
        taken[0] += 1
        if index + slots - 1 < len(sequence):
            weight_copy(index + slots - 1).start()
        weight_copy(index).wait()
        return r.weight.at[index % slots]

    def upper_copy(j):
        return pltpu.make_async_copy(
            r.upper.at[j], r.upper_slot.at[j % 2], r.upper_sem.at[j % 2]
        )

    upper_copy(0).start()
    upper_copy(1).start()
    greet_all(me)

    left = (
        r.left_pair, r.left.at[0], r.left.at[1], r.left.at[2],
        r.left.at[3], r.left_text, r.left.at[0], r.left.at[2],
    )
    right = [r.logit.at[k] for k in range(pieces)]
    right += [r.acts.at[j] for j in range(pieces)] + [r.ups.at[j] for j in range(pieces)]
    right += [r.lows.at[1], r.query2_grad, r.kv2_grad.at[0], r.kv2_grad.at[1]]
    right += [r.acts.at[3], r.acts.at[0], r.acts.at[1], r.acts.at[2]]

    def copy(src, dst, item, slot, target):
        return pltpu.make_async_remote_copy(
            src_ref=src,
            dst_ref=dst,
            send_sem=r.send_sem.at[item, slot],
            recv_sem=r.recv_sem.at[item, slot],
            device_id=target,
            device_id_type=MESH,
        )

    held_slots = r.held.shape[0]

    def head_cols(index):
        return pl.ds(pl.multiple_of(index * part_size, part_size), part_size)

    part_size = r.head_out.shape[3] // 2
    half_cols = (pl.ds(0, part_size), pl.ds(part_size, part_size))

    def used(ref, item):
        return ref.at[:, :, :, :, half_cols[0]] if items[item][0] == "h" else ref

    def to_core(item):
        slot = r.send_slot.at[item % 2]
        return copy(used(slot, item), used(r.core_in.at[item], item), item, 0, c_dev)

    def core_load(item):
        slot = r.core_slot.at[item % 2]
        return pltpu.make_async_copy(
            used(r.core_in.at[item], item), used(slot, item), r.core_sem.at[item % 2]
        )

    def held_of(item):
        kind, unit = items[item][:2]
        return r.head_held.at[unit] if kind == "h" else r.held.at[item % held_slots]

    def first(item):
        kind, unit = items[item][:2]
        held = held_of(item)
        if kind == "h":
            return [
                copy(
                    held.at[other],
                    r.head_line.at[unit, slot],
                    item,
                    1 + slot,
                    z_dev[slot],
                )
                for slot, other in enumerate(line)
            ]
        diagonal = held.at[:, 1 - y, 1 - x]
        return [
            copy(diagonal.at[:, :, half_cols[n]], r.diagonal_in.at[unit, n], item, 1 + n, target)
            for n, target in enumerate((x_dev, y_dev))
        ]

    def second(item):
        kind, unit = items[item][:2]
        if kind == "h":
            return [copy(r.head_send.at[unit], r.head_y.at[unit], item, 4, y_dev)]
        held = held_of(item)
        return [
            copy(held.at[:, 1 - y, x], r.side_in.at[unit, 0], item, 3, y_dev),
            copy(held.at[:, y, 1 - x], r.side_in.at[unit, 1], item, 4, x_dev),
        ]

    def third(item):
        kind, unit = items[item][:2]
        if kind == "h":
            return []
        return [
            copy(
                r.side_in.at[unit, 0, other], r.line_in.at[unit, slot], item, 5 + slot, z_dev[slot]
            )
            for slot, other in enumerate(line)
        ]

    def left_rows(name, core):
        ref = left[name]
        return jnp.concatenate(
            [ref[pl.ds(pl.multiple_of(k * 128 + core * 64, 64), 64), :] for k in range(8)], axis=0
        )

    def wide(value):
        return value.astype(F32)

    def column_parts(item):
        return 2 if items[item][0] == "h" else 4

    def make(item):
        kind, unit, left_name, right_name = items[item]
        if item >= 2:
            to_core(item - 2).wait_send()
        slot = r.send_slot.at[item % 2]

        def columns(n, carry):
            cols = chunk(n, 256)
            value = dot_nn(left_rows(left_name, 1 - c), right[right_name][:, cols]).astype(BF)
            slot[:, :, :, :, cols] = value.reshape(4, 2, 2, 32, 256)
            return carry

        lax.fori_loop(0, column_parts(item), columns, 0)
        to_core(item).start()

    def join_core(item):
        kind, unit, left_name, right_name = items[item]
        core_load(item).wait()
        if item >= held_slots and items[item - held_slots][0] == "a":
            for part in first(item - held_slots) + second(item - held_slots):
                part.wait_send()
        held, landed = held_of(item), r.core_slot.at[item % 2]

        def columns(n, carry):
            cols = chunk(n, 256)
            value = dot_nn(left_rows(left_name, c), right[right_name][:, cols])
            value = value.reshape(4, 2, 2, 32, 256) + wide(landed[:, :, :, :, cols])
            held[:, :, :, :, cols] = value.astype(BF)
            return carry

        lax.fori_loop(0, column_parts(item), columns, 0)
        for part in first(item):
            part.start()

    def join_first(item):
        kind, unit = items[item][:2]
        held = held_of(item)
        for part in first(item):
            part.wait_recv()
        if kind == "h":
            for side in range(2):
                total = wide(held[z, side])
                for slot in range(3):
                    total = total + wide(r.head_line[unit, slot, side])
                r.head_total[side] = total
            own = r.head_total[y]
            r.head_out[unit, :, :, head_cols(y)] = own
            squared = own * own
            r.squares[:, half_cols[0]] += squared[0] + squared[1]
            r.head_send[unit] = r.head_total[1 - y].astype(BF)
        else:

            def planes(k, carry):
                held[k, 1 - y, x, :, half_cols[0]] = (
                    wide(held[k, 1 - y, x, :, half_cols[0]]) + wide(r.diagonal_in[unit, 0, k])
                ).astype(BF)
                held[k, y, 1 - x, :, half_cols[1]] = (
                    wide(held[k, y, 1 - x, :, half_cols[1]]) + wide(r.diagonal_in[unit, 1, k])
                ).astype(BF)
                return carry

            lax.fori_loop(0, 4, planes, 0)
        for part in second(item):
            part.start()

    def join_second(item):
        kind, unit = items[item][:2]
        for part in second(item):
            part.wait_recv()
        if kind == "h":
            other = wide(r.head_y[unit])
            r.head_out[unit, :, :, head_cols(1 - y)] = other
            squared = other * other
            r.squares[:, half_cols[0]] += squared[0] + squared[1]
            return
        held = held_of(item)

        def planes(k, carry):
            total = wide(held[k, y, x]) + wide(r.side_in[unit, 0, k]) + wide(r.side_in[unit, 1, k])
            r.side_in[unit, 0, k] = total.astype(BF)
            return carry

        lax.fori_loop(0, 4, planes, 0)
        for part in third(item):
            part.start()

    def finish(item):
        kind, unit = items[item][:2]
        if kind == "h":
            return
        for part in third(item):
            part.wait_recv()
        total = wide(r.side_in[unit, 0, z])
        for slot in range(3):
            total = total + wide(r.line_in[unit, slot])
        r.squares[...] += total * total
        group, index = UNITS[unit]
        if group in (1, 4):
            r.out_out[group // 4] = total
        elif group < 5:
            r.in_out[(0, 0, 3, 4)[group] + index] = total
        else:
            r.ffn_out[group - 5, :, index * total.shape[1] : (index + 1) * total.shape[1]] = total

    ticks = [0]

    def pump():
        tick = ticks[0]
        ticks[0] += 1
        item = tick - 1
        if 0 <= item < count:
            to_core(item).wait_recv()
            core_load(item).start()
        for stage_number, stage in enumerate((join_core, join_first, join_second, finish)):
            for kind, late in (("h", HEAD_LATE), ("a", LATE)):
                item = tick - late[stage_number]
                if 0 <= item < count and items[item][0] == kind:
                    stage(item)

    def unit(right_name):
        item = ticks[0]
        assert items[item][3] == right_name
        make(item)
        pump()

    r.squares[...] = jnp.zeros_like(r.squares)
    load_logit.wait()
    load_pair.wait()
    r.left_pair[...] = r.pair_in[...].T
    unit(LOGIT + 0)
    unit(LOGIT + 1)

    def pair_rows_of(k, w):
        def columns(n, carry):
            cols = chunk(n, 256)
            value = dot_nt(r.logit[k], w[cols, 0:part_size])
            r.grad_h[:, cols] = value if k == 0 else r.grad_h[:, cols] + value
            return carry

        lax.fori_loop(0, 4, columns, 0)

    for k in range(pieces):
        pair_rows_of(k, next_weight())
    half = r.pair_send.shape[1]
    mine = y * 2 + x
    square = (y * 2 + 1 - x, (1 - y) * 2 + x, (1 - y) * 2 + 1 - x)
    trade = []
    for slot, (member, target) in enumerate(
        zip(square, (x_dev, y_dev, device(z, 1 - y, c, 1 - x)), strict=True)
    ):
        r.pair_send[slot] = r.grad_h[chunk(member, half), :].astype(BF)
        trade.append(
            pltpu.make_async_remote_copy(
                src_ref=r.pair_send.at[slot],
                dst_ref=r.pair_land.at[slot],
                send_sem=r.pair_sem.at[slot],
                recv_sem=r.pair_sem.at[3 + slot],
                device_id=target,
                device_id_type=MESH,
            )
        )
    for piece in trade:
        piece.start()
    unit(LOGIT + 2)
    load_h3.wait()
    r.left[1] = r.rows_in[0].T
    load_pick.wait()
    load_gains.wait()
    load_x3.wait()
    load_act.wait()
    for piece in trade:
        piece.wait()
    chosen = r.grad_h[chunk(mine, half), :]
    for slot in range(3):
        chosen = chosen + wide(r.pair_land[slot])
    chosen_top = chosen.astype(BF)
    chosen_rest = (chosen - wide(chosen_top)).astype(BF)
    r.grad_h[...] = dot_nn(r.pick_in[...], chosen_top) + dot_nn(r.pick_in[...], chosen_rest)

    def norm_back(index, add, low_ref):
        norm_back_rows(
            r.values,
            r.gain_in.at[index : index + 1],
            r.grad_h,
            add,
            r.grad_x,
            low_ref,
            r.norm_grads.at[index : index + 1],
            r.norm_grads.at[4 + index : 5 + index],
        )

    norm_back(3, None, r.lows.at[0])
    unit(LOGIT + 3)
    load_x2 = load(r.x2, r.values)
    r.left[0] = r.lows[0].T
    load_o2 = load(r.o2, r.rows_in.at[1])
    load_h2 = load(r.h2, r.rows_in.at[0])

    def down_back(j):
        w = next_weight()
        upper_copy(j).wait()

        def columns(n, carry):
            cols = chunk(n, 256)
            grad = dot_nn(r.lows[0], w[:, cols])
            upper = r.upper_slot[j % 2, :, cols]
            slope = 0.5 * (1.0 + lax.erf(upper * math.sqrt(0.5))) + upper * jnp.exp(
                -0.5 * upper * upper
            ) * (1.0 / math.sqrt(2.0 * math.pi))
            r.ups[j, :, cols] = (grad * slope).astype(BF)
            return carry

        lax.fori_loop(0, 4, columns, 0)
        if j + 2 < pieces:
            upper_copy(j + 2).start()

    def into_grad_h(value_ref, w, fresh):
        def columns(n, carry):
            cols = chunk(n, 256)
            value = dot_nt(value_ref[...], w[cols, :])
            r.grad_h[:, cols] = value if fresh else r.grad_h[:, cols] + value
            return carry

        lax.fori_loop(0, 4, columns, 0)

    def up_back(j):
        into_grad_h(r.ups.at[j], next_weight(), j == 0)

    unit(ACT + 0)
    down_back(0)
    unit(ACT + 1)
    up_back(0)
    down_back(1)
    unit(ACT + 2)
    up_back(1)
    down_back(2)
    up_back(2)
    down_back(3)
    unit(ACT + 3)
    up_back(3)
    load_x2.wait()
    norm_back(2, r.grad_x, r.lows.at[1])
    load_x1 = load(r.x1, r.values)

    load_o2.wait()
    r.left[2] = r.rows_in[1].T
    load_o1 = load(r.o1, r.rows_in.at[1])
    unit(UP + 0)
    for piece in (load_q2, load_k2, load_v2):
        piece.wait()

    def into_mixed(low_ref):
        w = next_weight()

        def columns(n, carry):
            cols = chunk(n, 256)
            r.lows[0, :, cols] = dot_nt(low_ref[...], w[cols, :]).astype(BF)
            return carry

        lax.fori_loop(0, 4, columns, 0)

    def cross_back(share):
        attend_back_rows(
            r.query2, r.kv2.at[0], r.kv2.at[1], r.lows.at[0],
            r.query2_grad, r.kv2_grad.at[0], r.kv2_grad.at[1], clips, False, share,
        )

    into_mixed(r.lows.at[1])
    cross_back((0, 2))
    unit(RES2)
    cross_back((1, 2))
    load_h2.wait()
    r.left[3] = r.rows_in[0].T
    load_text = load(r.text, r.pair_in.at[0 : r.text.shape[0]])
    load_h1 = load(r.h1, r.rows_in.at[0])
    unit(QUERY2)
    load_text.wait()
    r.left_text[...] = r.pair_in[0 : r.text.shape[0]].T
    into_grad_h(r.query2_grad, next_weight(), True)
    load_x1.wait()
    norm_back(1, r.grad_x, r.acts.at[3])
    load_x0 = load(r.x0, r.values)
    load_o1.wait()
    r.left[0] = r.rows_in[1].T
    unit(KEY2)

    def self_back(share):
        attend_back_rows(
            r.qkv.at[0], r.qkv.at[1], r.qkv.at[2], r.lows.at[0],
            r.acts.at[0], r.acts.at[1], r.acts.at[2], clips, True, share,
        )

    for piece in (load_q1, load_k1, load_v1):
        piece.wait()
    into_mixed(r.acts.at[3])
    self_back((0, 4))
    unit(VALUE2)
    self_back((1, 4))
    self_back((2, 4))
    unit(RES1)
    self_back((3, 4))
    unit(UP + 1)
    load_h1.wait()
    r.left[2] = r.rows_in[0].T
    into_grad_h(r.acts.at[0], next_weight(), True)
    unit(QUERY1)
    into_grad_h(r.acts.at[1], next_weight(), False)
    into_grad_h(r.acts.at[2], next_weight(), False)
    unit(KEY1)
    load_x0.wait()
    norm_back(0, r.grad_x, r.lows.at[1])
    columns, lanes = r.starts.shape[1], r.spread.shape[2]
    books, rows = r.embed_out.shape[0], r.starts.shape[2]
    table_rows = r.embed_out.shape[2]
    high_count = r.spread.shape[1] // columns
    for group in range(r.starts.shape[0] // 4):
        turned = r.lows[1, :, group * 128 : (group + 1) * 128].T
        r.starts[4 * group : 4 * group + 4] = turned.reshape(4, columns, rows)

    def far(src, dst, step, slot):
        return pltpu.make_async_remote_copy(
            src_ref=src,
            dst_ref=dst,
            send_sem=r.far_send.at[slot, step],
            recv_sem=r.far_recv.at[slot, step],
            device_id=device_of(lax.rem(me + step, DEVICES)),
            device_id_type=MESH,
        )

    def start_copy(step):
        return far(r.starts.at[lax.rem(me + step, DEVICES)], r.starts_in.at[me], step, 0)

    def norm_copy(step):
        group = lax.div(lax.rem(me + step, DEVICES), 4)
        return far(r.norm_grads.at[:, chunk(group, 128)], r.norms_in.at[me], step, 1)

    def total_copy(step):
        return far(r.totals, r.totals_in.at[me], step, 2)

    def each(action):
        def body(step, carry):
            action(step)
            return carry

        lax.fori_loop(1, DEVICES, body, 0)

    def send_far(step):
        start_copy(step).start()
        norm_copy(step).start()

    each(send_far)
    r.starts_in[me] = r.starts[me]
    r.norms_in[me] = r.norm_grads[:, chunk(lax.div(me, 4), 128)]
    r.spread[...] = jnp.zeros_like(r.spread)
    spread_code = lax.broadcasted_iota(jnp.int32, (lanes, rows), 0)

    def spread_block(step, carry):
        source = lax.rem(me - step + DEVICES, DEVICES)
        dp, member = lax.div(source, 2), lax.rem(source, 2)
        at = (lax.div(dp, 4), lax.rem(lax.div(dp, 2), 2), lax.rem(dp, 2))
        values = wide(r.starts_in[source])
        for book in range(books):
            ids = jnp.concatenate(
                [r.ids_all[(*at, clips * member + m, pl.ds(book, 1))] for m in range(clips)], axis=1
            )
            low_ids, high_ids = ids & (lanes - 1), lax.shift_right_logical(ids, 8)
            hot = jnp.where(spread_code == low_ids, 1.0, 0.0).astype(BF)
            parted = jnp.concatenate(
                [jnp.where(high_ids == high, values, 0.0) for high in range(high_count)], axis=0
            ).astype(BF)
            r.spread[book] += dot_nt(parted, hot)
        return carry

    def wait_and_spread(step, carry):
        start_copy(step).wait_recv()
        return spread_block(step, carry)

    unit(VALUE1)
    spread_block(0, 0)
    unit(UP + 2)
    lax.fori_loop(1, 9, wait_and_spread, 0)
    unit(UP + 3)
    for share in range(1, 4):
        lax.fori_loop(1 + 8 * share, min(9 + 8 * share, DEVICES), wait_and_spread, 0)
        pump()
    embed_squares = jnp.zeros((columns, lanes), F32)
    for book in range(books):
        for high in range(high_count):
            left_col = high * lanes
            width = min(table_rows, left_col + lanes) - left_col
            block = r.spread[book, high * columns : (high + 1) * columns, :]
            r.embed_out[book, :, left_col : left_col + width] = block[:, :width]
            embed_squares = embed_squares + block * block
    each(lambda step: norm_copy(step).wait_recv())
    norm_total = r.norms_in[0]
    for other in range(1, DEVICES):
        norm_total = norm_total + r.norms_in[other]
    r.norm_out[...] = norm_total
    lane = lax.broadcasted_iota(jnp.int32, norm_total.shape, 1)
    norm_squares = jnp.where(lax.div(lane, columns) == lax.rem(me, 4), norm_total * norm_total, 0.0)
    while ticks[0] < count + max(LATE[-1], HEAD_LATE[-1]):
        pump()

    sum_tile = norm_squares
    for k in range(4):
        for n in range(8):
            sum_tile = sum_tile + r.squares[8 * k : 8 * k + 8, 128 * n : 128 * n + 128]
        for n in range(lanes // 128):
            sum_tile = sum_tile + embed_squares[8 * k : 8 * k + 8, 128 * n : 128 * n + 128]
    r.totals[0] = sum_tile
    r.totals[1] = r.loss[...]
    each(lambda step: total_copy(step).start())
    r.totals_in[me] = r.totals[...]
    each(lambda step: total_copy(step).wait_recv())
    total = r.totals_in[0]
    for other in range(1, DEVICES):
        total = total + r.totals_in[other]
    r.total_out[...] = total

    def far_done(step):
        start_copy(step).wait_send()
        norm_copy(step).wait_send()
        total_copy(step).wait_send()

    each(far_done)
    for item in range(count):
        if item >= count - 2:
            to_core(item).wait_send()
        parts = third(item)
        if items[item][0] == "h" or item >= count - held_slots:
            parts = parts + first(item) + second(item)
        for part in parts:
            part.wait_send()


def backward_fast(clips, table_rows, operands):
    named = BackwardRefs(*operands, *(None,) * (len(BackwardRefs._fields) - len(operands)))
    rows, width = named.x0.shape
    pair_count = named.pair_rows.shape[0]
    text_rows = named.text.shape[0]
    books, codes = named.head.shape[0], named.head.shape[2]
    units, count = len(UNITS), len(PLAN)
    block = (32, width)
    columns, lanes = width // DEVICES, 256
    high_count = -(-table_rows // lanes)
    vmem, dma = pltpu.VMEM, pltpu.SemaphoreType.DMA
    any_spec, vmem_spec = pl.BlockSpec(memory_space=pl.ANY), pl.BlockSpec(memory_space=vmem)
    held_slots = LATE[2] - LATE[0] + 1
    results = pl.pallas_call(
        functools.partial(backward_kernel, clips),
        out_shape=(
            jax.ShapeDtypeStruct((6,) + block, F32),
            jax.ShapeDtypeStruct((2,) + block, F32),
            jax.ShapeDtypeStruct((2, 32, 4 * width), F32),
            jax.ShapeDtypeStruct((books, 2) + block, F32),
            jax.ShapeDtypeStruct((books, columns, table_rows), F32),
            jax.ShapeDtypeStruct((8, 128), F32),
            jax.ShapeDtypeStruct((2, 8, 128), F32),
            jax.ShapeDtypeStruct((count, 4, 2, 2) + block, BF),
        ),
        in_specs=[any_spec] * (len(operands) - 2) + [vmem_spec] * 2,
        out_specs=(vmem_spec,) * 7 + (any_spec,),
        scratch_shapes=[
            vmem((units, 2, 4, 32, width // 2), BF),
            vmem((units, 2, 4) + block, BF),
            vmem((units, 3) + block, BF),
            vmem((books, 3, 2, 2, 32, codes), BF),
            vmem((books, 2, 32, codes), BF),
            vmem((books, 2, 32, codes), BF),
            vmem((books, 4, 2, 2, 32, codes), BF),
            vmem((2, 4, 2, 2) + block, BF),
            vmem((2, 4, 2, 2) + block, BF),
            vmem((held_slots, 4, 2, 2) + block, BF),
            vmem((4, rows, width), BF),
            vmem((4, rows, width), BF),
            vmem((books, pair_count, codes), BF),
            vmem((2, rows, width), F32),
            vmem((3, rows, width), BF),
            vmem((rows, width), BF),
            vmem((2, text_rows, width), BF),
            vmem((4, width, rows), BF),
            vmem((width, pair_count), BF),
            vmem((width, text_rows), BF),
            vmem((2, width, width), BF),
            vmem((2, rows, width), BF),
            vmem((rows, width), BF),
            vmem((2, text_rows, width), BF),
            vmem((rows, width), F32),
            vmem((rows, width), F32),
            vmem((rows, width), F32),
            vmem((2, rows, width), BF),
            vmem((pair_count, width), BF),
            vmem(named.pick.shape, BF),
            vmem(named.gains.shape, F32),
            vmem((3, pair_count // 4, width), BF),
            vmem((3, pair_count // 4, width), BF),
            vmem((2, 2, 32, codes), F32),
            vmem((8, width), F32),
            vmem((DEVICES, columns, rows), BF),
            vmem((DEVICES, columns, rows), BF),
            vmem((DEVICES, 8, 128), F32),
            vmem((books, high_count * columns, lanes), F32),
            vmem(block, F32),
            vmem((2, 8, 128), F32),
            vmem((DEVICES, 2, 8, 128), F32),
            dma((count, 8)),
            dma((count, 8)),
            dma((2,)),
            dma((24,)),
            dma((2,)),
            dma((2,)),
            dma((6,)),
            dma((3, DEVICES)),
            dma((3, DEVICES)),
        ],
        compiler_params=pltpu.CompilerParams(
            collective_id=2, has_side_effects=True, vmem_limit_bytes=60 * 2**20
        ),
    )(*operands)
    return BackwardRefs(
        *operands,
        *results,
        *(None,) * (len(BackwardRefs._fields) - len(operands) - len(results)),
    )


class ForwardRefs(NamedTuple):
    ids: Any
    norms: Any
    table: Any
    layer: Any
    head_own: Any
    angles: Any
    text: Any
    pick: Any
    teach: Any
    row_info: Any
    ids_all: Any
    gains: Any
    loss: Any
    head: Any
    w0: Any
    w1: Any
    w2: Any
    w3: Any
    w4: Any
    w5: Any
    w6: Any
    grad_logits: Any
    pair_rows: Any
    x0: Any
    x1: Any
    x2: Any
    x3: Any
    h1: Any
    h2: Any
    h3: Any
    q1: Any
    k1: Any
    v1: Any
    o1: Any
    q2: Any
    k2: Any
    v2: Any
    o2: Any
    upper: Any
    act: Any
    norms_all: Any
    teach_all: Any
    rows_all: Any
    norm_rows: Any
    stacked: Any
    looked: Any
    landed: Any
    xs: Any
    hs: Any
    qkv: Any
    mixed: Any
    query2: Any
    kv2: Any
    uppers: Any
    acts: Any
    final: Any
    pair: Any
    wanted: Any
    logits: Any
    logit_grads: Any
    stats: Any
    weight: Any
    head_weight: Any
    send_sem: Any
    recv_sem: Any
    local_sem: Any
    small_send: Any
    small_recv: Any
    look_send: Any
    look_recv: Any
    weight_sem: Any
    store_sem: Any
    pair_send: Any
    pair_recv: Any


GATHER_LATE = (3, 5, 7, 8)
HOP_LATE = 1


def norm_rows_low(values_ref, gain_ref, bias_ref, low_ref):
    size = 32
    one_gain, bias = 1.0 + gain_ref[...], bias_ref[...]

    def block(index, carry):
        rows = chunk(index, size)
        values = values_ref[rows, :]
        average = jnp.mean(values, axis=-1, keepdims=True)
        centred = values - average
        spread = jnp.mean(centred * centred, axis=-1, keepdims=True)
        low_ref[rows, :] = (centred * lax.rsqrt(spread + NORM_EPS) * one_gain + bias).astype(BF)
        return carry

    lax.fori_loop(0, values_ref.shape[0] // size, block, 0)


def attend_rows(query, key, value, out, clips, causal):
    rows, keys = query.shape[0] // clips, key.shape[0] // clips
    pairs = query.shape[1] // 128
    lane = lax.broadcasted_iota(jnp.int32, (1, 128), 1)
    halves = [(lane < 64).astype(F32).astype(BF), (lane >= 64).astype(F32).astype(BF)]

    def pair(index, carry):
        at_q = chunk(lax.div(index, pairs), rows)
        at_k = chunk(lax.div(index, pairs), keys)
        lanes = chunk(lax.rem(index, pairs), 128)
        q, k, v = query[at_q, lanes], key[at_k, lanes], value[at_k, lanes]
        total = jnp.zeros((rows, 128), F32)
        for half in halves:
            scores = dot_nt(q * half, k) * SCORE_SCALE
            if causal:
                allowed = lax.broadcasted_iota(jnp.int32, (rows, keys), 0) >= lax.broadcasted_iota(
                    jnp.int32, (rows, keys), 1
                )
                scores = jnp.where(allowed, scores, NEG_FILL)
            exponents = jnp.exp(scores - jnp.max(scores, axis=-1, keepdims=True))
            probs = exponents / jnp.sum(exponents, axis=-1, keepdims=True)
            total = total + dot_nn(probs.astype(BF), v * half)
        out[at_q, lanes] = total.astype(BF)
        return carry

    lax.fori_loop(0, clips * pairs, pair, 0)


def forward_kernel(clips, denominator, special, *refs):
    r = ForwardRefs(*refs)
    z, y, c, x = place()
    me = lax.axis_index("dp") * 2 + x
    line, z_dev, y_dev, x_dev, c_dev = partners()
    books, frames = r.ids.shape[1], r.ids.shape[2]
    rows = clips * frames
    order = transfer_order(books)
    count = len(order)
    outs = (r.w0, r.w1, r.w2, r.w3, r.w4, r.w5, r.w6)
    columns, lanes = r.looked.shape[1], r.stacked.shape[2]
    high_count = r.stacked.shape[1] // columns
    devices = DEVICES

    greet_all(me)

    def copy(src, dst, item, slot, target):
        return pltpu.make_async_remote_copy(
            src_ref=src,
            dst_ref=dst,
            send_sem=r.send_sem.at[item, slot],
            recv_sem=r.recv_sem.at[item, slot],
            device_id=target,
            device_id_type=MESH,
        )

    def whole(unit):
        group, index = UNITS[unit]
        return outs[group].at[index]

    own = [
        pltpu.make_async_copy(r.layer.at[unit], whole(unit).at[z, y, c, x], r.local_sem.at[unit])
        for unit in range(len(UNITS))
    ]
    part_size = r.head_own.shape[2] // 2

    def part_cols(index):
        return pl.ds(pl.multiple_of(index * part_size, part_size), part_size)

    own.append(
        pltpu.make_async_copy(
            r.head_own.at[:, :, part_cols(y)], r.head.at[:, z, y, c], r.local_sem.at[len(UNITS)]
        )
    )
    half_cols = (pl.ds(0, r.layer.shape[2] // 2), pl.ds(r.layer.shape[2] // 2, r.layer.shape[2] // 2))

    def first(item):
        kind, unit = order[item]
        if kind == "h":
            src = r.head_own.at[unit, :, part_cols(1 - y)]
            return [copy(src, r.head.at[unit, z, y, c], item, 0, y_dev)]
        return []

    def hop(item, number, side):
        unit = order[item][1]
        step = 1 if side == 0 else -1
        target = device(lax.rem(z + step + 4, 4), y, c, x)
        block = whole(unit).at[lax.rem(z - step * (number - 1) + 4, 4), y, c, x]
        source = r.layer.at[unit] if number == 1 else block
        part = copy(source, block, item, (0, 1, 2, 11, 12, 13)[3 * side + number - 1], target)
        if side == 0:
            return part, (z < 3) & (z - number + 1 >= 0), z - number >= 0
        return part, (z > 0) & (z + number - 1 <= 3), z + number <= 3

    def hop_start(item, number):
        for side in range(2):
            part, sends, lands = hop(item, number, side)
            pl.when(sends)(part.start)

    def hop_wait(item, number):
        for side in range(2):
            part, sends, lands = hop(item, number, side)
            pl.when(lands)(part.wait_recv)

    def hop_done(item):
        for number in range(1, 4):
            for side in range(2):
                part, sends, lands = hop(item, number, side)
                pl.when(sends)(part.wait_send)

    def second(item):
        kind, unit = order[item]
        if kind == "h":
            block = r.head.at[unit, z, :, c]
            return [copy(block, block, item, 1 + slot, target) for slot, target in enumerate(z_dev)]
        block = whole(unit).at[:, y, c, x]
        return [
            copy(block, block, item, 3 + slot, target)
            for slot, target in enumerate((y_dev, x_dev, c_dev))
        ]

    def third(item):
        kind, unit = order[item]
        if kind == "h":
            block = r.head.at[unit, :, :, c]
            return [copy(block, block, item, 4, c_dev)]
        from_y, from_x = whole(unit).at[:, 1 - y, c, x], whole(unit).at[:, y, c, 1 - x]
        half_y, half_x = from_y.at[:, :, half_cols[0]], from_x.at[:, :, half_cols[1]]
        return [
            copy(half_y, half_y, item, 6, x_dev),
            copy(half_x, half_x, item, 7, y_dev),
            copy(from_y, from_y, item, 8, c_dev),
            copy(from_x, from_x, item, 9, c_dev),
        ]

    def fourth(item):
        kind, unit = order[item]
        if kind == "h":
            return []
        block = whole(unit).at[:, 1 - y, c, 1 - x]
        return [copy(block, block, item, 10, c_dev)]

    ticks = [0]

    def pump():
        tick = ticks[0]
        ticks[0] += 1
        if tick < count:
            for part in first(tick):
                part.start()
            if order[tick][0] == "a":
                hop_start(tick, 1)
        for number in (1, 2):
            item = tick - HOP_LATE * number
            if 0 <= item < count and order[item][0] == "a":
                hop_wait(item, number)
                hop_start(item, number + 1)
        item = tick - GATHER_LATE[0]
        if 0 <= item < count:
            for part in first(item):
                part.wait_recv()
            if order[item][0] == "a":
                hop_wait(item, 3)
            for part in second(item):
                part.start()
        item = tick - GATHER_LATE[1]
        if 0 <= item < count:
            for part in second(item) if order[item][0] == "h" else second(item)[:2]:
                part.wait_recv()
            for part in third(item):
                part.start()
        item = tick - GATHER_LATE[2]
        if 0 <= item < count and order[item][0] != "h":
            for part in third(item)[:2]:
                part.wait_recv()
            for part in fourth(item):
                part.start()
        item = tick - GATHER_LATE[3]
        if 0 <= item < count:
            late = third(item) if order[item][0] == "h" else second(item)[2:] + third(item)[2:]
            for part in late + fourth(item):
                part.wait_recv()
        advance_loads()

    item_of = {entry: item for item, entry in enumerate(order)}

    def ticks_for(kind, unit):
        return item_of[kind, unit] + GATHER_LATE[3] + 1

    taken, loading, heads_loading = [0], [0], [0]
    weight_slots = r.weight.shape[0]

    def weight_copy(unit):
        slot = unit % weight_slots
        return pltpu.make_async_copy(
            whole(unit), r.weight.at[slot].reshape(whole(unit).shape), r.weight_sem.at[slot]
        )

    def head_copy(book):
        return pltpu.make_async_copy(
            r.head.at[book], r.head_weight.at[book], r.weight_sem.at[weight_slots + book]
        )

    def advance_loads():
        while (
            loading[0] < min(len(UNITS), taken[0] + weight_slots)
            and ticks_for("a", loading[0]) <= ticks[0]
        ):
            weight_copy(loading[0]).start()
            loading[0] += 1
        while heads_loading[0] < books and ticks_for("h", heads_loading[0]) <= ticks[0]:
            head_copy(heads_loading[0]).start()
            heads_loading[0] += 1

    def next_weight():
        unit = taken[0]
        while loading[0] <= unit:
            pump()
        weight_copy(unit).wait()
        taken[0] += 1
        return r.weight.at[unit % weight_slots]

    stores = []

    def store(src, dst):
        piece = pltpu.make_async_copy(src, dst, r.store_sem.at[len(stores)])
        piece.start()
        stores.append(piece)

    def small(block, slot, target):
        return pltpu.make_async_remote_copy(
            src_ref=block,
            dst_ref=block,
            send_sem=r.small_send.at[slot],
            recv_sem=r.small_recv.at[slot],
            device_id=target,
            device_id_type=MESH,
        )

    for piece in own:
        piece.start()
    r.teach_all[y] = r.teach[...]
    r.rows_all[y] = r.row_info[...]
    small_y = [small(r.teach_all.at[y], 11, y_dev), small(r.rows_all.at[y], 12, y_dev)]
    for part in small_y:
        part.start()
    r.ids_all[z, y, c] = r.ids[...]
    r.norms_all[z, y, c, x] = r.norms[...]
    small_stages = (
        [small(r.ids_all.at[z, y, c], k, z_dev[k]) for k in range(3)]
        + [small(r.norms_all.at[z, y, c, x], 3 + k, z_dev[k]) for k in range(3)],
        [small(r.ids_all.at[:, y, c], 6, y_dev), small(r.norms_all.at[:, y, c, x], 7, y_dev)],
        [small(r.ids_all.at[:, :, c], 8, c_dev), small(r.norms_all.at[:, :, c, x], 9, c_dev)],
        [small(r.norms_all.at[:, :, :, x], 10, x_dev)],
    )
    for number, stage in enumerate(small_stages):
        for part in stage:
            part.start()
        if number == 0:
            for piece in own:
                piece.wait()
            pump()
            pump()
            for book in range(books):
                for high in range(high_count):
                    r.stacked[book, high * columns : (high + 1) * columns, :] = r.table[
                        book, :, high * lanes : (high + 1) * lanes
                    ].astype(BF)
        for part in stage:
            part.wait()
        if number == 2:
            pump()
    for group in range(8):
        parts = [
            r.norms_all[group // 2, group % 2, j // 2, j % 2] for j in range(4)
        ]
        r.norm_rows[:, group * 128 : (group + 1) * 128] = parts[0] + parts[1] + parts[2] + parts[3]
    r.gains[...] = r.norm_rows[0:4, :]

    spread = lax.broadcasted_iota(jnp.int32, (lanes, rows), 0)

    def look_block(step, carry):
        target = lax.rem(me + step, devices)
        dp, member = lax.div(target, 2), lax.rem(target, 2)
        at = (lax.div(dp, 4), lax.rem(lax.div(dp, 2), 2), lax.rem(dp, 2))
        total = jnp.zeros((columns, rows), F32)
        for book in range(books):
            ids = jnp.concatenate(
                [r.ids_all[(*at, clips * member + m, pl.ds(book, 1))] for m in range(clips)], axis=1
            )
            low_ids, high_ids = ids & (lanes - 1), lax.shift_right_logical(ids, 8)
            hot = jnp.where(spread == low_ids, 1.0, 0.0).astype(BF)
            found = dot_nn(r.stacked[book], hot)
            for high in range(high_count):
                total = total + jnp.where(
                    high_ids == high, found[high * columns : (high + 1) * columns], 0.0
                )
        r.looked[step] = total
        return carry

    def look_copy(step):
        return pltpu.make_async_remote_copy(
            src_ref=r.looked.at[step],
            dst_ref=r.landed.at[me],
            send_sem=r.look_send.at[step],
            recv_sem=r.look_recv.at[step],
            device_id=device_of(lax.rem(me + step, devices)),
            device_id_type=MESH,
        )

    def look_and_send(step, carry):
        look_block(step, carry)
        look_copy(step).start()
        return carry

    for part in range(4):
        lax.fori_loop(1 + 8 * part, min(9 + 8 * part, devices), look_and_send, 0)
        pump()
    look_block(0, 0)
    r.landed[me] = r.looked[0]

    for part_in in small_y:
        part_in.wait()
    code = lax.broadcasted_iota(jnp.int32, (128, r.teach.shape[2]), 0) + (x * 2 + y) * part_size
    teach_count = r.teach.shape[1] - 8

    def want(book):
        def block(index, carry):
            here = code + index * 128
            for side in range(2):
                total = jnp.zeros(here.shape, F32)
                for i in range(teach_count):
                    total = total + jnp.where(here == r.teach_all[side, book, i : i + 1, :], 1.0, 0.0)
                hit = jnp.where(
                    here == r.teach_all[side, book, teach_count : teach_count + 1, :], 1.0, 0.0
                )
                r.wanted[book, side * 128 : side * 128 + 128, chunk(index, 128)] = (
                    total * (1.0 / teach_count) + hit
                ).T
            return carry

        lax.fori_loop(0, part_size // 128, block, 0)

    for book in range(books):
        want(book)
        pump()

    def look_wait(step, carry):
        look_copy(step).wait_recv()
        return carry

    lax.fori_loop(1, devices, look_wait, 0)

    def place_rows(index, carry):
        cols = chunk(index, 128)
        block = jnp.concatenate([r.landed[index * 4 + j] for j in range(4)], axis=0).T
        angles = r.angles[:, cols]
        r.xs[0, :, cols] = block + jnp.concatenate([angles] * clips, axis=0)
        return carry

    lax.fori_loop(0, r.xs.shape[2] // 128, place_rows, 0)

    def norm(index, low_ref):
        norm_rows_low(
            r.xs.at[index],
            r.norm_rows.at[index : index + 1],
            r.norm_rows.at[4 + index : 5 + index],
            low_ref,
        )

    def product(left_ref, w, out_ref):
        def part(n, carry):
            cols = chunk(n, 256)
            out_ref[:, cols] = dot_nn(left_ref[...], w[:, cols]).astype(BF)
            return carry

        lax.fori_loop(0, 4, part, 0)

    def residual(left_ref, w, before, after):
        def part(n, carry):
            cols = chunk(n, 256)
            r.xs[after, :, cols] = r.xs[before, :, cols] + dot_nn(left_ref[...], w[:, cols])
            return carry

        lax.fori_loop(0, 4, part, 0)

    store(r.xs.at[0], r.x0)
    norm(0, r.hs.at[0])
    store(r.hs.at[0], r.h1)
    for k in range(3):
        product(r.hs.at[0], next_weight(), r.qkv.at[k])
        store(r.qkv.at[k], (r.q1, r.k1, r.v1)[k])
    pump()
    attend_rows(r.qkv.at[0], r.qkv.at[1], r.qkv.at[2], r.mixed.at[0], clips, True)
    store(r.mixed.at[0], r.o1)
    residual(r.mixed.at[0], next_weight(), 0, 1)
    store(r.xs.at[1], r.x1)
    norm(1, r.hs.at[1])
    store(r.hs.at[1], r.h2)
    product(r.hs.at[1], next_weight(), r.query2)
    store(r.query2, r.q2)
    for k in range(2):
        product(r.text, next_weight(), r.kv2.at[k])
        store(r.kv2.at[k], (r.k2, r.v2)[k])
    pump()
    attend_rows(r.query2, r.kv2.at[0], r.kv2.at[1], r.mixed.at[1], clips, False)
    store(r.mixed.at[1], r.o2)
    residual(r.mixed.at[1], next_weight(), 1, 2)
    store(r.xs.at[2], r.x2)
    norm(2, r.hs.at[2])
    store(r.hs.at[2], r.h3)
    pieces = r.uppers.shape[0]
    for j in range(pieces):
        w = next_weight()

        def part(n, carry):
            cols = chunk(n, 256)
            upper = dot_nn(r.hs[2], w[:, cols])
            r.uppers[j, :, cols] = upper
            r.acts[j, :, cols] = (upper * (0.5 * (1.0 + lax.erf(upper * math.sqrt(0.5))))).astype(BF)
            return carry

        lax.fori_loop(0, 4, part, 0)
        store(r.uppers.at[j], r.upper.at[j])
        store(r.acts.at[j], r.act.at[j])
    for j in range(pieces):
        w = next_weight()

        def part(n, carry):
            cols = chunk(n, 256)
            before = r.xs[2, :, cols] if j == 0 else r.xs[3, :, cols]
            r.xs[3, :, cols] = before + dot_nt(r.acts[j], w[cols, :])
            return carry

        lax.fori_loop(0, 4, part, 0)
    store(r.xs.at[3], r.x3)
    norm(3, r.final)
    half = r.pair.shape[1]
    mine = y * 2 + x
    r.pair[mine] = dot_nn(r.pick[...], r.final[...]).astype(BF)

    square = (x_dev, y_dev, device(z, 1 - y, c, 1 - x))

    def exchange(ref, first_slot):
        return [
            pltpu.make_async_remote_copy(
                src_ref=ref.at[mine],
                dst_ref=ref.at[mine],
                send_sem=r.pair_send.at[first_slot + slot],
                recv_sem=r.pair_recv.at[first_slot + slot],
                device_id=target,
                device_id_type=MESH,
            )
            for slot, target in enumerate(square)
        ]

    trade = exchange(r.pair, 0)
    for piece in trade:
        piece.start()
    for piece in trade:
        piece.wait()
    pair_count = 4 * half
    stat_lane = lax.broadcasted_iota(jnp.int32, (pair_count, 128), 1)
    stats = jnp.zeros((pair_count, 128), F32)
    for k in range(books):
        while heads_loading[0] <= k:
            pump()
        head_copy(k).wait()

        def logit_part(n, carry):
            cols = chunk(n, 256)
            pair = jnp.concatenate([r.pair[m] for m in range(4)], axis=0)
            w = r.head_weight[k, :, :, :, :, cols].reshape(-1, 256)
            r.logits[k, :, cols] = dot_nn(pair, w)
            return carry

        lax.fori_loop(0, part_size // 256, logit_part, 0)
        highest = jnp.max(r.logits[k], axis=-1, keepdims=True)
        exp_sum = jnp.sum(jnp.exp(r.logits[k] - highest), axis=-1, keepdims=True)
        stats = jnp.where(stat_lane == k, highest, stats)
        stats = jnp.where(stat_lane == books + k, exp_sum, stats)
    r.stats[mine] = stats
    trade = exchange(r.stats, 3)
    for piece in trade:
        piece.start()
    for m in range(4):
        store(r.pair.at[m], r.pair_rows.at[m])
    for piece in trade:
        piece.wait()
    row_info = jnp.concatenate([r.rows_all[0], r.rows_all[1]], axis=0)
    weight_col = row_info[:, books : books + 1]
    member = lax.div(lax.broadcasted_iota(jnp.int32, (pair_count, 1), 0), half)
    owned = jnp.where(member == mine, 1.0, 0.0)
    loss_col = jnp.zeros((pair_count, 1), F32)
    for k in range(books):
        valid = row_info[:, k : k + 1]
        tops = [r.stats[m][:, k : k + 1] for m in range(4)]
        sums = [r.stats[m][:, books + k : books + k + 1] for m in range(4)]
        top = jnp.maximum(jnp.maximum(tops[0], tops[1]), jnp.maximum(tops[2], tops[3]))
        exp_sum = sum(sums[m] * jnp.exp(tops[m] - top) for m in range(4))
        log_total = top + jnp.log(exp_sum)
        loss_col = loss_col + owned * weight_col * (valid + 1.0) * log_total
        scaled = weight_col * (1.0 / denominator)

        def grad_part(n, total):
            cols = chunk(n, 256)
            logits, wanted = r.logits[k, :, cols], r.wanted[k, :, cols]
            r.logit_grads[k, :, cols] = (
                scaled * ((valid + 1.0) * jnp.exp(logits - log_total) - wanted)
            ).astype(BF)
            return total + jnp.sum(wanted * logits, axis=-1, keepdims=True)

        picked = lax.fori_loop(0, part_size // 256, grad_part, jnp.zeros((pair_count, 1), F32))
        loss_col = loss_col - weight_col * picked
        store(r.logit_grads.at[k], r.grad_logits.at[k])
    r.loss[...] = jnp.broadcast_to(jnp.sum(loss_col, axis=0, keepdims=True), r.loss.shape)

    def look_done(step, carry):
        look_copy(step).wait_send()
        return carry

    lax.fori_loop(1, devices, look_done, 0)
    for item in range(count):
        for part in first(item) + second(item) + third(item) + fourth(item):
            part.wait_send()
        if order[item][0] == "a":
            hop_done(item)
    for piece in stores:
        piece.wait()


def forward_fast(clips, denominator, special, operands):
    named = ForwardRefs(*operands, *(None,) * (len(ForwardRefs._fields) - len(operands)))
    books, frames = named.ids.shape[1:]
    rows, width = clips * frames, named.layer.shape[2]
    text_rows, pair_count = named.text.shape[0], 2 * named.teach.shape[2]
    codes, columns = named.head_own.shape[2] // 2, named.table.shape[1]
    lanes = 256
    high_count = named.table.shape[2] // lanes
    count = books + len(UNITS)
    pieces = GROUPS[-1]
    vmem, dma = pltpu.VMEM, pltpu.SemaphoreType.DMA
    any_spec, vmem_spec = pl.BlockSpec(memory_space=pl.ANY), pl.BlockSpec(memory_space=vmem)

    def shaped(shape, dtype=BF):
        return jax.ShapeDtypeStruct(shape, dtype)

    in_vmem = (
        shaped((4, 2, 2) + named.ids.shape, jnp.int32),
        shaped((4, width), F32),
        shaped((8, 128), F32),
    )
    in_hbm = (
        (shaped((books, 4, 2, 2, named.head_own.shape[1], codes)),)
        + tuple(shaped((size, 4, 2, 2, 2) + named.layer.shape[1:]) for size in GROUPS)
        + (shaped((books, pair_count, codes)), shaped((4, pair_count // 4, width)))
        + (shaped((rows, width), F32),) * 4
        + (shaped((rows, width)),) * 8
        + (shaped((text_rows, width)),) * 2
        + (shaped((rows, width)), shaped((pieces, rows, width), F32), shaped((pieces, rows, width)))
    )
    results = pl.pallas_call(
        functools.partial(forward_kernel, clips, denominator, special),
        out_shape=in_vmem + in_hbm,
        in_specs=[vmem_spec] * len(operands),
        out_specs=(vmem_spec,) * len(in_vmem) + (any_spec,) * len(in_hbm),
        scratch_shapes=[
            vmem((4, 2, 2, 2, 8, 128), F32),
            vmem((2,) + named.teach.shape, jnp.int32),
            vmem((2,) + named.row_info.shape, F32),
            vmem((8, width), F32),
            vmem((books, high_count * columns, lanes), BF),
            vmem((32, columns, rows), F32),
            vmem((32, columns, rows), F32),
            vmem((4, rows, width), F32),
            vmem((3, rows, width), BF),
            vmem((3, rows, width), BF),
            vmem((2, rows, width), BF),
            vmem((rows, width), BF),
            vmem((2, text_rows, width), BF),
            vmem((pieces, rows, width), F32),
            vmem((pieces, rows, width), BF),
            vmem((rows, width), BF),
            vmem((4, pair_count // 4, width), BF),
            vmem((books, pair_count, codes), F32),
            vmem((books, pair_count, codes), F32),
            vmem((books, pair_count, codes), BF),
            vmem((4, pair_count, 128), F32),
            vmem((3, width, width), BF),
            vmem((books, 4, 2, 2, named.head_own.shape[1], codes), BF),
            dma((count, 14)),
            dma((count, 14)),
            dma((len(UNITS) + 1,)),
            dma((13,)),
            dma((13,)),
            dma((32,)),
            dma((32,)),
            dma((3 + books,)),
            dma((44,)),
            dma((6,)),
            dma((6,)),
        ],
        compiler_params=pltpu.CompilerParams(
            collective_id=1, has_side_effects=True, vmem_limit_bytes=58 * 2**20
        ),
    )(*operands)
    return ForwardRefs(
        *operands,
        *results,
        *(None,) * (len(ForwardRefs._fields) - len(operands) - len(results)),
    )


def low(values):
    return values.astype(BF)


def ein(formula, left, right):
    return jnp.einsum(formula, left, right, preferred_element_type=F32)


def norm_stats(values):
    average = jnp.mean(values, axis=-1, keepdims=True)
    centred = values - average
    spread = jnp.mean(centred * centred, axis=-1, keepdims=True)
    scale = lax.rsqrt(spread + NORM_EPS)
    return centred * scale, scale


def norm_forward(values, gain, bias):
    hat, scale = norm_stats(values)
    return hat * (1.0 + gain) + bias


def norm_backward(values, gain, cotangent):
    hat, scale = norm_stats(values)
    scaled = cotangent * (1.0 + gain)
    mean_one = jnp.mean(scaled, axis=-1, keepdims=True)
    mean_two = jnp.mean(scaled * hat, axis=-1, keepdims=True)
    return (
        (scaled - mean_one - hat * mean_two) * scale,
        jnp.sum(cotangent * hat, axis=0),
        jnp.sum(cotangent, axis=0),
    )


def sinusoid(frames, model_width):
    half_width = model_width // 2
    freq_rates = jnp.exp(
        jnp.arange(half_width, dtype=F32) * (-math.log(10000.0) / (half_width - 1))
    )
    angles = jnp.arange(frames, dtype=F32)[:, None] * freq_rates[None, :]
    return jnp.concatenate([jnp.sin(angles), jnp.cos(angles)], axis=1)


def delay_ids(codes, offsets, special):
    frames = codes.shape[2]
    frame = jnp.arange(frames, dtype=jnp.int32)[None, None, :]
    inputs = jnp.full_like(codes, special)
    targets = jnp.full_like(codes, special)
    padded = jnp.pad(codes, ((0, 0), (0, 0), (4, 0)), constant_values=special)
    for shift in range(4):
        is_shift = (offsets == shift)[:, :, None]
        targets = jnp.where(is_shift, padded[:, :, 4 - shift : 4 - shift + frames], targets)
        inputs = jnp.where(is_shift, padded[:, :, 3 - shift : 3 - shift + frames], inputs)
    return inputs, targets


def split_heads(matrix, clips):
    return matrix.reshape(clips, matrix.shape[0] // clips, HEADS, -1)


def raw_scores(queries, keyset, causal):
    scores = ein("bqhe,bkhe->bhqk", queries, keyset) * SCORE_SCALE
    if causal:
        length = scores.shape[2]
        allowed = jnp.arange(length)[:, None] >= jnp.arange(length)[None, :]
        scores = jnp.where(allowed[None, None], scores, NEG_FILL)
    return scores


def attend_forward(queries, keyset, valset, clips, causal):
    queries, keyset, valset = (split_heads(m, clips) for m in (queries, keyset, valset))
    scores = raw_scores(queries, keyset, causal)
    highest = jnp.max(scores, axis=-1, keepdims=True)
    exponents = jnp.exp(scores - highest)
    denominator = jnp.sum(exponents, axis=-1, keepdims=True)
    probs = exponents / denominator
    mixed = ein("bhqk,bkhe->bqhe", low(probs), valset)
    return low(mixed).reshape(mixed.shape[0] * mixed.shape[1], -1), probs


def attend_backward(queries, keyset, valset, probs, grad_mixed, clips):
    queries, keyset, valset, grad_mixed = (
        split_heads(m, clips) for m in (queries, keyset, valset, grad_mixed)
    )
    grad_probs = ein("bqhe,bkhe->bhqk", grad_mixed, valset)
    grad_values = low(ein("bhqk,bqhe->bkhe", low(probs), grad_mixed))
    grad_scores = low(
        probs * (grad_probs - jnp.sum(probs * grad_probs, axis=-1, keepdims=True))
    )
    grad_queries = low(ein("bhqk,bkhe->bqhe", grad_scores, keyset) * SCORE_SCALE)
    grad_keys = low(ein("bhqk,bqhe->bkhe", grad_scores, queries) * SCORE_SCALE)
    return tuple(
        m.reshape(m.shape[0] * m.shape[1], -1) for m in (grad_queries, grad_keys, grad_values)
    )


def normal_cdf(values):
    return 0.5 * (1.0 + lax.erf(values * math.sqrt(0.5)))


def adam_step(weight, first_moment, second_moment, gradient, factor, corr_one, corr_two):
    clipped = gradient * factor
    first_next = BETA_ONE * first_moment + (1.0 - BETA_ONE) * clipped
    second_next = BETA_TWO * second_moment + (1.0 - BETA_TWO) * clipped * clipped
    update = (
        first_next / corr_one / (jnp.sqrt(second_next / corr_two) + ADAM_EPS) + DECAY_RATE * weight
    )
    return (weight - LEARN_RATE * update, first_next, second_next)


def columns_apart(matrix, pieces):
    count, rows, width = matrix.shape
    parts = matrix.reshape(count, rows, pieces, width // pieces).transpose(0, 2, 1, 3)
    return parts.reshape(count * pieces, rows, width // pieces)


def columns_together(parts, pieces):
    total, rows, width = parts.shape
    matrix = parts.reshape(total // pieces, pieces, rows, width).transpose(0, 2, 1, 3)
    return matrix.reshape(total // pieces, rows, pieces * width)


def local(
    fast,
    audio_codes,
    delay_offsets,
    clip_lengths,
    loss_positions,
    teacher_ids,
    text_states,
    step_count,
    in_proj,
    in_proj_mean,
    in_proj_sq,
    out_proj,
    out_proj_mean,
    out_proj_sq,
    ffn_proj,
    ffn_proj_mean,
    ffn_proj_sq,
    embed_table,
    embed_table_mean,
    embed_table_sq,
    head_table,
    head_table_mean,
    head_table_sq,
    norm_gain,
    norm_gain_mean,
    norm_gain_sq,
    norm_bias,
    norm_bias_mean,
    norm_bias_sq,
):
    clips = text_states.shape[0]
    vocab_count = lax.axis_size("vocab")
    device_count = lax.axis_size("dp") * vocab_count
    vocab_index = lax.axis_index("vocab")
    book_count = head_table.shape[0]
    pos_count = loss_positions.shape[1]
    frames = audio_codes.shape[2]
    table_rows = embed_table.shape[1]
    special = table_rows - 1
    half_vocab = head_table.shape[2]
    vocab_base = vocab_index * half_vocab
    model_width = text_states.shape[2]
    rows = clips * frames
    ffn_pieces = ffn_proj.shape[2] // model_width
    denominator = float(clips * device_count * pos_count * book_count)

    inputs, targets = delay_ids(audio_codes, delay_offsets, special)
    own_first = vocab_index * clips
    own_inputs = lax.dynamic_slice_in_dim(inputs, own_first, clips, 0)
    own_positions = lax.dynamic_slice_in_dim(loss_positions, own_first, clips, 0)

    layer_local = jnp.concatenate(
        [
            low(in_proj[0:3]),
            low(out_proj[0:1]),
            low(in_proj[3:6]),
            low(out_proj[1:2]),
            columns_apart(low(ffn_proj), ffn_pieces),
        ],
        axis=0,
    )
    head_local = low(head_table)
    norms_local = low(jnp.concatenate([norm_gain, norm_bias], axis=0))
    target_at = jnp.take_along_axis(targets, loss_positions[:, None, :], axis=2)
    pair_count = target_at.shape[0] * pos_count
    target_at = target_at.transpose(1, 0, 2).reshape(book_count, pair_count)
    valid = (target_at != special).astype(F32)
    row_weight = (loss_positions < clip_lengths[:, None]).astype(F32).reshape(pair_count)
    flat_positions = (own_positions + jnp.arange(clips, dtype=jnp.int32)[:, None] * frames).reshape(-1)
    pick = flat_positions[:, None] == jnp.arange(rows, dtype=jnp.int32)[None, :]
    text = text_states.reshape(-1, model_width)
    angles = sinusoid(frames, model_width)
    if fast:
        device_index = lax.axis_index("dp") * vocab_count + vocab_index
        norm_width = norm_gain.shape[1]
        norms_placed = lax.dynamic_update_slice(
            jnp.zeros((8, 128), F32),
            norms_local.astype(F32),
            (0, lax.rem(device_index, 128 // norm_width) * norm_width),
        )
        table_t = jnp.swapaxes(embed_table, 1, 2)
        table_t = jnp.pad(table_t, ((0, 0), (0, 0), (0, -table_rows % 256)))
        teach = jnp.concatenate(
            [
                teacher_ids.transpose(1, 3, 0, 2).reshape(book_count, -1, pair_count),
                jnp.where(target_at == special, -1, target_at)[:, None, :],
                jnp.full((book_count, 7, pair_count), -1, jnp.int32),
            ],
            axis=1,
        )
        row_info = jnp.concatenate([valid, row_weight[None]], axis=0).T
        row_info = jnp.pad(row_info, ((0, 0), (0, 128 - row_info.shape[1])))
        kept = forward_fast(
            clips,
            denominator,
            special,
            (
                inputs,
                norms_placed,
                table_t,
                layer_local,
                head_local,
                angles,
                text,
                pick.astype(BF),
                teach,
                row_info,
            ),
        )

        def joined(part):
            return part.reshape(part.shape[0], -1, part.shape[-1])

        done = backward_fast(
            clips,
            table_rows,
            (
                kept.grad_logits,
                kept.pair_rows.reshape(-1, model_width),
                pick.T.astype(BF),
                kept.x0,
                kept.x1,
                kept.x2,
                kept.x3,
                kept.h1,
                kept.h2,
                kept.h3,
                kept.q1,
                kept.k1,
                kept.v1,
                kept.o1,
                kept.q2,
                kept.k2,
                kept.v2,
                kept.o2,
                kept.upper,
                kept.act,
                text,
                kept.gains,
                joined(kept.head),
                joined(kept.w0),
                joined(kept.w1),
                joined(kept.w2),
                joined(kept.w3),
                joined(kept.w4),
                joined(kept.w5),
                joined(kept.w6),
                kept.ids_all,
                kept.loss,
            ),
        )
        norm_shard = lax.dynamic_slice_in_dim(
            done.norm_out, lax.rem(device_index, 128 // norm_width) * norm_width, norm_width, 1
        )
        gradients = (
            done.in_out,
            done.out_out,
            done.ffn_out,
            jnp.swapaxes(done.embed_out, 1, 2),
            done.head_out.reshape(head_table.shape),
            norm_shard[:4],
            norm_shard[4:],
        )
        square_total, loss_total = jnp.sum(done.total_out[0]), done.total_out[1, 0, 0]
    else:
        norms = lax.all_gather(norms_local, BOTH, axis=1, tiled=True).astype(F32)
        table = lax.all_gather(low(embed_table), BOTH, axis=2, tiled=True)
        embedded = jnp.zeros((rows, model_width), F32)
        for book in range(book_count):
            embedded = embedded + jnp.take(
                table[book], own_inputs[:, book].reshape(-1), axis=0
            ).astype(F32)
        layer_all = lax.all_gather(layer_local, BOTH, axis=1, tiled=True)
        starts = [sum(GROUPS[:g]) for g in range(len(GROUPS))]
        layer_parts = [layer_all[s : s + g] for s, g in zip(starts, GROUPS)]
        head_all = lax.all_gather(head_local, "dp", axis=1, tiled=True)
        w_self, w_self_out, w_query, w_text, w_cross_out, w_up, w_down = layer_parts
        gains, biases = norms[:4], norms[4:]

        start = embedded + jnp.tile(angles, (clips, 1))
        normed_self = low(norm_forward(start, gains[0], biases[0]))
        proj = low(ein("rd,kde->kre", normed_self, w_self))
        self_out, self_probs = attend_forward(proj[0], proj[1], proj[2], clips, True)
        after_self = start + ein("rd,de->re", self_out, w_self_out[0])
        normed_cross = low(norm_forward(after_self, gains[1], biases[1]))
        cross_query = low(ein("rd,de->re", normed_cross, w_query[0]))
        cross_text = low(ein("td,kde->kte", text, w_text))
        cross_out, cross_probs = attend_forward(cross_query, cross_text[0], cross_text[1], clips, False)
        after_cross = after_self + ein("rd,de->re", cross_out, w_cross_out[0])
        normed_ffn = low(norm_forward(after_cross, gains[2], biases[2]))
        upper = ein("rd,jdf->jrf", normed_ffn, w_up)
        cdf = normal_cdf(upper)
        active = low(upper * cdf)
        after_ffn = after_cross + ein("jrf,jdf->rd", active, w_down)
        final_norm = low(norm_forward(after_ffn, gains[3], biases[3]))
        chosen = low(ein("pr,rd->pd", pick.astype(BF), final_norm))

        pair_rows = lax.all_gather(chosen, "vocab", axis=0, tiled=True)
        teach = teacher_ids.transpose(1, 0, 2, 3).reshape(book_count, pair_count, -1)
        local_ids = vocab_base + jnp.arange(half_vocab, dtype=jnp.int32)
        counts = jnp.sum(
            (teach[:, :, :, None] == local_ids[None, None, None, :]).astype(F32), axis=2
        )
        wanted = counts / teach.shape[2] + valid[:, :, None] * (
            target_at[:, :, None] == local_ids[None, None, :]
        ).astype(F32)
        logits = ein("rd,kdv->krv", pair_rows, head_all)
        highest = jnp.max(logits, axis=-1)
        exp_sum = jnp.sum(jnp.exp(logits - highest[:, :, None]), axis=-1)
        stats = lax.all_gather(jnp.stack([highest, exp_sum]), "vocab")
        top_all = jnp.max(stats[:, 0], axis=0)
        sum_all = jnp.sum(stats[:, 1] * jnp.exp(stats[:, 0] - top_all[None]), axis=0)
        log_total = top_all + jnp.log(sum_all)
        row_loss = row_weight[None, :] * (valid + 1.0) * log_total
        own_rows = clips * pos_count
        loss_sum = jnp.sum(
            lax.dynamic_slice_in_dim(row_loss, vocab_index * own_rows, own_rows, 1)
        ) - jnp.sum(row_weight[None, :] * jnp.sum(wanted * logits, axis=-1))
        scaled = (row_weight / denominator)[None, :, None]
        grad_logits = low(
            scaled * ((valid + 1.0)[:, :, None] * jnp.exp(logits - log_total[:, :, None]) - wanted)
        )
        grad_head = ein("rd,krv->kdv", pair_rows, grad_logits)
        grad_rows = ein("krv,kdv->rd", grad_logits, head_all)
        grad_chosen = lax.psum_scatter(low(grad_rows), "vocab", scatter_dimension=0, tiled=True).astype(F32)

        grad_final = jnp.einsum(
            "pr,pd->rd", pick.astype(F32), grad_chosen, precision=lax.Precision.HIGHEST
        )
        grad_ffn_res, gain_three, bias_three = norm_backward(after_ffn, gains[3], grad_final)
        low_ffn = low(grad_ffn_res)
        grad_down = ein("rd,jrf->jdf", low_ffn, active)
        grad_active = ein("rd,jdf->jrf", low_ffn, w_down)
        slope = cdf + upper * jnp.exp(-0.5 * upper * upper) * (1.0 / math.sqrt(2.0 * math.pi))
        grad_upper = low(grad_active * slope)
        grad_up = ein("rd,jrf->jdf", normed_ffn, grad_upper)
        grad_normed = ein("jrf,jdf->rd", grad_upper, w_up)
        grad_inner, gain_two, bias_two = norm_backward(after_cross, gains[2], grad_normed)
        grad_cross_res = grad_ffn_res + grad_inner
        low_cross = low(grad_cross_res)
        grad_cross_out = ein("rd,re->de", cross_out, low_cross)[None]
        grad_mixed = low(ein("re,de->rd", low_cross, w_cross_out[0]))
        grad_query, grad_key, grad_value = attend_backward(
            cross_query, cross_text[0], cross_text[1], cross_probs, grad_mixed, clips
        )
        grad_w_query = ein("rd,re->de", normed_cross, grad_query)[None]
        grad_w_text = ein("td,kte->kde", text, jnp.stack([grad_key, grad_value]))
        grad_normed = ein("re,de->rd", grad_query, w_query[0])
        grad_inner, gain_one, bias_one = norm_backward(after_self, gains[1], grad_normed)
        grad_self_res = grad_cross_res + grad_inner
        low_self = low(grad_self_res)
        grad_self_out = ein("rd,re->de", self_out, low_self)[None]
        grad_mixed = low(ein("re,de->rd", low_self, w_self_out[0]))
        grad_proj = jnp.stack(
            attend_backward(proj[0], proj[1], proj[2], self_probs, grad_mixed, clips)
        )
        grad_w_self = ein("rd,kre->kde", normed_self, grad_proj)
        grad_normed = ein("kre,kde->rd", grad_proj, w_self)
        grad_inner, gain_zero, bias_zero = norm_backward(start, gains[0], grad_normed)
        grad_start = grad_self_res + grad_inner

        layer_grads = (
            grad_w_self, grad_self_out, grad_w_query, grad_w_text, grad_cross_out, grad_up, grad_down
        )
        norm_grads = jnp.stack(
            [gain_zero, gain_one, gain_two, gain_three, bias_zero, bias_one, bias_two, bias_three]
        )
        embed_sum = jnp.stack(
            [
                jax.ops.segment_sum(
                    grad_start, own_inputs[:, book].reshape(-1), num_segments=table_rows
                )
                for book in range(book_count)
            ]
        )
        embed_shard = lax.psum_scatter(embed_sum, BOTH, scatter_dimension=2, tiled=True)
        layer_shard = lax.psum_scatter(
            jnp.concatenate(layer_grads, axis=0), BOTH, scatter_dimension=1, tiled=True
        )
        head_shard = lax.psum_scatter(grad_head, "dp", scatter_dimension=1, tiled=True)
        big_gradients = (
            jnp.concatenate([layer_shard[0:3], layer_shard[4:7]], axis=0),
            jnp.concatenate([layer_shard[3:4], layer_shard[7:8]], axis=0),
            columns_together(layer_shard[8:], ffn_pieces),
            embed_shard,
            head_shard,
        )
        square_sum = jnp.zeros((), F32)
        for shard_grad in big_gradients:
            square_sum = square_sum + jnp.sum(shard_grad * shard_grad)
        norm_total = lax.psum(norm_grads, BOTH)
        square_total, loss_total = lax.psum((square_sum, loss_sum), BOTH)
        square_total = square_total + jnp.sum(norm_total * norm_total)
        norm_width = norm_gain.shape[1]
        norm_shard = lax.dynamic_slice_in_dim(
            norm_total, (lax.axis_index("dp") * vocab_count + vocab_index) * norm_width, norm_width, 1
        )
        gradients = big_gradients + (norm_shard[:4], norm_shard[4:])
    loss_value = loss_total / denominator
    grad_norm = jnp.sqrt(square_total)
    factor = CLIP_LIMIT / jnp.maximum(grad_norm, CLIP_LIMIT)
    steps_float = step_count.astype(F32)
    corr_one = 1.0 - jnp.power(BETA_ONE, steps_float)
    corr_two = 1.0 - jnp.power(BETA_TWO, steps_float)
    masters = (in_proj, out_proj, ffn_proj, embed_table, head_table, norm_gain, norm_bias)
    mean_list = (
        in_proj_mean,
        out_proj_mean,
        ffn_proj_mean,
        embed_table_mean,
        head_table_mean,
        norm_gain_mean,
        norm_bias_mean,
    )
    square_list = (
        in_proj_sq,
        out_proj_sq,
        ffn_proj_sq,
        embed_table_sq,
        head_table_sq,
        norm_gain_sq,
        norm_bias_sq,
    )
    outputs = [loss_value, grad_norm]
    for index in range(7):
        outputs.extend(
            adam_step(
                masters[index],
                mean_list[index],
                square_list[index],
                gradients[index],
                factor,
                corr_one,
                corr_two,
            )
        )
    return tuple(outputs)


def solution(mesh):
    by_row = P(None, BOTH, None)
    by_column = P(None, None, BOTH)
    by_head = P(None, "dp", "vocab")
    by_feature = P(None, BOTH)
    weights = (
        (by_row,) * 9 + (by_column,) * 3 + (by_head,) * 3 + (by_feature,) * 6
    )
    placed = (
        P("dp", None, None),
        P("dp", None),
        P("dp"),
        P("dp", None),
        P("dp", None, None, None),
        P(BOTH, None, None),
        P(),
    ) + weights
    fast = dict(mesh.shape) == {"dp": 16, "vocab": 2}
    return jax.shard_map(
        functools.partial(local, fast),
        mesh=mesh,
        in_specs=placed,
        out_specs=(P(), P()) + weights,
        check_vma=False,
    )
```

```python
import functools
import math
from typing import Any, NamedTuple

import jax
import jax.numpy as jnp
from jax import lax
from jax.experimental import pallas as pl
from jax.experimental.pallas import tpu as pltpu
from jax.sharding import PartitionSpec as P

HEADS = 16
NORM_EPS = 1e-05
SCORE_SCALE = 0.125
NEG_FILL = -1e30
CLIP_LIMIT = 3.0
BETA_ONE = 0.9
BETA_TWO = 0.95
LEARN_RATE = 0.05
DECAY_RATE = 0.1
ADAM_EPS = 1e-08
BOTH = ("dp", "vocab")
MESH = pl.DeviceIdType.MESH
BF = jnp.bfloat16
F32 = jnp.float32
DEVICES = 32
GROUPS = (3, 1, 1, 2, 1, 4, 4)
UNITS = tuple((group, index) for group, size in enumerate(GROUPS) for index in range(size))


def place():
    dp, x = lax.axis_index("dp"), lax.axis_index("vocab")
    return lax.div(dp, 4), lax.rem(lax.div(dp, 2), 2), lax.rem(dp, 2), x


def device(z, y, c, x):
    return ((z * 2 + y) * 2 + c, x)


def partners():
    z, y, c, x = place()
    line = [lax.rem(z + step, 4) for step in (1, 2, 3)]
    return (
        line,
        [device(other, y, c, x) for other in line],
        device(z, 1 - y, c, x),
        device(z, y, c, 1 - x),
        device(z, y, 1 - c, x),
    )


def device_of(index):
    return (lax.div(index, 2), lax.rem(index, 2))


def greet_all(me):
    barrier = pltpu.get_barrier_semaphore()

    def signal(step, carry):
        pl.semaphore_signal(
            barrier, inc=1, device_id=device_of(lax.rem(me + step, DEVICES)), device_id_type=MESH
        )
        return carry

    lax.fori_loop(1, DEVICES, signal, 0)
    pl.semaphore_wait(barrier, DEVICES - 1)


def transfer_order(heads):
    order, head = [], 0
    for unit in range(len(UNITS)):
        order.append(("a", unit))
        if unit % 4 == 1 and head < heads:
            order.append(("h", head))
            head += 1
    return tuple(order)


PAIR, RES3, FFN, MIX2, CROSS, TEXT, MIX1, SELF = range(8)
LOGIT, ACT, UP = 0, 4, 8
RES2, QUERY2, KEY2, VALUE2, RES1, QUERY1, KEY1, VALUE1 = range(12, 20)
PLAN = (
    ("h", 0, PAIR, LOGIT + 0),
    ("h", 1, PAIR, LOGIT + 1),
    ("h", 2, PAIR, LOGIT + 2),
    ("h", 3, PAIR, LOGIT + 3),
    ("a", 12, RES3, ACT + 0),
    ("a", 13, RES3, ACT + 1),
    ("a", 14, RES3, ACT + 2),
    ("a", 15, RES3, ACT + 3),
    ("a", 8, FFN, UP + 0),
    ("a", 7, MIX2, RES2),
    ("a", 4, CROSS, QUERY2),
    ("a", 5, TEXT, KEY2),
    ("a", 6, TEXT, VALUE2),
    ("a", 3, MIX1, RES1),
    ("a", 9, FFN, UP + 1),
    ("a", 0, SELF, QUERY1),
    ("a", 1, SELF, KEY1),
    ("a", 2, SELF, VALUE1),
    ("a", 10, FFN, UP + 2),
    ("a", 11, FFN, UP + 3),
)
LATE = (2, 4, 6, 8)
HEAD_LATE = (2, 10, 12, 13)


def dot_nn(left, right):
    return jnp.dot(left, right, preferred_element_type=F32)


def dot_nt(left, right):
    return lax.dot_general(left, right, (((1,), (1,)), ((), ())), preferred_element_type=F32)


def dot_tn(left, right):
    return lax.dot_general(left, right, (((0,), (0,)), ((), ())), preferred_element_type=F32)


def chunk(index, size):
    return pl.ds(pl.multiple_of(index * size, size), size)


def norm_back_rows(values_ref, gain_ref, grad_ref, add_ref, out_ref, low_ref, gain_out, bias_out):
    size = 32
    one_gain = 1.0 + gain_ref[...]

    def block(index, carry):
        gain_sum, bias_sum = carry
        rows = chunk(index, size)
        values, cotangent = values_ref[rows, :], grad_ref[rows, :]
        average = jnp.mean(values, axis=-1, keepdims=True)
        centred = values - average
        scale = lax.rsqrt(jnp.mean(centred * centred, axis=-1, keepdims=True) + NORM_EPS)
        hat = centred * scale
        scaled = cotangent * one_gain
        mean_one = jnp.mean(scaled, axis=-1, keepdims=True)
        mean_two = jnp.mean(scaled * hat, axis=-1, keepdims=True)
        result = (scaled - mean_one - hat * mean_two) * scale
        if add_ref is not None:
            result = result + add_ref[rows, :]
        out_ref[rows, :] = result
        if low_ref is not None:
            low_ref[rows, :] = result.astype(BF)
        return (
            gain_sum + jnp.sum(cotangent * hat, axis=0, keepdims=True),
            bias_sum + jnp.sum(cotangent, axis=0, keepdims=True),
        )

    zero = jnp.zeros((1, values_ref.shape[1]), F32)
    gain_sum, bias_sum = lax.fori_loop(0, values_ref.shape[0] // size, block, (zero, zero))
    gain_out[...] = gain_sum
    bias_out[...] = bias_sum


def attend_back_rows(query, key, value, grad, query_out, key_out, value_out, clips, causal, share):
    rows, keys = query.shape[0] // clips, key.shape[0] // clips
    pairs = query.shape[1] // 128
    lane = lax.broadcasted_iota(jnp.int32, (1, 128), 1)
    halves = [(lane < 64).astype(F32).astype(BF), (lane >= 64).astype(F32).astype(BF)]

    def pair(index, carry):
        at_q = chunk(lax.div(index, pairs), rows)
        at_k = chunk(lax.div(index, pairs), keys)
        lanes = chunk(lax.rem(index, pairs), 128)
        q, k, v, g = query[at_q, lanes], key[at_k, lanes], value[at_k, lanes], grad[at_q, lanes]
        dq = jnp.zeros((rows, 128), F32)
        dk = jnp.zeros((keys, 128), F32)
        dv = jnp.zeros((keys, 128), F32)
        for half in halves:
            qh, kh, gh = q * half, k * half, g * half
            scores = dot_nt(qh, k) * SCORE_SCALE
            if causal:
                allowed = lax.broadcasted_iota(jnp.int32, (rows, keys), 0) >= lax.broadcasted_iota(
                    jnp.int32, (rows, keys), 1
                )
                scores = jnp.where(allowed, scores, NEG_FILL)
            exponents = jnp.exp(scores - jnp.max(scores, axis=-1, keepdims=True))
            probs = exponents / jnp.sum(exponents, axis=-1, keepdims=True)
            grad_probs = dot_nt(gh, v)
            dv = dv + dot_tn(probs.astype(BF), gh)
            inner = jnp.sum(probs * grad_probs, axis=-1, keepdims=True)
            grad_scores = (probs * (grad_probs - inner)).astype(BF)
            dq = dq + dot_nn(grad_scores, kh)
            dk = dk + dot_tn(grad_scores, qh)
        query_out[at_q, lanes] = (dq * SCORE_SCALE).astype(BF)
        key_out[at_k, lanes] = (dk * SCORE_SCALE).astype(BF)
        value_out[at_k, lanes] = dv.astype(BF)
        return carry

    first, count = share[0] * clips * pairs // share[1], clips * pairs // share[1]
    lax.fori_loop(first, first + count, pair, 0)


class BackwardRefs(NamedTuple):
    grad_logits: Any
    pair_rows: Any
    pick: Any
    x0: Any
    x1: Any
    x2: Any
    x3: Any
    h1: Any
    h2: Any
    h3: Any
    q1: Any
    k1: Any
    v1: Any
    o1: Any
    q2: Any
    k2: Any
    v2: Any
    o2: Any
    upper: Any
    act: Any
    text: Any
    gains: Any
    head: Any
    w0: Any
    w1: Any
    w2: Any
    w3: Any
    w4: Any
    w5: Any
    w6: Any
    ids_all: Any
    loss: Any
    in_out: Any
    out_out: Any
    ffn_out: Any
    head_out: Any
    embed_out: Any
    norm_out: Any
    total_out: Any
    core_in: Any
    diagonal_in: Any
    side_in: Any
    line_in: Any
    head_line: Any
    head_send: Any
    head_y: Any
    head_held: Any
    core_slot: Any
    send_slot: Any
    held: Any
    acts: Any
    ups: Any
    logit: Any
    upper_slot: Any
    qkv: Any
    query2: Any
    kv2: Any
    left: Any
    left_pair: Any
    left_text: Any
    weight: Any
    lows: Any
    query2_grad: Any
    kv2_grad: Any
    grad_x: Any
    grad_h: Any
    values: Any
    rows_in: Any
    pair_in: Any
    pick_in: Any
    gain_in: Any
    pair_send: Any
    pair_land: Any
    head_total: Any
    norm_grads: Any
    starts: Any
    starts_in: Any
    norms_in: Any
    squares: Any
    totals: Any
    totals_in: Any
    send_sem: Any
    recv_sem: Any
    weight_sem: Any
    load_sem: Any
    core_sem: Any
    upper_sem: Any
    pair_sem: Any
    far_send: Any
    far_recv: Any


def backward_kernel(clips, *refs):
    r = BackwardRefs(*refs)
    z, y, c, x = place()
    me = lax.axis_index("dp") * 2 + x
    line, z_dev, y_dev, x_dev, c_dev = partners()
    items = PLAN
    count = len(items)
    frames_all = r.x0.shape[0]
    pieces = 4

    load_count = [0]

    def load(src, dst):
        piece = pltpu.make_async_copy(src, dst, r.load_sem.at[load_count[0]])
        load_count[0] += 1
        piece.start()
        return piece

    load_logit = load(r.grad_logits, r.logit)
    load_pair = load(r.pair_rows, r.pair_in)
    load_pick = load(r.pick, r.pick_in)
    load_gains = load(r.gains, r.gain_in)
    load_x3 = load(r.x3, r.values)
    load_act = load(r.act, r.acts)
    load_h3 = load(r.h3, r.rows_in.at[0])
    load_q1 = load(r.q1, r.qkv.at[0])
    load_k1 = load(r.k1, r.qkv.at[1])
    load_v1 = load(r.v1, r.qkv.at[2])
    load_q2 = load(r.q2, r.query2)
    load_k2 = load(r.k2, r.kv2.at[0])
    load_v2 = load(r.v2, r.kv2.at[1])

    sequence = [(r.head, k) for k in range(pieces)]
    sequence += [(ref, j) for j in range(pieces) for ref in (r.w6, r.w5)]
    sequence += [(r.w4, 0), (r.w2, 0), (r.w1, 0)] + [(r.w0, k) for k in range(3)]
    slots = r.weight.shape[0]
    taken = [0]

    def weight_copy(index):
        ref, at = sequence[index]
        slot = r.weight.at[index % slots]
        if ref is r.head:
            slot = slot.at[:, 0 : ref.shape[2]]
        return pltpu.make_async_copy(ref.at[at], slot, r.weight_sem.at[index % slots])

    for index in range(slots - 1):
        weight_copy(index).start()

    def next_weight():
        index = taken[0]
        taken[0] += 1
        if index + slots - 1 < len(sequence):
            weight_copy(index + slots - 1).start()
        weight_copy(index).wait()
        return r.weight.at[index % slots]

    def upper_copy(j):
        return pltpu.make_async_copy(
            r.upper.at[j], r.upper_slot.at[j % 2], r.upper_sem.at[j % 2]
        )

    upper_copy(0).start()
    upper_copy(1).start()
    greet_all(me)

    left = (
        r.left_pair, r.left.at[0], r.left.at[1], r.left.at[2],
        r.left.at[3], r.left_text, r.left.at[0], r.left.at[2],
    )
    right = [r.logit.at[k] for k in range(pieces)]
    right += [r.acts.at[j] for j in range(pieces)] + [r.ups.at[j] for j in range(pieces)]
    right += [r.lows.at[1], r.query2_grad, r.kv2_grad.at[0], r.kv2_grad.at[1]]
    right += [r.acts.at[3], r.acts.at[0], r.acts.at[1], r.acts.at[2]]

    def copy(src, dst, item, slot, target):
        return pltpu.make_async_remote_copy(
            src_ref=src,
            dst_ref=dst,
            send_sem=r.send_sem.at[item, slot],
            recv_sem=r.recv_sem.at[item, slot],
            device_id=target,
            device_id_type=MESH,
        )

    held_slots = r.held.shape[0]

    def head_cols(index):
        return pl.ds(pl.multiple_of(index * part_size, part_size), part_size)

    part_size = r.head_out.shape[3] // 2
    half_cols = (pl.ds(0, part_size), pl.ds(part_size, part_size))

    def used(ref, item):
        return ref.at[:, :, :, :, half_cols[0]] if items[item][0] == "h" else ref

    def to_core(item):
        slot = r.send_slot.at[item % 2]
        return copy(used(slot, item), used(r.core_in.at[item], item), item, 0, c_dev)

    def core_load(item):
        slot = r.core_slot.at[item % 2]
        return pltpu.make_async_copy(
            used(r.core_in.at[item], item), used(slot, item), r.core_sem.at[item % 2]
        )

    def held_of(item):
        kind, unit = items[item][:2]
        return r.head_held.at[unit] if kind == "h" else r.held.at[item % held_slots]

    def first(item):
        kind, unit = items[item][:2]
        held = held_of(item)
        if kind == "h":
            return [
                copy(
                    held.at[other],
                    r.head_line.at[unit, slot],
                    item,
                    1 + slot,
                    z_dev[slot],
                )
                for slot, other in enumerate(line)
            ]
        diagonal = held.at[:, 1 - y, 1 - x]
        return [
            copy(diagonal.at[:, :, half_cols[n]], r.diagonal_in.at[unit, n], item, 1 + n, target)
            for n, target in enumerate((x_dev, y_dev))
        ]

    def second(item):
        kind, unit = items[item][:2]
        if kind == "h":
            return [copy(r.head_send.at[unit], r.head_y.at[unit], item, 4, y_dev)]
        held = held_of(item)
        return [
            copy(held.at[:, 1 - y, x], r.side_in.at[unit, 0], item, 3, y_dev),
            copy(held.at[:, y, 1 - x], r.side_in.at[unit, 1], item, 4, x_dev),
        ]

    def third(item):
        kind, unit = items[item][:2]
        if kind == "h":
            return []
        return [
            copy(
                r.side_in.at[unit, 0, other], r.line_in.at[unit, slot], item, 5 + slot, z_dev[slot]
            )
            for slot, other in enumerate(line)
        ]

    def left_rows(name, core):
        ref = left[name]
        return jnp.concatenate(
            [ref[pl.ds(pl.multiple_of(k * 128 + core * 64, 64), 64), :] for k in range(8)], axis=0
        )

    def wide(value):
        return value.astype(F32)

    def column_parts(item):
        return 2 if items[item][0] == "h" else 4

    def make(item):
        kind, unit, left_name, right_name = items[item]
        if item >= 2:
            to_core(item - 2).wait_send()
        slot = r.send_slot.at[item % 2]

        def columns(n, carry):
            cols = chunk(n, 256)
            value = dot_nn(left_rows(left_name, 1 - c), right[right_name][:, cols]).astype(BF)
            slot[:, :, :, :, cols] = value.reshape(4, 2, 2, 32, 256)
            return carry

        lax.fori_loop(0, column_parts(item), columns, 0)
        to_core(item).start()

    def join_core(item):
        kind, unit, left_name, right_name = items[item]
        core_load(item).wait()
        if item >= held_slots and items[item - held_slots][0] == "a":
            for part in first(item - held_slots) + second(item - held_slots):
                part.wait_send()
        held, landed = held_of(item), r.core_slot.at[item % 2]

        def columns(n, carry):
            cols = chunk(n, 256)
            value = dot_nn(left_rows(left_name, c), right[right_name][:, cols])
            value = value.reshape(4, 2, 2, 32, 256) + wide(landed[:, :, :, :, cols])
            held[:, :, :, :, cols] = value.astype(BF)
            return carry

        lax.fori_loop(0, column_parts(item), columns, 0)
        for part in first(item):
            part.start()

    def join_first(item):
        kind, unit = items[item][:2]
        held = held_of(item)
        for part in first(item):
            part.wait_recv()
        if kind == "h":
            for side in range(2):
                total = wide(held[z, side])
                for slot in range(3):
                    total = total + wide(r.head_line[unit, slot, side])
                r.head_total[side] = total
            own = r.head_total[y]
            r.head_out[unit, :, :, head_cols(y)] = own
            squared = own * own
            r.squares[:, half_cols[0]] += squared[0] + squared[1]
            r.head_send[unit] = r.head_total[1 - y].astype(BF)
        else:

            def planes(k, carry):
                held[k, 1 - y, x, :, half_cols[0]] = (
                    wide(held[k, 1 - y, x, :, half_cols[0]]) + wide(r.diagonal_in[unit, 0, k])
                ).astype(BF)
                held[k, y, 1 - x, :, half_cols[1]] = (
                    wide(held[k, y, 1 - x, :, half_cols[1]]) + wide(r.diagonal_in[unit, 1, k])
                ).astype(BF)
                return carry

            lax.fori_loop(0, 4, planes, 0)
        for part in second(item):
            part.start()

    def join_second(item):
        kind, unit = items[item][:2]
        for part in second(item):
            part.wait_recv()
        if kind == "h":
            other = wide(r.head_y[unit])
            r.head_out[unit, :, :, head_cols(1 - y)] = other
            squared = other * other
            r.squares[:, half_cols[0]] += squared[0] + squared[1]
            return
        held = held_of(item)

        def planes(k, carry):
            total = wide(held[k, y, x]) + wide(r.side_in[unit, 0, k]) + wide(r.side_in[unit, 1, k])
            r.side_in[unit, 0, k] = total.astype(BF)
            return carry

        lax.fori_loop(0, 4, planes, 0)
        for part in third(item):
            part.start()

    def finish(item):
        kind, unit = items[item][:2]
        if kind == "h":
            return
        for part in third(item):
            part.wait_recv()
        total = wide(r.side_in[unit, 0, z])
        for slot in range(3):
            total = total + wide(r.line_in[unit, slot])
        r.squares[...] += total * total
        group, index = UNITS[unit]
        if group in (1, 4):
            r.out_out[group // 4] = total
        elif group < 5:
            r.in_out[(0, 0, 3, 4)[group] + index] = total
        else:
            r.ffn_out[group - 5, :, index * total.shape[1] : (index + 1) * total.shape[1]] = total

    ticks = [0]

    def pump():
        tick = ticks[0]
        ticks[0] += 1
        item = tick - 1
        if 0 <= item < count:
            to_core(item).wait_recv()
            core_load(item).start()
        for stage_number, stage in enumerate((join_core, join_first, join_second, finish)):
            for kind, late in (("h", HEAD_LATE), ("a", LATE)):
                item = tick - late[stage_number]
                if 0 <= item < count and items[item][0] == kind:
                    stage(item)

    def unit(right_name):
        item = ticks[0]
        assert items[item][3] == right_name
        make(item)
        pump()

    r.squares[...] = jnp.zeros_like(r.squares)
    load_logit.wait()
    load_pair.wait()
    r.left_pair[...] = r.pair_in[...].T
    unit(LOGIT + 0)
    unit(LOGIT + 1)

    def pair_rows_of(k, w):
        def columns(n, carry):
            cols = chunk(n, 256)
            value = dot_nt(r.logit[k], w[cols, 0:part_size])
            r.grad_h[:, cols] = value if k == 0 else r.grad_h[:, cols] + value
            return carry

        lax.fori_loop(0, 4, columns, 0)

    for k in range(pieces):
        pair_rows_of(k, next_weight())
    half = r.pair_send.shape[1]
    mine = y * 2 + x
    square = (y * 2 + 1 - x, (1 - y) * 2 + x, (1 - y) * 2 + 1 - x)
    trade = []
    for slot, (member, target) in enumerate(
        zip(square, (x_dev, y_dev, device(z, 1 - y, c, 1 - x)), strict=True)
    ):
        r.pair_send[slot] = r.grad_h[chunk(member, half), :].astype(BF)
        trade.append(
            pltpu.make_async_remote_copy(
                src_ref=r.pair_send.at[slot],
                dst_ref=r.pair_land.at[slot],
                send_sem=r.pair_sem.at[slot],
                recv_sem=r.pair_sem.at[3 + slot],
                device_id=target,
                device_id_type=MESH,
            )
        )
    for piece in trade:
        piece.start()
    unit(LOGIT + 2)
    load_h3.wait()
    r.left[1] = r.rows_in[0].T
    load_pick.wait()
    load_gains.wait()
    load_x3.wait()
    load_act.wait()
    for piece in trade:
        piece.wait()
    chosen = r.grad_h[chunk(mine, half), :]
    for slot in range(3):
        chosen = chosen + wide(r.pair_land[slot])
    chosen_top = chosen.astype(BF)
    chosen_rest = (chosen - wide(chosen_top)).astype(BF)
    r.grad_h[...] = dot_nn(r.pick_in[...], chosen_top) + dot_nn(r.pick_in[...], chosen_rest)

    def norm_back(index, add, low_ref):
        norm_back_rows(
            r.values,
            r.gain_in.at[index : index + 1],
            r.grad_h,
            add,
            r.grad_x,
            low_ref,
            r.norm_grads.at[index : index + 1],
            r.norm_grads.at[4 + index : 5 + index],
        )

    norm_back(3, None, r.lows.at[0])
    unit(LOGIT + 3)
    load_x2 = load(r.x2, r.values)
    r.left[0] = r.lows[0].T
    load_o2 = load(r.o2, r.rows_in.at[1])
    load_h2 = load(r.h2, r.rows_in.at[0])

    def down_back(j):
        w = next_weight()
        upper_copy(j).wait()

        def columns(n, carry):
            cols = chunk(n, 256)
            grad = dot_nn(r.lows[0], w[:, cols])
            upper = r.upper_slot[j % 2, :, cols]
            slope = 0.5 * (1.0 + lax.erf(upper * math.sqrt(0.5))) + upper * jnp.exp(
                -0.5 * upper * upper
            ) * (1.0 / math.sqrt(2.0 * math.pi))
            r.ups[j, :, cols] = (grad * slope).astype(BF)
            return carry

        lax.fori_loop(0, 4, columns, 0)
        if j + 2 < pieces:
            upper_copy(j + 2).start()

    def into_grad_h(value_ref, w, fresh):
        def columns(n, carry):
            cols = chunk(n, 256)
            value = dot_nt(value_ref[...], w[cols, :])
            r.grad_h[:, cols] = value if fresh else r.grad_h[:, cols] + value
            return carry

        lax.fori_loop(0, 4, columns, 0)

    def up_back(j):
        into_grad_h(r.ups.at[j], next_weight(), j == 0)

    unit(ACT + 0)
    down_back(0)
    unit(ACT + 1)
    up_back(0)
    down_back(1)
    unit(ACT + 2)
    up_back(1)
    down_back(2)
    up_back(2)
    down_back(3)
    unit(ACT + 3)
    up_back(3)
    load_x2.wait()
    norm_back(2, r.grad_x, r.lows.at[1])
    load_x1 = load(r.x1, r.values)

    load_o2.wait()
    r.left[2] = r.rows_in[1].T
    load_o1 = load(r.o1, r.rows_in.at[1])
    unit(UP + 0)
    for piece in (load_q2, load_k2, load_v2):
        piece.wait()

    def into_mixed(low_ref):
        w = next_weight()

        def columns(n, carry):
            cols = chunk(n, 256)
            r.lows[0, :, cols] = dot_nt(low_ref[...], w[cols, :]).astype(BF)
            return carry

        lax.fori_loop(0, 4, columns, 0)

    def cross_back(share):
        attend_back_rows(
            r.query2, r.kv2.at[0], r.kv2.at[1], r.lows.at[0],
            r.query2_grad, r.kv2_grad.at[0], r.kv2_grad.at[1], clips, False, share,
        )

    into_mixed(r.lows.at[1])
    cross_back((0, 2))
    unit(RES2)
    cross_back((1, 2))
    load_h2.wait()
    r.left[3] = r.rows_in[0].T
    load_text = load(r.text, r.pair_in.at[0 : r.text.shape[0]])
    load_h1 = load(r.h1, r.rows_in.at[0])
    unit(QUERY2)
    load_text.wait()
    r.left_text[...] = r.pair_in[0 : r.text.shape[0]].T
    into_grad_h(r.query2_grad, next_weight(), True)
    load_x1.wait()
    norm_back(1, r.grad_x, r.acts.at[3])
    load_x0 = load(r.x0, r.values)
    load_o1.wait()
    r.left[0] = r.rows_in[1].T
    unit(KEY2)

    def self_back(share):
        attend_back_rows(
            r.qkv.at[0], r.qkv.at[1], r.qkv.at[2], r.lows.at[0],
            r.acts.at[0], r.acts.at[1], r.acts.at[2], clips, True, share,
        )

    for piece in (load_q1, load_k1, load_v1):
        piece.wait()
    into_mixed(r.acts.at[3])
    self_back((0, 4))
    unit(VALUE2)
    self_back((1, 4))
    self_back((2, 4))
    unit(RES1)
    self_back((3, 4))
    unit(UP + 1)
    load_h1.wait()
    r.left[2] = r.rows_in[0].T
    into_grad_h(r.acts.at[0], next_weight(), True)
    unit(QUERY1)
    into_grad_h(r.acts.at[1], next_weight(), False)
    into_grad_h(r.acts.at[2], next_weight(), False)
    unit(KEY1)
    load_x0.wait()
    norm_back(0, r.grad_x, r.lows.at[1])
    columns, lanes = r.starts.shape[1], 256
    books, rows = r.embed_out.shape[0], r.starts.shape[2]
    table_rows = r.embed_out.shape[2]
    high_count = -(-table_rows // lanes)
    spread_rows = lanes
    for group in range(r.starts.shape[0] // 4):
        turned = r.lows[1, :, group * 128 : (group + 1) * 128].T
        r.starts[4 * group : 4 * group + 4] = turned.reshape(4, columns, rows)

    def far(src, dst, step, slot):
        return pltpu.make_async_remote_copy(
            src_ref=src,
            dst_ref=dst,
            send_sem=r.far_send.at[slot, step],
            recv_sem=r.far_recv.at[slot, step],
            device_id=device_of(lax.rem(me + step, DEVICES)),
            device_id_type=MESH,
        )

    def start_copy(step):
        return far(r.starts.at[lax.rem(me + step, DEVICES)], r.starts_in.at[me], step, 0)

    def norm_copy(step):
        group = lax.div(lax.rem(me + step, DEVICES), 4)
        return far(r.norm_grads.at[:, chunk(group, 128)], r.norms_in.at[me], step, 1)

    def total_copy(step):
        return far(r.totals, r.totals_in.at[me], step, 2)

    def each(action):
        def body(step, carry):
            action(step)
            return carry

        lax.fori_loop(1, DEVICES, body, 0)

    def send_far(step):
        start_copy(step).start()
        norm_copy(step).start()

    each(send_far)
    r.starts_in[me] = r.starts[me]
    r.norms_in[me] = r.norm_grads[:, chunk(lax.div(me, 4), 128)]
    def book_cols(book, side):
        return pl.ds((book % 2) * 512 + side * lanes, lanes)

    r.upper_slot[...] = jnp.zeros_like(r.upper_slot)
    spread_code = lax.broadcasted_iota(jnp.int32, (lanes, rows), 0)

    def spread_block(step, carry):
        source = lax.rem(me - step + DEVICES, DEVICES)
        dp, member = lax.div(source, 2), lax.rem(source, 2)
        at = (lax.div(dp, 4), lax.rem(lax.div(dp, 2), 2), lax.rem(dp, 2))
        values = wide(r.starts_in[source])
        for book in range(books):
            ids = jnp.concatenate(
                [r.ids_all[(*at, clips * member + m, pl.ds(book, 1))] for m in range(clips)], axis=1
            )
            low_ids, high_ids = ids & (lanes - 1), lax.shift_right_logical(ids, 8)
            hot = jnp.where(spread_code == low_ids, 1.0, 0.0).astype(BF)
            parted = jnp.concatenate(
                [jnp.where(high_ids == high, values, 0.0) for high in range(high_count)], axis=0
            ).astype(BF)
            found = dot_nt(parted, hot)
            r.upper_slot[book // 2, :, book_cols(book, 0)] += found[:spread_rows]
            r.upper_slot[book // 2, 0:columns, book_cols(book, 1)] += found[spread_rows:]
        return carry

    def wait_and_spread(step, carry):
        start_copy(step).wait_recv()
        return spread_block(step, carry)

    unit(VALUE1)
    spread_block(0, 0)
    unit(UP + 2)
    lax.fori_loop(1, 9, wait_and_spread, 0)
    unit(UP + 3)
    for share in range(1, 4):
        lax.fori_loop(1 + 8 * share, min(9 + 8 * share, DEVICES), wait_and_spread, 0)
        pump()
    embed_squares = jnp.zeros((columns, lanes), F32)
    for book in range(books):
        for high in range(high_count):
            left_col = high * lanes
            width = min(table_rows, left_col + lanes) - left_col
            side = high * columns // spread_rows
            row = high * columns - side * spread_rows
            block = r.upper_slot[book // 2, row : row + columns, book_cols(book, side)]
            r.embed_out[book, :, left_col : left_col + width] = block[:, :width]
            embed_squares = embed_squares + block * block
    each(lambda step: norm_copy(step).wait_recv())
    norm_total = r.norms_in[0]
    for other in range(1, DEVICES):
        norm_total = norm_total + r.norms_in[other]
    r.norm_out[...] = norm_total
    lane = lax.broadcasted_iota(jnp.int32, norm_total.shape, 1)
    norm_squares = jnp.where(lax.div(lane, columns) == lax.rem(me, 4), norm_total * norm_total, 0.0)
    while ticks[0] < count + max(LATE[-1], HEAD_LATE[-1]):
        pump()

    sum_tile = norm_squares
    for k in range(4):
        for n in range(8):
            sum_tile = sum_tile + r.squares[8 * k : 8 * k + 8, 128 * n : 128 * n + 128]
        for n in range(lanes // 128):
            sum_tile = sum_tile + embed_squares[8 * k : 8 * k + 8, 128 * n : 128 * n + 128]
    r.totals[0] = sum_tile
    r.totals[1] = r.loss[...]
    each(lambda step: total_copy(step).start())
    r.totals_in[me] = r.totals[...]
    each(lambda step: total_copy(step).wait_recv())
    total = r.totals_in[0]
    for other in range(1, DEVICES):
        total = total + r.totals_in[other]
    r.total_out[...] = total

    def far_done(step):
        start_copy(step).wait_send()
        norm_copy(step).wait_send()
        total_copy(step).wait_send()

    each(far_done)
    for item in range(count):
        if item >= count - 2:
            to_core(item).wait_send()
        parts = third(item)
        if items[item][0] == "h" or item >= count - held_slots:
            parts = parts + first(item) + second(item)
        for part in parts:
            part.wait_send()


def backward_fast(clips, table_rows, operands):
    named = BackwardRefs(*operands, *(None,) * (len(BackwardRefs._fields) - len(operands)))
    rows, width = named.x0.shape
    pair_count = named.pair_rows.shape[0]
    text_rows = named.text.shape[0]
    books, codes = named.head.shape[0], named.head.shape[2]
    units, count = len(UNITS), len(PLAN)
    block = (32, width)
    columns = width // DEVICES
    vmem, dma = pltpu.VMEM, pltpu.SemaphoreType.DMA
    any_spec, vmem_spec = pl.BlockSpec(memory_space=pl.ANY), pl.BlockSpec(memory_space=vmem)
    held_slots = LATE[2] - LATE[0] + 1
    results = pl.pallas_call(
        functools.partial(backward_kernel, clips),
        out_shape=(
            jax.ShapeDtypeStruct((6,) + block, F32),
            jax.ShapeDtypeStruct((2,) + block, F32),
            jax.ShapeDtypeStruct((2, 32, 4 * width), F32),
            jax.ShapeDtypeStruct((books, 2) + block, F32),
            jax.ShapeDtypeStruct((books, columns, table_rows), F32),
            jax.ShapeDtypeStruct((8, 128), F32),
            jax.ShapeDtypeStruct((2, 8, 128), F32),
            jax.ShapeDtypeStruct((count, 4, 2, 2) + block, BF),
        ),
        in_specs=[any_spec] * (len(operands) - 2) + [vmem_spec] * 2,
        out_specs=(vmem_spec,) * 7 + (any_spec,),
        scratch_shapes=[
            vmem((units, 2, 4, 32, width // 2), BF),
            vmem((units, 2, 4) + block, BF),
            vmem((units, 3) + block, BF),
            vmem((books, 3, 2, 2, 32, codes), BF),
            vmem((books, 2, 32, codes), BF),
            vmem((books, 2, 32, codes), BF),
            vmem((books, 4, 2, 2, 32, codes), BF),
            vmem((2, 4, 2, 2) + block, BF),
            vmem((2, 4, 2, 2) + block, BF),
            vmem((held_slots, 4, 2, 2) + block, BF),
            vmem((4, rows, width), BF),
            vmem((4, rows, width), BF),
            vmem((books, pair_count, codes), BF),
            vmem((2, rows, width), F32),
            vmem((3, rows, width), BF),
            vmem((rows, width), BF),
            vmem((2, text_rows, width), BF),
            vmem((4, width, rows), BF),
            vmem((width, pair_count), BF),
            vmem((width, text_rows), BF),
            vmem((2, width, width), BF),
            vmem((2, rows, width), BF),
            vmem((rows, width), BF),
            vmem((2, text_rows, width), BF),
            vmem((rows, width), F32),
            vmem((rows, width), F32),
            vmem((rows, width), F32),
            vmem((2, rows, width), BF),
            vmem((pair_count, width), BF),
            vmem(named.pick.shape, BF),
            vmem(named.gains.shape, F32),
            vmem((3, pair_count // 4, width), BF),
            vmem((3, pair_count // 4, width), BF),
            vmem((2, 2, 32, codes), F32),
            vmem((8, width), F32),
            vmem((DEVICES, columns, rows), BF),
            vmem((DEVICES, columns, rows), BF),
            vmem((DEVICES, 8, 128), F32),
            vmem(block, F32),
            vmem((2, 8, 128), F32),
            vmem((DEVICES, 2, 8, 128), F32),
            dma((count, 8)),
            dma((count, 8)),
            dma((2,)),
            dma((24,)),
            dma((2,)),
            dma((2,)),
            dma((6,)),
            dma((3, DEVICES)),
            dma((3, DEVICES)),
        ],
        compiler_params=pltpu.CompilerParams(
            collective_id=2, has_side_effects=True, vmem_limit_bytes=60 * 2**20
        ),
    )(*operands)
    return BackwardRefs(
        *operands,
        *results,
        *(None,) * (len(BackwardRefs._fields) - len(operands) - len(results)),
    )


class ForwardRefs(NamedTuple):
    ids: Any
    norms: Any
    table: Any
    layer: Any
    head_own: Any
    angles: Any
    text: Any
    pick: Any
    teach: Any
    row_info: Any
    ids_all: Any
    gains: Any
    loss: Any
    head: Any
    w0: Any
    w1: Any
    w2: Any
    w3: Any
    w4: Any
    w5: Any
    w6: Any
    grad_logits: Any
    pair_rows: Any
    x0: Any
    x1: Any
    x2: Any
    x3: Any
    h1: Any
    h2: Any
    h3: Any
    q1: Any
    k1: Any
    v1: Any
    o1: Any
    q2: Any
    k2: Any
    v2: Any
    o2: Any
    upper: Any
    act: Any
    norms_all: Any
    teach_all: Any
    rows_all: Any
    norm_rows: Any
    stacked: Any
    looked: Any
    landed: Any
    xs: Any
    hs: Any
    qkv: Any
    mixed: Any
    query2: Any
    kv2: Any
    uppers: Any
    acts: Any
    final: Any
    pair: Any
    wanted: Any
    logits: Any
    logit_grads: Any
    stats: Any
    weight: Any
    head_weight: Any
    send_sem: Any
    recv_sem: Any
    local_sem: Any
    small_send: Any
    small_recv: Any
    look_send: Any
    look_recv: Any
    weight_sem: Any
    store_sem: Any
    pair_send: Any
    pair_recv: Any


GATHER_LATE = (5, 7, 9, 10)
HOP_LATE = 2


def norm_rows_low(values_ref, gain_ref, bias_ref, low_ref):
    size = 32
    one_gain, bias = 1.0 + gain_ref[...], bias_ref[...]

    def block(index, carry):
        rows = chunk(index, size)
        values = values_ref[rows, :]
        average = jnp.mean(values, axis=-1, keepdims=True)
        centred = values - average
        spread = jnp.mean(centred * centred, axis=-1, keepdims=True)
        low_ref[rows, :] = (centred * lax.rsqrt(spread + NORM_EPS) * one_gain + bias).astype(BF)
        return carry

    lax.fori_loop(0, values_ref.shape[0] // size, block, 0)


def attend_rows(query, key, value, out, clips, causal, share):
    rows, keys = query.shape[0] // clips, key.shape[0] // clips
    pairs = query.shape[1] // 128
    lane = lax.broadcasted_iota(jnp.int32, (1, 128), 1)
    halves = [(lane < 64).astype(F32).astype(BF), (lane >= 64).astype(F32).astype(BF)]

    def pair(index, carry):
        at_q = chunk(lax.div(index, pairs), rows)
        at_k = chunk(lax.div(index, pairs), keys)
        lanes = chunk(lax.rem(index, pairs), 128)
        q, k, v = query[at_q, lanes], key[at_k, lanes], value[at_k, lanes]
        total = jnp.zeros((rows, 128), F32)
        for half in halves:
            scores = dot_nt(q * half, k) * SCORE_SCALE
            if causal:
                allowed = lax.broadcasted_iota(jnp.int32, (rows, keys), 0) >= lax.broadcasted_iota(
                    jnp.int32, (rows, keys), 1
                )
                scores = jnp.where(allowed, scores, NEG_FILL)
            exponents = jnp.exp(scores - jnp.max(scores, axis=-1, keepdims=True))
            probs = exponents / jnp.sum(exponents, axis=-1, keepdims=True)
            total = total + dot_nn(probs.astype(BF), v * half)
        out[at_q, lanes] = total.astype(BF)
        return carry

    first, count = share[0] * clips * pairs // share[1], clips * pairs // share[1]
    lax.fori_loop(first, first + count, pair, 0)


def forward_kernel(clips, denominator, special, *refs):
    r = ForwardRefs(*refs)
    z, y, c, x = place()
    me = lax.axis_index("dp") * 2 + x
    line, z_dev, y_dev, x_dev, c_dev = partners()
    books, frames = r.ids.shape[1], r.ids.shape[2]
    rows = clips * frames
    order = transfer_order(books)
    count = len(order)
    outs = (r.w0, r.w1, r.w2, r.w3, r.w4, r.w5, r.w6)
    columns, lanes = r.looked.shape[1], r.stacked.shape[2]
    high_count = r.stacked.shape[1] // columns
    devices = DEVICES

    greet_all(me)

    def copy(src, dst, item, slot, target):
        return pltpu.make_async_remote_copy(
            src_ref=src,
            dst_ref=dst,
            send_sem=r.send_sem.at[item, slot],
            recv_sem=r.recv_sem.at[item, slot],
            device_id=target,
            device_id_type=MESH,
        )

    def whole(unit):
        group, index = UNITS[unit]
        return outs[group].at[index]

    own = [
        pltpu.make_async_copy(r.layer.at[unit], whole(unit).at[z, y, c, x], r.local_sem.at[unit])
        for unit in range(len(UNITS))
    ]
    part_size = r.head_own.shape[2] // 2

    def part_cols(index):
        return pl.ds(pl.multiple_of(index * part_size, part_size), part_size)

    own.append(
        pltpu.make_async_copy(
            r.head_own.at[:, :, part_cols(y)], r.head.at[:, z, y, c], r.local_sem.at[len(UNITS)]
        )
    )
    half_cols = (pl.ds(0, r.layer.shape[2] // 2), pl.ds(r.layer.shape[2] // 2, r.layer.shape[2] // 2))

    def first(item):
        kind, unit = order[item]
        if kind == "h":
            src = r.head_own.at[unit, :, part_cols(1 - y)]
            return [copy(src, r.head.at[unit, z, y, c], item, 0, y_dev)]
        return []

    def hop(item, number, side):
        unit = order[item][1]
        step = 1 if side == 0 else -1
        target = device(lax.rem(z + step + 4, 4), y, c, x)
        block = whole(unit).at[lax.rem(z - step * (number - 1) + 4, 4), y, c, x]
        source = r.layer.at[unit] if number == 1 else block
        part = copy(source, block, item, (0, 1, 2, 11, 12, 13)[3 * side + number - 1], target)
        if side == 0:
            return part, (z < 3) & (z - number + 1 >= 0), z - number >= 0
        return part, (z > 0) & (z + number - 1 <= 3), z + number <= 3

    def hop_start(item, number):
        for side in range(2):
            part, sends, lands = hop(item, number, side)
            pl.when(sends)(part.start)

    def hop_wait(item, number):
        for side in range(2):
            part, sends, lands = hop(item, number, side)
            pl.when(lands)(part.wait_recv)

    def hop_done(item):
        for number in range(1, 4):
            for side in range(2):
                part, sends, lands = hop(item, number, side)
                pl.when(sends)(part.wait_send)

    def second(item):
        kind, unit = order[item]
        if kind == "h":
            block = r.head.at[unit, z, :, c]
            return [copy(block, block, item, 1 + slot, target) for slot, target in enumerate(z_dev)]
        block = whole(unit).at[:, y, c, x]
        return [
            copy(block, block, item, 3 + slot, target)
            for slot, target in enumerate((y_dev, x_dev, c_dev))
        ]

    def third(item):
        kind, unit = order[item]
        if kind == "h":
            block = r.head.at[unit, :, :, c]
            return [copy(block, block, item, 4, c_dev)]
        from_y, from_x = whole(unit).at[:, 1 - y, c, x], whole(unit).at[:, y, c, 1 - x]
        half_y, half_x = from_y.at[:, :, half_cols[0]], from_x.at[:, :, half_cols[1]]
        return [
            copy(half_y, half_y, item, 6, x_dev),
            copy(half_x, half_x, item, 7, y_dev),
            copy(from_y, from_y, item, 8, c_dev),
            copy(from_x, from_x, item, 9, c_dev),
        ]

    def fourth(item):
        kind, unit = order[item]
        if kind == "h":
            return []
        block = whole(unit).at[:, 1 - y, c, 1 - x]
        return [copy(block, block, item, 10, c_dev)]

    ticks = [0]

    def pump():
        tick = ticks[0]
        ticks[0] += 1
        if tick < count:
            for part in first(tick):
                part.start()
            if order[tick][0] == "a":
                hop_start(tick, 1)
        for number in (1, 2):
            item = tick - HOP_LATE * number
            if 0 <= item < count and order[item][0] == "a":
                hop_wait(item, number)
                hop_start(item, number + 1)
        item = tick - GATHER_LATE[0]
        if 0 <= item < count:
            for part in first(item):
                part.wait_recv()
            if order[item][0] == "a":
                hop_wait(item, 3)
            for part in second(item):
                part.start()
        item = tick - GATHER_LATE[1]
        if 0 <= item < count:
            for part in second(item) if order[item][0] == "h" else second(item)[:2]:
                part.wait_recv()
            for part in third(item):
                part.start()
        item = tick - GATHER_LATE[2]
        if 0 <= item < count and order[item][0] != "h":
            for part in third(item)[:2]:
                part.wait_recv()
            for part in fourth(item):
                part.start()
        item = tick - GATHER_LATE[3]
        if 0 <= item < count:
            late = third(item) if order[item][0] == "h" else second(item)[2:] + third(item)[2:]
            for part in late + fourth(item):
                part.wait_recv()
        advance_loads()

    item_of = {entry: item for item, entry in enumerate(order)}

    def ticks_for(kind, unit):
        return item_of[kind, unit] + GATHER_LATE[3] + 1

    taken, loading, heads_loading = [0], [0], [0]
    weight_slots = r.weight.shape[0]

    def weight_copy(unit):
        slot = unit % weight_slots
        return pltpu.make_async_copy(
            whole(unit), r.weight.at[slot].reshape(whole(unit).shape), r.weight_sem.at[slot]
        )

    def head_copy(book):
        return pltpu.make_async_copy(
            r.head.at[book], r.head_weight.at[book], r.weight_sem.at[weight_slots + book]
        )

    def advance_loads():
        while (
            loading[0] < min(len(UNITS), taken[0] + weight_slots)
            and ticks_for("a", loading[0]) <= ticks[0]
        ):
            weight_copy(loading[0]).start()
            loading[0] += 1
        while heads_loading[0] < books and ticks_for("h", heads_loading[0]) <= ticks[0]:
            head_copy(heads_loading[0]).start()
            heads_loading[0] += 1

    def next_weight():
        unit = taken[0]
        while loading[0] <= unit:
            pump()
        weight_copy(unit).wait()
        taken[0] += 1
        return r.weight.at[unit % weight_slots]

    stores = []

    def store(src, dst):
        piece = pltpu.make_async_copy(src, dst, r.store_sem.at[len(stores)])
        piece.start()
        stores.append(piece)

    def small(block, slot, target):
        return pltpu.make_async_remote_copy(
            src_ref=block,
            dst_ref=block,
            send_sem=r.small_send.at[slot],
            recv_sem=r.small_recv.at[slot],
            device_id=target,
            device_id_type=MESH,
        )

    for piece in own:
        piece.start()
    r.teach_all[y] = r.teach[...]
    r.rows_all[y] = r.row_info[...]
    small_y = [small(r.teach_all.at[y], 11, y_dev), small(r.rows_all.at[y], 12, y_dev)]
    for part in small_y:
        part.start()
    r.ids_all[z, y, c] = r.ids[...]
    r.norms_all[z, y, c, x] = r.norms[...]
    small_stages = (
        [small(r.ids_all.at[z, y, c], k, z_dev[k]) for k in range(3)]
        + [small(r.norms_all.at[z, y, c, x], 3 + k, z_dev[k]) for k in range(3)],
        [small(r.ids_all.at[:, y, c], 6, y_dev), small(r.norms_all.at[:, y, c, x], 7, y_dev)],
        [small(r.ids_all.at[:, :, c], 8, c_dev), small(r.norms_all.at[:, :, c, x], 9, c_dev)],
        [small(r.norms_all.at[:, :, :, x], 10, x_dev)],
    )
    for number, stage in enumerate(small_stages):
        for part in stage:
            part.start()
        if number == 0:
            for piece in own:
                piece.wait()
            pump()
            pump()
            for book in range(books):
                for high in range(high_count):
                    left = high * lanes
                    size = min(r.table.shape[2], left + lanes) - left
                    if size < lanes:
                        r.stacked[book, high * columns : (high + 1) * columns, :] = jnp.zeros(
                            (columns, lanes), BF
                        )
                    r.stacked[book, high * columns : (high + 1) * columns, 0:size] = r.table[
                        book, :, left : left + size
                    ].astype(BF)
        for part in stage:
            part.wait()
        pump()
    for group in range(8):
        parts = [
            r.norms_all[group // 2, group % 2, j // 2, j % 2] for j in range(4)
        ]
        r.norm_rows[:, group * 128 : (group + 1) * 128] = parts[0] + parts[1] + parts[2] + parts[3]
    r.gains[...] = r.norm_rows[0:4, :]

    spread = lax.broadcasted_iota(jnp.int32, (lanes, rows), 0)

    def look_block(step, carry):
        target = lax.rem(me + step, devices)
        dp, member = lax.div(target, 2), lax.rem(target, 2)
        at = (lax.div(dp, 4), lax.rem(lax.div(dp, 2), 2), lax.rem(dp, 2))
        total = jnp.zeros((columns, rows), F32)
        for book in range(books):
            ids = jnp.concatenate(
                [r.ids_all[(*at, clips * member + m, pl.ds(book, 1))] for m in range(clips)], axis=1
            )
            low_ids, high_ids = ids & (lanes - 1), lax.shift_right_logical(ids, 8)
            hot = jnp.where(spread == low_ids, 1.0, 0.0).astype(BF)
            found = dot_nn(r.stacked[book], hot)
            for high in range(high_count):
                total = total + jnp.where(
                    high_ids == high, found[high * columns : (high + 1) * columns], 0.0
                )
        r.looked[step] = total
        return carry

    def look_copy(step):
        return pltpu.make_async_remote_copy(
            src_ref=r.looked.at[step],
            dst_ref=r.landed.at[me],
            send_sem=r.look_send.at[step],
            recv_sem=r.look_recv.at[step],
            device_id=device_of(lax.rem(me + step, devices)),
            device_id_type=MESH,
        )

    def look_and_send(step, carry):
        look_block(step, carry)
        look_copy(step).start()
        return carry

    for part in range(4):
        lax.fori_loop(1 + 8 * part, min(9 + 8 * part, devices), look_and_send, 0)
        pump()
    look_block(0, 0)
    r.landed[me] = r.looked[0]

    for part_in in small_y:
        part_in.wait()
    code = lax.broadcasted_iota(jnp.int32, (128, r.teach.shape[2]), 0) + (x * 2 + y) * part_size
    teach_count = r.teach.shape[1] - 8

    def want(book):
        def block(index, carry):
            here = code + index * 128
            for side in range(2):
                total = jnp.zeros(here.shape, F32)
                for i in range(teach_count):
                    total = total + jnp.where(here == r.teach_all[side, book, i : i + 1, :], 1.0, 0.0)
                hit = jnp.where(
                    here == r.teach_all[side, book, teach_count : teach_count + 1, :], 1.0, 0.0
                )
                r.wanted[book, side * 128 : side * 128 + 128, chunk(index, 128)] = (
                    total * (1.0 / teach_count) + hit
                ).T
            return carry

        lax.fori_loop(0, part_size // 128, block, 0)

    for book in range(books):
        want(book)
        pump()

    def look_wait(step, carry):
        look_copy(step).wait_recv()
        return carry

    lax.fori_loop(1, devices, look_wait, 0)

    def place_rows(index, carry):
        cols = chunk(index, 128)
        block = jnp.concatenate([r.landed[index * 4 + j] for j in range(4)], axis=0).T
        angles = r.angles[:, cols]
        r.xs[0, :, cols] = block + jnp.concatenate([angles] * clips, axis=0)
        return carry

    lax.fori_loop(0, r.xs.shape[2] // 128, place_rows, 0)

    def norm(index, low_ref):
        norm_rows_low(
            r.xs.at[index],
            r.norm_rows.at[index : index + 1],
            r.norm_rows.at[4 + index : 5 + index],
            low_ref,
        )

    def product(left_ref, w, out_ref):
        def part(n, carry):
            cols = chunk(n, 256)
            out_ref[:, cols] = dot_nn(left_ref[...], w[:, cols]).astype(BF)
            return carry

        lax.fori_loop(0, 4, part, 0)

    def residual(left_ref, w, before, after):
        def part(n, carry):
            cols = chunk(n, 256)
            r.xs[after, :, cols] = r.xs[before, :, cols] + dot_nn(left_ref[...], w[:, cols])
            return carry

        lax.fori_loop(0, 4, part, 0)

    store(r.xs.at[0], r.x0)
    norm(0, r.hs.at[0])
    store(r.hs.at[0], r.h1)
    for k in range(3):
        product(r.hs.at[0], next_weight(), r.qkv.at[k])
        store(r.qkv.at[k], (r.q1, r.k1, r.v1)[k])
    for share in range(4):
        pump()
        attend_rows(
            r.qkv.at[0], r.qkv.at[1], r.qkv.at[2], r.mixed.at[0], clips, True, (share, 4)
        )
    store(r.mixed.at[0], r.o1)
    residual(r.mixed.at[0], next_weight(), 0, 1)
    store(r.xs.at[1], r.x1)
    norm(1, r.hs.at[1])
    store(r.hs.at[1], r.h2)
    product(r.hs.at[1], next_weight(), r.query2)
    store(r.query2, r.q2)
    for k in range(2):
        product(r.text, next_weight(), r.kv2.at[k])
        store(r.kv2.at[k], (r.k2, r.v2)[k])
    for share in range(2):
        pump()
        attend_rows(
            r.query2, r.kv2.at[0], r.kv2.at[1], r.mixed.at[1], clips, False, (share, 2)
        )
    store(r.mixed.at[1], r.o2)
    residual(r.mixed.at[1], next_weight(), 1, 2)
    store(r.xs.at[2], r.x2)
    norm(2, r.hs.at[2])
    store(r.hs.at[2], r.h3)
    pieces = r.uppers.shape[0]
    for j in range(pieces):
        w = next_weight()

        def part(n, carry):
            cols = chunk(n, 256)
            upper = dot_nn(r.hs[2], w[:, cols])
            r.uppers[j, :, cols] = upper
            r.acts[j, :, cols] = (upper * (0.5 * (1.0 + lax.erf(upper * math.sqrt(0.5))))).astype(BF)
            return carry

        lax.fori_loop(0, 4, part, 0)
        store(r.uppers.at[j], r.upper.at[j])
        store(r.acts.at[j], r.act.at[j])
    for j in range(pieces):
        w = next_weight()

        def part(n, carry):
            cols = chunk(n, 256)
            before = r.xs[2, :, cols] if j == 0 else r.xs[3, :, cols]
            r.xs[3, :, cols] = before + dot_nt(r.acts[j], w[cols, :])
            return carry

        lax.fori_loop(0, 4, part, 0)
    store(r.xs.at[3], r.x3)
    norm(3, r.final)
    half = r.pair.shape[1]
    mine = y * 2 + x
    r.pair[mine] = dot_nn(r.pick[...], r.final[...]).astype(BF)

    square = (x_dev, y_dev, device(z, 1 - y, c, 1 - x))

    def exchange(ref, first_slot):
        return [
            pltpu.make_async_remote_copy(
                src_ref=ref.at[mine],
                dst_ref=ref.at[mine],
                send_sem=r.pair_send.at[first_slot + slot],
                recv_sem=r.pair_recv.at[first_slot + slot],
                device_id=target,
                device_id_type=MESH,
            )
            for slot, target in enumerate(square)
        ]

    trade = exchange(r.pair, 0)
    for piece in trade:
        piece.start()
    for piece in trade:
        piece.wait()
    pair_count = 4 * half
    stat_lane = lax.broadcasted_iota(jnp.int32, (pair_count, 128), 1)
    stats = jnp.zeros((pair_count, 128), F32)
    for k in range(books):
        while heads_loading[0] <= k:
            pump()
        head_copy(k).wait()

        def logit_part(n, carry):
            cols = chunk(n, 256)
            pair = jnp.concatenate([r.pair[m] for m in range(4)], axis=0)
            w = r.head_weight[k, :, :, :, :, cols].reshape(-1, 256)
            r.logits[k, :, cols] = dot_nn(pair, w)
            return carry

        lax.fori_loop(0, part_size // 256, logit_part, 0)
        highest = jnp.max(r.logits[k], axis=-1, keepdims=True)
        exp_sum = jnp.sum(jnp.exp(r.logits[k] - highest), axis=-1, keepdims=True)
        stats = jnp.where(stat_lane == k, highest, stats)
        stats = jnp.where(stat_lane == books + k, exp_sum, stats)
    r.stats[mine] = stats
    trade = exchange(r.stats, 3)
    for piece in trade:
        piece.start()
    for m in range(4):
        store(r.pair.at[m], r.pair_rows.at[m])
    for piece in trade:
        piece.wait()
    row_info = jnp.concatenate([r.rows_all[0], r.rows_all[1]], axis=0)
    weight_col = row_info[:, books : books + 1]
    member = lax.div(lax.broadcasted_iota(jnp.int32, (pair_count, 1), 0), half)
    owned = jnp.where(member == mine, 1.0, 0.0)
    loss_col = jnp.zeros((pair_count, 1), F32)
    for k in range(books):
        valid = row_info[:, k : k + 1]
        tops = [r.stats[m][:, k : k + 1] for m in range(4)]
        sums = [r.stats[m][:, books + k : books + k + 1] for m in range(4)]
        top = jnp.maximum(jnp.maximum(tops[0], tops[1]), jnp.maximum(tops[2], tops[3]))
        exp_sum = sum(sums[m] * jnp.exp(tops[m] - top) for m in range(4))
        log_total = top + jnp.log(exp_sum)
        loss_col = loss_col + owned * weight_col * (valid + 1.0) * log_total
        scaled = weight_col * (1.0 / denominator)

        def grad_part(n, total):
            cols = chunk(n, 256)
            logits, wanted = r.logits[k, :, cols], r.wanted[k, :, cols]
            r.logit_grads[k, :, cols] = (
                scaled * ((valid + 1.0) * jnp.exp(logits - log_total) - wanted)
            ).astype(BF)
            return total + jnp.sum(wanted * logits, axis=-1, keepdims=True)

        picked = lax.fori_loop(0, part_size // 256, grad_part, jnp.zeros((pair_count, 1), F32))
        loss_col = loss_col - weight_col * picked
        store(r.logit_grads.at[k], r.grad_logits.at[k])
    r.loss[...] = jnp.broadcast_to(jnp.sum(loss_col, axis=0, keepdims=True), r.loss.shape)

    def look_done(step, carry):
        look_copy(step).wait_send()
        return carry

    lax.fori_loop(1, devices, look_done, 0)
    for item in range(count):
        for part in first(item) + second(item) + third(item) + fourth(item):
            part.wait_send()
        if order[item][0] == "a":
            hop_done(item)
    for piece in stores:
        piece.wait()


def forward_fast(clips, denominator, special, operands):
    named = ForwardRefs(*operands, *(None,) * (len(ForwardRefs._fields) - len(operands)))
    books, frames = named.ids.shape[1:]
    rows, width = clips * frames, named.layer.shape[2]
    text_rows, pair_count = named.text.shape[0], 2 * named.teach.shape[2]
    codes, columns = named.head_own.shape[2] // 2, named.table.shape[1]
    lanes = 256
    high_count = -(-named.table.shape[2] // lanes)
    count = books + len(UNITS)
    pieces = GROUPS[-1]
    vmem, dma = pltpu.VMEM, pltpu.SemaphoreType.DMA
    any_spec, vmem_spec = pl.BlockSpec(memory_space=pl.ANY), pl.BlockSpec(memory_space=vmem)

    def shaped(shape, dtype=BF):
        return jax.ShapeDtypeStruct(shape, dtype)

    in_vmem = (
        shaped((4, 2, 2) + named.ids.shape, jnp.int32),
        shaped((4, width), F32),
        shaped((8, 128), F32),
    )
    in_hbm = (
        (shaped((books, 4, 2, 2, named.head_own.shape[1], codes)),)
        + tuple(shaped((size, 4, 2, 2, 2) + named.layer.shape[1:]) for size in GROUPS)
        + (shaped((books, pair_count, codes)), shaped((4, pair_count // 4, width)))
        + (shaped((rows, width), F32),) * 4
        + (shaped((rows, width)),) * 8
        + (shaped((text_rows, width)),) * 2
        + (shaped((rows, width)), shaped((pieces, rows, width), F32), shaped((pieces, rows, width)))
    )
    results = pl.pallas_call(
        functools.partial(forward_kernel, clips, denominator, special),
        out_shape=in_vmem + in_hbm,
        in_specs=[vmem_spec] * len(operands),
        out_specs=(vmem_spec,) * len(in_vmem) + (any_spec,) * len(in_hbm),
        scratch_shapes=[
            vmem((4, 2, 2, 2, 8, 128), F32),
            vmem((2,) + named.teach.shape, jnp.int32),
            vmem((2,) + named.row_info.shape, F32),
            vmem((8, width), F32),
            vmem((books, high_count * columns, lanes), BF),
            vmem((32, columns, rows), F32),
            vmem((32, columns, rows), F32),
            vmem((4, rows, width), F32),
            vmem((3, rows, width), BF),
            vmem((3, rows, width), BF),
            vmem((2, rows, width), BF),
            vmem((rows, width), BF),
            vmem((2, text_rows, width), BF),
            vmem((pieces, rows, width), F32),
            vmem((pieces, rows, width), BF),
            vmem((rows, width), BF),
            vmem((4, pair_count // 4, width), BF),
            vmem((books, pair_count, codes), F32),
            vmem((books, pair_count, codes), F32),
            vmem((books, pair_count, codes), BF),
            vmem((4, pair_count, 128), F32),
            vmem((3, width, width), BF),
            vmem((books, 4, 2, 2, named.head_own.shape[1], codes), BF),
            dma((count, 14)),
            dma((count, 14)),
            dma((len(UNITS) + 1,)),
            dma((13,)),
            dma((13,)),
            dma((32,)),
            dma((32,)),
            dma((3 + books,)),
            dma((44,)),
            dma((6,)),
            dma((6,)),
        ],
        compiler_params=pltpu.CompilerParams(
            collective_id=1, has_side_effects=True, vmem_limit_bytes=58 * 2**20
        ),
    )(*operands)
    return ForwardRefs(
        *operands,
        *results,
        *(None,) * (len(ForwardRefs._fields) - len(operands) - len(results)),
    )


def adam_kernel(chunks, *refs):
    arrays = refs[:20]
    totals, corrections = refs[20:22]
    results = refs[22:37]
    buffers, load_sem, store_sem = refs[37:42], refs[42], refs[43]
    depth = buffers[0].shape[0]
    seen = [0] * 5
    places = []
    for array, index in chunks:
        places.append((array, index, seen[array] % depth))
        seen[array] += 1

    def loads(item):
        array, index, slot = places[item]
        return [
            pltpu.make_async_copy(
                arrays[5 * kind + array].at[index],
                buffers[array].at[slot, kind],
                load_sem.at[item, kind],
            )
            for kind in range(4)
        ]

    def stores(item):
        array, index, slot = places[item]
        return [
            pltpu.make_async_copy(
                buffers[array].at[slot, 4 + kind],
                results[3 * array + kind].at[index],
                store_sem.at[item, kind],
            )
            for kind in range(3)
        ]

    def last_use(item):
        array, index, slot = places[item]
        for other in range(item - 1, -1, -1):
            if places[other][0] == array and places[other][2] == slot:
                return other
        return None

    ahead = depth
    for item in range(ahead):
        for piece in loads(item):
            piece.start()
    norm = jnp.sqrt(
        jnp.sum(jnp.sum(totals[0], axis=0, keepdims=True), axis=1, keepdims=True)
    )
    factor = CLIP_LIMIT / jnp.maximum(norm, CLIP_LIMIT)
    one, two = corrections[0, 0:1, 0:1], corrections[1, 0:1, 0:1]
    waited = set()
    for item in range(len(places)):
        array, index, slot = places[item]
        for piece in loads(item):
            piece.wait()
        before = last_use(item)
        if before is not None:
            waited.add(before)
            for piece in stores(before):
                piece.wait()
        buffer = buffers[array]

        def block(n, carry):
            rows = chunk(n, 8)
            weight, first, second, grad = (buffer[slot, kind, rows, :] for kind in range(4))
            clipped = grad * factor
            first_next = BETA_ONE * first + (1.0 - BETA_ONE) * clipped
            second_next = BETA_TWO * second + (1.0 - BETA_TWO) * clipped * clipped
            update = first_next * one / (jnp.sqrt(second_next * two) + ADAM_EPS)
            buffer[slot, 4, rows, :] = weight - LEARN_RATE * (update + DECAY_RATE * weight)
            buffer[slot, 5, rows, :] = first_next
            buffer[slot, 6, rows, :] = second_next
            return carry

        lax.fori_loop(0, buffer.shape[2] // 8, block, 0)
        for piece in stores(item):
            piece.start()
        if item + ahead < len(places):
            for piece in loads(item + ahead):
                piece.start()
    for item in range(len(places)):
        if item not in waited:
            for piece in stores(item):
                piece.wait()


def adam_fast(weights, firsts, seconds, grads, totals, corrections):
    chunks = [(array, index) for array in (2, 4, 3, 0, 1) for index in range(weights[array].shape[0])]
    any_spec, vmem_spec = pl.BlockSpec(memory_space=pl.ANY), pl.BlockSpec(memory_space=pltpu.VMEM)
    results = pl.pallas_call(
        functools.partial(adam_kernel, tuple(chunks)),
        out_shape=tuple(
            jax.ShapeDtypeStruct(part.shape, F32) for part in weights for kind in range(3)
        ),
        in_specs=[any_spec] * 20 + [vmem_spec] * 2,
        out_specs=(any_spec,) * 15,
        scratch_shapes=[pltpu.VMEM((4, 7) + part.shape[1:], F32) for part in weights]
        + [pltpu.SemaphoreType.DMA((len(chunks), 4)), pltpu.SemaphoreType.DMA((len(chunks), 3))],
        compiler_params=pltpu.CompilerParams(vmem_limit_bytes=56 * 2**20),
    )(*weights, *firsts, *seconds, *grads, totals, corrections)
    return [results[3 * array : 3 * array + 3] for array in range(5)]


def low(values):
    return values.astype(BF)


def ein(formula, left, right):
    return jnp.einsum(formula, left, right, preferred_element_type=F32)


def norm_stats(values):
    average = jnp.mean(values, axis=-1, keepdims=True)
    centred = values - average
    spread = jnp.mean(centred * centred, axis=-1, keepdims=True)
    scale = lax.rsqrt(spread + NORM_EPS)
    return centred * scale, scale


def norm_forward(values, gain, bias):
    hat, scale = norm_stats(values)
    return hat * (1.0 + gain) + bias


def norm_backward(values, gain, cotangent):
    hat, scale = norm_stats(values)
    scaled = cotangent * (1.0 + gain)
    mean_one = jnp.mean(scaled, axis=-1, keepdims=True)
    mean_two = jnp.mean(scaled * hat, axis=-1, keepdims=True)
    return (
        (scaled - mean_one - hat * mean_two) * scale,
        jnp.sum(cotangent * hat, axis=0),
        jnp.sum(cotangent, axis=0),
    )


def sinusoid(frames, model_width):
    half_width = model_width // 2
    freq_rates = jnp.exp(
        jnp.arange(half_width, dtype=F32) * (-math.log(10000.0) / (half_width - 1))
    )
    angles = jnp.arange(frames, dtype=F32)[:, None] * freq_rates[None, :]
    return jnp.concatenate([jnp.sin(angles), jnp.cos(angles)], axis=1)


def delay_ids(codes, offsets, special):
    frames = codes.shape[2]
    frame = jnp.arange(frames, dtype=jnp.int32)[None, None, :]
    inputs = jnp.full_like(codes, special)
    targets = jnp.full_like(codes, special)
    padded = jnp.pad(codes, ((0, 0), (0, 0), (4, 0)), constant_values=special)
    for shift in range(4):
        is_shift = (offsets == shift)[:, :, None]
        targets = jnp.where(is_shift, padded[:, :, 4 - shift : 4 - shift + frames], targets)
        inputs = jnp.where(is_shift, padded[:, :, 3 - shift : 3 - shift + frames], inputs)
    return inputs, targets


def split_heads(matrix, clips):
    return matrix.reshape(clips, matrix.shape[0] // clips, HEADS, -1)


def raw_scores(queries, keyset, causal):
    scores = ein("bqhe,bkhe->bhqk", queries, keyset) * SCORE_SCALE
    if causal:
        length = scores.shape[2]
        allowed = jnp.arange(length)[:, None] >= jnp.arange(length)[None, :]
        scores = jnp.where(allowed[None, None], scores, NEG_FILL)
    return scores


def attend_forward(queries, keyset, valset, clips, causal):
    queries, keyset, valset = (split_heads(m, clips) for m in (queries, keyset, valset))
    scores = raw_scores(queries, keyset, causal)
    highest = jnp.max(scores, axis=-1, keepdims=True)
    exponents = jnp.exp(scores - highest)
    denominator = jnp.sum(exponents, axis=-1, keepdims=True)
    probs = exponents / denominator
    mixed = ein("bhqk,bkhe->bqhe", low(probs), valset)
    return low(mixed).reshape(mixed.shape[0] * mixed.shape[1], -1), probs


def attend_backward(queries, keyset, valset, probs, grad_mixed, clips):
    queries, keyset, valset, grad_mixed = (
        split_heads(m, clips) for m in (queries, keyset, valset, grad_mixed)
    )
    grad_probs = ein("bqhe,bkhe->bhqk", grad_mixed, valset)
    grad_values = low(ein("bhqk,bqhe->bkhe", low(probs), grad_mixed))
    grad_scores = low(
        probs * (grad_probs - jnp.sum(probs * grad_probs, axis=-1, keepdims=True))
    )
    grad_queries = low(ein("bhqk,bkhe->bqhe", grad_scores, keyset) * SCORE_SCALE)
    grad_keys = low(ein("bhqk,bqhe->bkhe", grad_scores, queries) * SCORE_SCALE)
    return tuple(
        m.reshape(m.shape[0] * m.shape[1], -1) for m in (grad_queries, grad_keys, grad_values)
    )


def normal_cdf(values):
    return 0.5 * (1.0 + lax.erf(values * math.sqrt(0.5)))


def adam_step(weight, first_moment, second_moment, gradient, factor, corr_one, corr_two):
    clipped = gradient * factor
    first_next = BETA_ONE * first_moment + (1.0 - BETA_ONE) * clipped
    second_next = BETA_TWO * second_moment + (1.0 - BETA_TWO) * clipped * clipped
    update = (
        first_next / corr_one / (jnp.sqrt(second_next / corr_two) + ADAM_EPS) + DECAY_RATE * weight
    )
    return (weight - LEARN_RATE * update, first_next, second_next)


def columns_apart(matrix, pieces):
    count, rows, width = matrix.shape
    parts = matrix.reshape(count, rows, pieces, width // pieces).transpose(0, 2, 1, 3)
    return parts.reshape(count * pieces, rows, width // pieces)


def columns_together(parts, pieces):
    total, rows, width = parts.shape
    matrix = parts.reshape(total // pieces, pieces, rows, width).transpose(0, 2, 1, 3)
    return matrix.reshape(total // pieces, rows, pieces * width)


def local(
    fast,
    audio_codes,
    delay_offsets,
    clip_lengths,
    loss_positions,
    teacher_ids,
    text_states,
    step_count,
    in_proj,
    in_proj_mean,
    in_proj_sq,
    out_proj,
    out_proj_mean,
    out_proj_sq,
    ffn_proj,
    ffn_proj_mean,
    ffn_proj_sq,
    embed_table,
    embed_table_mean,
    embed_table_sq,
    head_table,
    head_table_mean,
    head_table_sq,
    norm_gain,
    norm_gain_mean,
    norm_gain_sq,
    norm_bias,
    norm_bias_mean,
    norm_bias_sq,
):
    clips = text_states.shape[0]
    vocab_count = lax.axis_size("vocab")
    device_count = lax.axis_size("dp") * vocab_count
    vocab_index = lax.axis_index("vocab")
    book_count = head_table.shape[0]
    pos_count = loss_positions.shape[1]
    frames = audio_codes.shape[2]
    table_rows = embed_table.shape[1]
    special = table_rows - 1
    half_vocab = head_table.shape[2]
    vocab_base = vocab_index * half_vocab
    model_width = text_states.shape[2]
    rows = clips * frames
    ffn_pieces = ffn_proj.shape[2] // model_width
    denominator = float(clips * device_count * pos_count * book_count)

    inputs, targets = delay_ids(audio_codes, delay_offsets, special)
    own_first = vocab_index * clips
    own_inputs = lax.dynamic_slice_in_dim(inputs, own_first, clips, 0)
    own_positions = lax.dynamic_slice_in_dim(loss_positions, own_first, clips, 0)

    layer_local = jnp.concatenate(
        [
            low(in_proj[0:3]),
            low(out_proj[0:1]),
            low(in_proj[3:6]),
            low(out_proj[1:2]),
            columns_apart(low(ffn_proj), ffn_pieces),
        ],
        axis=0,
    )
    head_local = low(head_table)
    norms_local = low(jnp.concatenate([norm_gain, norm_bias], axis=0))
    target_at = jnp.take_along_axis(targets, loss_positions[:, None, :], axis=2)
    pair_count = target_at.shape[0] * pos_count
    target_at = target_at.transpose(1, 0, 2).reshape(book_count, pair_count)
    valid = (target_at != special).astype(F32)
    row_weight = (loss_positions < clip_lengths[:, None]).astype(F32).reshape(pair_count)
    flat_positions = (own_positions + jnp.arange(clips, dtype=jnp.int32)[:, None] * frames).reshape(-1)
    pick = flat_positions[:, None] == jnp.arange(rows, dtype=jnp.int32)[None, :]
    text = text_states.reshape(-1, model_width)
    angles = sinusoid(frames, model_width)
    if fast:
        device_index = lax.axis_index("dp") * vocab_count + vocab_index
        norm_width = norm_gain.shape[1]
        norms_placed = lax.dynamic_update_slice(
            jnp.zeros((8, 128), F32),
            norms_local.astype(F32),
            (0, lax.rem(device_index, 128 // norm_width) * norm_width),
        )
        table_t = jnp.swapaxes(embed_table, 1, 2)
        teach = jnp.concatenate(
            [
                teacher_ids.transpose(1, 3, 0, 2).reshape(book_count, -1, pair_count),
                jnp.where(target_at == special, -1, target_at)[:, None, :],
                jnp.full((book_count, 7, pair_count), -1, jnp.int32),
            ],
            axis=1,
        )
        row_info = jnp.concatenate([valid, row_weight[None]], axis=0).T
        row_info = jnp.pad(row_info, ((0, 0), (0, 128 - row_info.shape[1])))
        kept = forward_fast(
            clips,
            denominator,
            special,
            (
                inputs,
                norms_placed,
                table_t,
                layer_local,
                head_local,
                angles,
                text,
                pick.astype(BF),
                teach,
                row_info,
            ),
        )

        def joined(part):
            return part.reshape(part.shape[0], -1, part.shape[-1])

        done = backward_fast(
            clips,
            table_rows,
            (
                kept.grad_logits,
                kept.pair_rows.reshape(-1, model_width),
                pick.T.astype(BF),
                kept.x0,
                kept.x1,
                kept.x2,
                kept.x3,
                kept.h1,
                kept.h2,
                kept.h3,
                kept.q1,
                kept.k1,
                kept.v1,
                kept.o1,
                kept.q2,
                kept.k2,
                kept.v2,
                kept.o2,
                kept.upper,
                kept.act,
                text,
                kept.gains,
                joined(kept.head),
                joined(kept.w0),
                joined(kept.w1),
                joined(kept.w2),
                joined(kept.w3),
                joined(kept.w4),
                joined(kept.w5),
                joined(kept.w6),
                kept.ids_all,
                kept.loss,
            ),
        )
        norm_shard = lax.dynamic_slice_in_dim(
            done.norm_out, lax.rem(device_index, 128 // norm_width) * norm_width, norm_width, 1
        )
        big_gradients = (
            done.in_out,
            done.out_out,
            done.ffn_out,
            done.embed_out,
            done.head_out.reshape(head_table.shape),
        )
        gradients = big_gradients + (norm_shard[:4], norm_shard[4:])
        square_total, loss_total = jnp.sum(done.total_out[0]), done.total_out[1, 0, 0]
    else:
        norms = lax.all_gather(norms_local, BOTH, axis=1, tiled=True).astype(F32)
        table = lax.all_gather(low(embed_table), BOTH, axis=2, tiled=True)
        embedded = jnp.zeros((rows, model_width), F32)
        for book in range(book_count):
            embedded = embedded + jnp.take(
                table[book], own_inputs[:, book].reshape(-1), axis=0
            ).astype(F32)
        layer_all = lax.all_gather(layer_local, BOTH, axis=1, tiled=True)
        starts = [sum(GROUPS[:g]) for g in range(len(GROUPS))]
        layer_parts = [layer_all[s : s + g] for s, g in zip(starts, GROUPS)]
        head_all = lax.all_gather(head_local, "dp", axis=1, tiled=True)
        w_self, w_self_out, w_query, w_text, w_cross_out, w_up, w_down = layer_parts
        gains, biases = norms[:4], norms[4:]

        start = embedded + jnp.tile(angles, (clips, 1))
        normed_self = low(norm_forward(start, gains[0], biases[0]))
        proj = low(ein("rd,kde->kre", normed_self, w_self))
        self_out, self_probs = attend_forward(proj[0], proj[1], proj[2], clips, True)
        after_self = start + ein("rd,de->re", self_out, w_self_out[0])
        normed_cross = low(norm_forward(after_self, gains[1], biases[1]))
        cross_query = low(ein("rd,de->re", normed_cross, w_query[0]))
        cross_text = low(ein("td,kde->kte", text, w_text))
        cross_out, cross_probs = attend_forward(cross_query, cross_text[0], cross_text[1], clips, False)
        after_cross = after_self + ein("rd,de->re", cross_out, w_cross_out[0])
        normed_ffn = low(norm_forward(after_cross, gains[2], biases[2]))
        upper = ein("rd,jdf->jrf", normed_ffn, w_up)
        cdf = normal_cdf(upper)
        active = low(upper * cdf)
        after_ffn = after_cross + ein("jrf,jdf->rd", active, w_down)
        final_norm = low(norm_forward(after_ffn, gains[3], biases[3]))
        chosen = low(ein("pr,rd->pd", pick.astype(BF), final_norm))

        pair_rows = lax.all_gather(chosen, "vocab", axis=0, tiled=True)
        teach = teacher_ids.transpose(1, 0, 2, 3).reshape(book_count, pair_count, -1)
        local_ids = vocab_base + jnp.arange(half_vocab, dtype=jnp.int32)
        counts = jnp.sum(
            (teach[:, :, :, None] == local_ids[None, None, None, :]).astype(F32), axis=2
        )
        wanted = counts / teach.shape[2] + valid[:, :, None] * (
            target_at[:, :, None] == local_ids[None, None, :]
        ).astype(F32)
        logits = ein("rd,kdv->krv", pair_rows, head_all)
        highest = jnp.max(logits, axis=-1)
        exp_sum = jnp.sum(jnp.exp(logits - highest[:, :, None]), axis=-1)
        stats = lax.all_gather(jnp.stack([highest, exp_sum]), "vocab")
        top_all = jnp.max(stats[:, 0], axis=0)
        sum_all = jnp.sum(stats[:, 1] * jnp.exp(stats[:, 0] - top_all[None]), axis=0)
        log_total = top_all + jnp.log(sum_all)
        row_loss = row_weight[None, :] * (valid + 1.0) * log_total
        own_rows = clips * pos_count
        loss_sum = jnp.sum(
            lax.dynamic_slice_in_dim(row_loss, vocab_index * own_rows, own_rows, 1)
        ) - jnp.sum(row_weight[None, :] * jnp.sum(wanted * logits, axis=-1))
        scaled = (row_weight / denominator)[None, :, None]
        grad_logits = low(
            scaled * ((valid + 1.0)[:, :, None] * jnp.exp(logits - log_total[:, :, None]) - wanted)
        )
        grad_head = ein("rd,krv->kdv", pair_rows, grad_logits)
        grad_rows = ein("krv,kdv->rd", grad_logits, head_all)
        grad_chosen = lax.psum_scatter(low(grad_rows), "vocab", scatter_dimension=0, tiled=True).astype(F32)

        grad_final = jnp.einsum(
            "pr,pd->rd", pick.astype(F32), grad_chosen, precision=lax.Precision.HIGHEST
        )
        grad_ffn_res, gain_three, bias_three = norm_backward(after_ffn, gains[3], grad_final)
        low_ffn = low(grad_ffn_res)
        grad_down = ein("rd,jrf->jdf", low_ffn, active)
        grad_active = ein("rd,jdf->jrf", low_ffn, w_down)
        slope = cdf + upper * jnp.exp(-0.5 * upper * upper) * (1.0 / math.sqrt(2.0 * math.pi))
        grad_upper = low(grad_active * slope)
        grad_up = ein("rd,jrf->jdf", normed_ffn, grad_upper)
        grad_normed = ein("jrf,jdf->rd", grad_upper, w_up)
        grad_inner, gain_two, bias_two = norm_backward(after_cross, gains[2], grad_normed)
        grad_cross_res = grad_ffn_res + grad_inner
        low_cross = low(grad_cross_res)
        grad_cross_out = ein("rd,re->de", cross_out, low_cross)[None]
        grad_mixed = low(ein("re,de->rd", low_cross, w_cross_out[0]))
        grad_query, grad_key, grad_value = attend_backward(
            cross_query, cross_text[0], cross_text[1], cross_probs, grad_mixed, clips
        )
        grad_w_query = ein("rd,re->de", normed_cross, grad_query)[None]
        grad_w_text = ein("td,kte->kde", text, jnp.stack([grad_key, grad_value]))
        grad_normed = ein("re,de->rd", grad_query, w_query[0])
        grad_inner, gain_one, bias_one = norm_backward(after_self, gains[1], grad_normed)
        grad_self_res = grad_cross_res + grad_inner
        low_self = low(grad_self_res)
        grad_self_out = ein("rd,re->de", self_out, low_self)[None]
        grad_mixed = low(ein("re,de->rd", low_self, w_self_out[0]))
        grad_proj = jnp.stack(
            attend_backward(proj[0], proj[1], proj[2], self_probs, grad_mixed, clips)
        )
        grad_w_self = ein("rd,kre->kde", normed_self, grad_proj)
        grad_normed = ein("kre,kde->rd", grad_proj, w_self)
        grad_inner, gain_zero, bias_zero = norm_backward(start, gains[0], grad_normed)
        grad_start = grad_self_res + grad_inner

        layer_grads = (
            grad_w_self, grad_self_out, grad_w_query, grad_w_text, grad_cross_out, grad_up, grad_down
        )
        norm_grads = jnp.stack(
            [gain_zero, gain_one, gain_two, gain_three, bias_zero, bias_one, bias_two, bias_three]
        )
        embed_sum = jnp.stack(
            [
                jax.ops.segment_sum(
                    grad_start, own_inputs[:, book].reshape(-1), num_segments=table_rows
                )
                for book in range(book_count)
            ]
        )
        embed_shard = lax.psum_scatter(embed_sum, BOTH, scatter_dimension=2, tiled=True)
        layer_shard = lax.psum_scatter(
            jnp.concatenate(layer_grads, axis=0), BOTH, scatter_dimension=1, tiled=True
        )
        head_shard = lax.psum_scatter(grad_head, "dp", scatter_dimension=1, tiled=True)
        big_gradients = (
            jnp.concatenate([layer_shard[0:3], layer_shard[4:7]], axis=0),
            jnp.concatenate([layer_shard[3:4], layer_shard[7:8]], axis=0),
            columns_together(layer_shard[8:], ffn_pieces),
            embed_shard,
            head_shard,
        )
        square_sum = jnp.zeros((), F32)
        for shard_grad in big_gradients:
            square_sum = square_sum + jnp.sum(shard_grad * shard_grad)
        norm_total = lax.psum(norm_grads, BOTH)
        square_total, loss_total = lax.psum((square_sum, loss_sum), BOTH)
        square_total = square_total + jnp.sum(norm_total * norm_total)
        norm_width = norm_gain.shape[1]
        norm_shard = lax.dynamic_slice_in_dim(
            norm_total, (lax.axis_index("dp") * vocab_count + vocab_index) * norm_width, norm_width, 1
        )
        gradients = big_gradients + (norm_shard[:4], norm_shard[4:])
    loss_value = loss_total / denominator
    grad_norm = jnp.sqrt(square_total)
    factor = CLIP_LIMIT / jnp.maximum(grad_norm, CLIP_LIMIT)
    steps_float = step_count.astype(F32)
    corr_one = 1.0 - jnp.power(BETA_ONE, steps_float)
    corr_two = 1.0 - jnp.power(BETA_TWO, steps_float)
    masters = (in_proj, out_proj, ffn_proj, embed_table, head_table, norm_gain, norm_bias)
    mean_list = (
        in_proj_mean,
        out_proj_mean,
        ffn_proj_mean,
        embed_table_mean,
        head_table_mean,
        norm_gain_mean,
        norm_bias_mean,
    )
    square_list = (
        in_proj_sq,
        out_proj_sq,
        ffn_proj_sq,
        embed_table_sq,
        head_table_sq,
        norm_gain_sq,
        norm_bias_sq,
    )
    if fast:
        corrections = jnp.broadcast_to(
            jnp.stack([1.0 / corr_one, 1.0 / corr_two])[:, None, None], (2, 8, 128)
        )
        turned = [
            [jnp.swapaxes(part, 1, 2) if index == 3 else part for index, part in enumerate(parts)]
            for parts in (masters[:5], mean_list[:5], square_list[:5])
        ]
        stepped = adam_fast(*turned, big_gradients, done.total_out, corrections)
        stepped = [
            [jnp.swapaxes(part, 1, 2) if index == 3 else part for part in parts]
            for index, parts in enumerate(stepped)
        ]
    outputs = [loss_value, grad_norm]
    for index in range(7):
        if fast and index < 5:
            outputs.extend(stepped[index])
            continue
        outputs.extend(
            adam_step(
                masters[index],
                mean_list[index],
                square_list[index],
                gradients[index],
                factor,
                corr_one,
                corr_two,
            )
        )
    return tuple(outputs)


def solution(mesh):
    by_row = P(None, BOTH, None)
    by_column = P(None, None, BOTH)
    by_head = P(None, "dp", "vocab")
    by_feature = P(None, BOTH)
    weights = (
        (by_row,) * 9 + (by_column,) * 3 + (by_head,) * 3 + (by_feature,) * 6
    )
    placed = (
        P("dp", None, None),
        P("dp", None),
        P("dp"),
        P("dp", None),
        P("dp", None, None, None),
        P(BOTH, None, None),
        P(),
    ) + weights
    fast = dict(mesh.shape) == {"dp": 16, "vocab": 2}
    return jax.shard_map(
        functools.partial(local, fast),
        mesh=mesh,
        in_specs=placed,
        out_specs=(P(), P()) + weights,
        check_vma=False,
    )
```
